32 devices in a mesh: groups: 2 (over y), ctx: 4 (over z), head: 4 (over x, core).
Axes of the slice: x: 2, y: 2, z: 4, core: 2. Of those that a mesh axis runs over, the one named last changes fastest.
Arguments:
- queries: bfloat16 [1536, 8, 8, 128], P(('groups', 'ctx'), None, 'head'), parts along dimension 0, may hold values from -80 to 80
- keys: bfloat16 [512, 4, 8, 128], P(('groups', 'ctx')), parts along dimension 0, may hold values from -6 to 6
- span_start: int32 [2], P('groups'), parts along dimension 0, may hold values from 13568 to 15616
- tile_first: int32 [24], P(('groups', 'ctx')), parts along dimension 0, may hold values from 0 to 255
Outputs:
- importance: float32 [1536, 8, 256], P(('groups', 'ctx'), 'head'), parts along dimension 0
The draws below stay inside these ranges and needn't reach their ends.
There are 2 independent parts, one for each index of `groups`. The reference program is written for one: setup_inputs(seed, part) draws one part's arguments, and reference() takes and returns one part's arrays. A program takes and returns all parts, laid end to end along the dimension named above; each array names one. Nothing has to cross between parts.
All inputs are finite; a program needn't handle non-finite values.
Results may differ from the reference program's by a relative error of at most 0.0003.
Values may be sent and summed in bfloat16 or wider, within the bound.
No kernel may reach another device: no remote copies, remote signals or barrier semaphores. Data moves between devices by JAX's collectives and lax.ppermute only.
A program may use at most 512 MiB of HBM per device.

```python
import jax
import jax.numpy as jnp
from jax import lax

KVH = 8
GQ = 8
DH = 128
QTOK_DEV = 192
QTILE = 64
NCMP = 1024
NSEL = 256
CTXT = 16384
SPAN = 768
TILES = 12
N_CTX = 4


def shared_keys(key):
    normal_keys = jax.random.normal(key, (NCMP, KVH, DH), jnp.float32)
    return normal_keys


def draw_keys(key, part):
    normal_keys = shared_keys(key)
    flat = jnp.clip(normal_keys, -6.0, 6.0)
    return flat.reshape(NSEL, 4, KVH, DH).astype(jnp.bfloat16)


def draw_queries(key, part):
    key = jax.random.fold_in(key, 5)
    shape = (SPAN, KVH, GQ, DH)
    flat = jnp.clip(jax.random.normal(key, shape, jnp.float32), -6.0, 6.0)
    return flat.astype(jnp.bfloat16)


def with_ends(values, own_key, low, largest):
    spot = [jax.random.randint(jax.random.fold_in(own_key, axis), (), 0, length) for axis, length in enumerate(values.shape)]
    widest = values.shape.index(max(values.shape))
    beside = spot[:widest] + [(spot[widest] + 1) % values.shape[widest]] + spot[widest + 1:]
    return values.at[tuple(spot)].set(low).at[tuple(beside)].set(largest)


def setup_inputs(seed: int = 0, part: int = 0) -> dict:
    key_of = jax.random.split(jax.random.key(seed), 5)
    own_keys = jax.random.split(jax.random.fold_in(key_of[4], part), 5)
    queries = draw_queries(jax.random.fold_in(jax.random.fold_in(key_of[4], part), 71), part)
    keys = draw_keys(jax.random.fold_in(jax.random.fold_in(key_of[4], part), 71), part)
    span_start = jax.random.randint(own_keys[2], (1,), CTXT - SPAN - CTXT // 8, CTXT - SPAN + 1).astype(jnp.int32)
    tile_first = with_ends(jax.random.randint(own_keys[3], (TILES,), 0, NCMP // 4), jax.random.fold_in(own_keys[3], 1), 0, (NCMP // 4) - 1).astype(jnp.int32)
    return dict(queries=queries, keys=keys, span_start=span_start, tile_first=tile_first)


masked_score = -1.0e30


def reference(queries, keys, span_start, tile_first):
    flat_keys = keys.reshape(NCMP, KVH, DH).astype(jnp.float32)
    positions = span_start[0] + jnp.arange(SPAN, dtype=jnp.int32)
    firsts = jnp.repeat(tile_first, QTILE)
    index = jnp.arange(NCMP, dtype=jnp.int32)
    factor = NSEL / (2.0 * GQ)

    def one_block(block):
        query_rows, places, first = block
        scores = jnp.einsum("rghd,ngd->rghn", query_rows.astype(jnp.float32), flat_keys) * (DH ** -0.5)
        visible = (index[None, :] >= first[:, None]) & (16 * index[None, :] + 31 <= places[:, None])
        visible = visible[:, None, None, :]
        scores = jnp.where(visible, scores, masked_score)
        top = jnp.max(scores, axis=-1, keepdims=True)
        weights = jnp.where(visible, jnp.exp(scores - top), 0.0)
        probs = weights / jnp.sum(weights, axis=-1, keepdims=True)
        grouped = jnp.sum(probs, axis=2).reshape(QTOK_DEV, KVH, NSEL, 4)
        lead = grouped[..., 0]
        weighted = lead + 2.0 * (grouped[..., 1] + grouped[..., 2] + grouped[..., 3])
        zeros = jnp.zeros((QTOK_DEV, KVH, 1), jnp.float32)
        shifted = jnp.concatenate([zeros, weighted[..., :-1]], axis=-1)
        return (lead + shifted) * factor

    result = lax.map(one_block, (queries.reshape(N_CTX, QTOK_DEV, KVH, GQ, DH),
                                 positions.reshape(N_CTX, QTOK_DEV),
                                 firsts.reshape(N_CTX, QTOK_DEV)))
    return result.reshape(SPAN, KVH, NSEL)
```

```python
import math
from functools import partial

import jax
import jax.numpy as jnp
from jax import lax
from jax.experimental import pallas as pl
from jax.experimental.pallas import tpu as pltpu
from jax.sharding import PartitionSpec as P

QTILE = 64
PACK = 16
LANES = 128
MASKED = -1e30
NT = (((1,), (1,)), ((), ()))


def pack_kernel(n_head, key_heads, heads, q_ref, k_ref, *out_refs):
    q_outs, k_out = out_refs[:n_head], out_refs[n_head]
    me = lax.axis_index("head")
    own = key_heads // n_head
    width = own * heads
    tokens = q_outs[0].shape[2]
    rows = PACK * key_heads * heads
    out_row = lax.broadcasted_iota(jnp.int32, (n_head * width * PACK, rows), 0)
    in_row = lax.broadcasted_iota(jnp.int32, (n_head * width * PACK, rows), 1)
    step = out_row // (width * PACK)
    unit = out_row // PACK % width
    source = out_row % PACK * (key_heads * heads) + (step ^ me) * width + unit
    select = jnp.where(in_row == source, 1.0, 0.0).astype(jnp.bfloat16)
    for block in range(tokens // PACK):
        moved = jnp.dot(
            select, q_ref[block * rows:(block + 1) * rows, :], preferred_element_type=jnp.float32
        ).astype(jnp.bfloat16)
        for d in range(n_head):
            for u in range(width):
                at = (d * width + u) * PACK
                q_outs[d][u // heads, u % heads, block * PACK:(block + 1) * PACK, :] = moved[at:at + PACK]

    blocks = k_out.shape[2]
    rows = PACK * 4 * key_heads
    out_row = lax.broadcasted_iota(jnp.int32, (own * 4 * PACK, rows), 0)
    in_row = lax.broadcasted_iota(jnp.int32, (own * 4 * PACK, rows), 1)
    head = out_row // (4 * PACK)
    part = out_row // PACK % 4
    source = out_row % PACK * (4 * key_heads) + part * key_heads + me * own + head
    select = jnp.where(in_row == source, 1.0, 0.0).astype(jnp.bfloat16)
    for block in range(blocks // PACK):
        moved = jnp.dot(
            select, k_ref[block * rows:(block + 1) * rows, :], preferred_element_type=jnp.float32
        ).astype(jnp.bfloat16)
        for u in range(own * 4):
            k_out[u // 4, u % 4, block * PACK:(block + 1) * PACK, :] = moved[u * PACK:(u + 1) * PACK]


def main_kernel(n_head, n_ctx, start_ref, first_ref, *refs):
    q_refs, k_refs = refs[:n_head], refs[n_head:n_head + n_ctx]
    out_ref, keys, scores = refs[n_head + n_ctx:]
    own, heads, tokens, _ = q_refs[0].shape
    local = k_refs[0].shape[2]
    nsel = local * n_ctx
    me = lax.axis_index("ctx")
    step = scores.shape[0] // (n_head * heads)
    scale = math.log2(math.e) / math.sqrt(q_refs[0].shape[3])
    factor = nsel / (2.0 * n_head * heads)
    least_position = 16 * 4 * nsel * 7 // 8 - n_ctx * tokens
    most_first = nsel - 1

    for j in range(n_ctx):
        source = lax.rem(me - j + n_ctx, n_ctx)
        at = pl.ds(pl.multiple_of(source * local, local), local)
        keys[:, :, at, :] = k_refs[j][...]

    def tile(index, _):
        begin = pl.multiple_of(index * step, step)
        first = first_ref[begin // QTILE]
        position = start_ref[0] + me * tokens + begin
        for g in range(own):
            rows = jnp.concatenate(
                [q[g, h, pl.ds(begin, step), :] for q in q_refs for h in range(heads)], axis=0
            )
            for s in range(4):
                scores[:, s * nsel:(s + 1) * nsel] = lax.dot_general(
                    rows, keys[g, s], NT, preferred_element_type=jnp.float32
                )
            for t in range(0, step, 8):
                masks = []
                place = position + t + lax.broadcasted_iota(jnp.int32, (8, LANES), 0)
                for s in range(4):
                    for lane in range(0, nsel, LANES):
                        i = 4 * (lane + lax.broadcasted_iota(jnp.int32, (8, LANES), 1)) + s
                        mask = None
                        if 4 * lane <= most_first:
                            mask = i >= first
                        if 16 * (4 * (lane + LANES - 1) + s) + 31 > least_position:
                            below = 16 * i + 31 <= place
                            mask = below if mask is None else mask & below
                        masks.append(mask)
                lead_sum, rest_sum = None, None
                for h in range(n_head * heads):
                    at = h * step + t
                    pieces = []
                    for n, mask in enumerate(masks):
                        piece = scores[at:at + 8, n * LANES:(n + 1) * LANES]
                        pieces.append(piece if mask is None else jnp.where(mask, piece, MASKED))
                    top = pieces[0]
                    for piece in pieces[1:]:
                        top = jnp.maximum(top, piece)
                    top = jnp.max(top, axis=1, keepdims=True)
                    pieces = [jnp.exp2((piece - top) * scale) for piece in pieces]
                    width = nsel // LANES
                    lead = pieces[:width]
                    rest = [pieces[n + width] + pieces[n + 2 * width] + pieces[n + 3 * width] for n in range(width)]
                    total = lead[0] + rest[0]
                    for n in range(1, width):
                        total = total + (lead[n] + rest[n])
                    inverse = 1.0 / jnp.sum(total, axis=1, keepdims=True)
                    lead = [piece * inverse for piece in lead]
                    rest = [piece * inverse for piece in rest]
                    if lead_sum is None:
                        lead_sum, rest_sum = lead, rest
                    else:
                        lead_sum = [a + b for a, b in zip(lead_sum, lead)]
                        rest_sum = [a + b for a, b in zip(rest_sum, rest)]
                lead = jnp.concatenate(lead_sum, axis=1)
                weighted = lead + 2.0 * jnp.concatenate(rest_sum, axis=1)
                column = lax.broadcasted_iota(jnp.int32, (8, nsel), 1)
                shifted = jnp.where(column == 0, 0.0, pltpu.roll(weighted, 1, 1))
                out_ref[pl.ds(begin + t, 8), g, :] = (lead + shifted) * factor
        return 0

    lax.fori_loop(0, tokens // step, tile, 0)


def per_device(n_head, n_ctx, queries, keys, span_start, tile_first):
    tokens, key_heads, heads, depth = queries.shape
    blocks = keys.shape[0]
    own = key_heads // n_head
    nsel = blocks * n_ctx
    vmem = pl.BlockSpec(memory_space=pltpu.VMEM)
    smem = pl.BlockSpec(memory_space=pltpu.SMEM)
    q_part = jax.ShapeDtypeStruct((own, heads, tokens, depth), queries.dtype)
    k_part = jax.ShapeDtypeStruct((own, 4, blocks, depth), keys.dtype)
    packed = pl.pallas_call(
        partial(pack_kernel, n_head, key_heads, heads),
        out_shape=[q_part] * n_head + [k_part],
        in_specs=[vmem, vmem],
        out_specs=[vmem] * (n_head + 1),
        compiler_params=pltpu.CompilerParams(vmem_limit_bytes=32 * 2 ** 20),
        name="pack",
    )(queries.reshape(-1, depth), keys.reshape(-1, depth))
    q_parts, k_own = packed[:n_head], packed[n_head]
    q_parts = [q_parts[0]] + [
        lax.ppermute(q_parts[d], "head", [(i, i ^ d) for i in range(n_head)]) for d in range(1, n_head)
    ]
    k_parts = [k_own] + [
        lax.ppermute(k_own, "ctx", [(i, (i + j) % n_ctx) for i in range(n_ctx)]) for j in range(1, n_ctx)
    ]
    step = min(QTILE, max(PACK, QTILE * 1024 // (4 * nsel)))
    return pl.pallas_call(
        partial(main_kernel, n_head, n_ctx),
        out_shape=jax.ShapeDtypeStruct((tokens, own, nsel), jnp.float32),
        in_specs=[smem, smem] + [vmem] * (n_head + n_ctx),
        out_specs=vmem,
        scratch_shapes=[
            pltpu.VMEM((own, 4, nsel, depth), keys.dtype),
            pltpu.VMEM((n_head * heads * step, 4 * nsel), jnp.float32),
        ],
        compiler_params=pltpu.CompilerParams(vmem_limit_bytes=56 * 2 ** 20),
        name="importance",
    )(span_start, tile_first, *q_parts, *k_parts)


def solution(mesh):
    placed = (
        P(("groups", "ctx"), None, "head", None),
        P(("groups", "ctx"), None, None, None),
        P("groups"),
        P(("groups", "ctx")),
    )
    return jax.shard_map(
        partial(per_device, mesh.shape["head"], mesh.shape["ctx"]),
        mesh=mesh,
        in_specs=placed,
        out_specs=P(("groups", "ctx"), "head", None),
        check_vma=False,
    )
```

```python
import math
from functools import partial

import jax
import jax.numpy as jnp
from jax import lax
from jax.experimental import pallas as pl
from jax.experimental.pallas import tpu as pltpu
from jax.sharding import PartitionSpec as P

QTILE = 64
PACK = 16
LANES = 128
MASKED = -1e30
NT = (((1,), (1,)), ((), ()))


def pack_kernel(n_head, n_ctx, key_heads, heads, q_hbm, k_hbm, q_out, k_out, q_ref, k_ref, q_sems, k_sems):
    me = lax.axis_index("head")
    own = key_heads // n_head
    width = own * heads
    tokens = q_out.shape[3]
    blocks = k_out.shape[3]
    q_rows = PACK * key_heads * heads
    k_rows = PACK * 4 * key_heads
    k_copies, q_copies = [], []
    for block in range(blocks // PACK):
        at = pl.ds(block * k_rows, k_rows)
        k_copies.append(pltpu.make_async_copy(k_hbm.at[at], k_ref.at[at], k_sems.at[block]))
    for block in range(tokens // PACK):
        at = pl.ds(block * q_rows, q_rows)
        q_copies.append(pltpu.make_async_copy(q_hbm.at[at], q_ref.at[at], q_sems.at[block]))
    for copy in k_copies + q_copies:
        copy.start()

    out_row = lax.broadcasted_iota(jnp.int32, (own * 4 * PACK, k_rows), 0)
    in_row = lax.broadcasted_iota(jnp.int32, (own * 4 * PACK, k_rows), 1)
    head = out_row // (4 * PACK)
    part = out_row // PACK % 4
    source = out_row % PACK * (4 * key_heads) + part * key_heads + me * own + head
    select = jnp.where(in_row == source, 1.0, 0.0).astype(jnp.bfloat16)
    for block in range(blocks // PACK):
        k_copies[block].wait()
        moved = jnp.dot(
            select, k_ref[block * k_rows:(block + 1) * k_rows, :], preferred_element_type=jnp.float32
        ).astype(jnp.bfloat16)
        for u in range(own * 4):
            for j in range(n_ctx):
                k_out[j, u // 4, u % 4, block * PACK:(block + 1) * PACK, :] = moved[u * PACK:(u + 1) * PACK]

    out_row = lax.broadcasted_iota(jnp.int32, (n_head * width * PACK, q_rows), 0)
    in_row = lax.broadcasted_iota(jnp.int32, (n_head * width * PACK, q_rows), 1)
    unit = out_row // PACK
    source = out_row % PACK * (key_heads * heads) + unit
    select = jnp.where(in_row == source, 1.0, 0.0).astype(jnp.bfloat16)
    for block in range(tokens // PACK):
        q_copies[block].wait()
        moved = jnp.dot(
            select, q_ref[block * q_rows:(block + 1) * q_rows, :], preferred_element_type=jnp.float32
        ).astype(jnp.bfloat16)
        for u in range(n_head * width):
            d, g, h = u // width, u % width // heads, u % heads
            q_out[d, g, h, block * PACK:(block + 1) * PACK, :] = moved[u * PACK:(u + 1) * PACK]


def main_kernel(start_ref, first_ref, q_ref, k_ref, out_ref, keys, scores):
    n_head, own, heads, tokens, depth = q_ref.shape
    n_ctx, local = k_ref.shape[0], k_ref.shape[3]
    nsel = local * n_ctx
    me = lax.axis_index("ctx")
    step = scores.shape[0] // (n_head * heads)
    scale = math.log2(math.e) / math.sqrt(depth)
    factor = nsel / (2.0 * n_head * heads)
    least_position = 16 * 4 * nsel * 7 // 8 - n_ctx * tokens
    most_first = nsel - 1

    for j in range(n_ctx):
        keys[:, :, j * local:(j + 1) * local, :] = k_ref[j]

    def tile(index, _):
        begin = pl.multiple_of(index * step, step)
        first = first_ref[begin // QTILE]
        position = start_ref[0] + me * tokens + begin
        for g in range(own):
            rows = jnp.concatenate(
                [q_ref[d, g, h, pl.ds(begin, step), :] for d in range(n_head) for h in range(heads)], axis=0
            )
            for s in range(4):
                scores[:, s * nsel:(s + 1) * nsel] = lax.dot_general(
                    rows, keys[g, s], NT, preferred_element_type=jnp.float32
                )
            for t in range(0, step, 8):
                masks = []
                place = position + t + lax.broadcasted_iota(jnp.int32, (8, LANES), 0)
                for s in range(4):
                    for lane in range(0, nsel, LANES):
                        i = 4 * (lane + lax.broadcasted_iota(jnp.int32, (8, LANES), 1)) + s
                        mask = None
                        if 4 * lane <= most_first:
                            mask = i >= first
                        if 16 * (4 * (lane + LANES - 1) + s) + 31 > least_position:
                            below = 16 * i + 31 <= place
                            mask = below if mask is None else mask & below
                        masks.append(mask)
                lead_sum, rest_sum = None, None
                for h in range(n_head * heads):
                    at = h * step + t
                    pieces = []
                    for n, mask in enumerate(masks):
                        piece = scores[at:at + 8, n * LANES:(n + 1) * LANES]
                        pieces.append(piece if mask is None else jnp.where(mask, piece, MASKED))
                    top = pieces[0]
                    for piece in pieces[1:]:
                        top = jnp.maximum(top, piece)
                    top = jnp.max(top, axis=1, keepdims=True)
                    pieces = [jnp.exp2((piece - top) * scale) for piece in pieces]
                    width = nsel // LANES
                    lead = pieces[:width]
                    rest = [pieces[n + width] + pieces[n + 2 * width] + pieces[n + 3 * width] for n in range(width)]
                    total = lead[0] + rest[0]
                    for n in range(1, width):
                        total = total + (lead[n] + rest[n])
                    inverse = 1.0 / jnp.sum(total, axis=1, keepdims=True)
                    lead = [piece * inverse for piece in lead]
                    rest = [piece * inverse for piece in rest]
                    if lead_sum is None:
                        lead_sum, rest_sum = lead, rest
                    else:
                        lead_sum = [a + b for a, b in zip(lead_sum, lead)]
                        rest_sum = [a + b for a, b in zip(rest_sum, rest)]
                lead = jnp.concatenate(lead_sum, axis=1)
                weighted = lead + 2.0 * jnp.concatenate(rest_sum, axis=1)
                column = lax.broadcasted_iota(jnp.int32, (8, nsel), 1)
                shifted = jnp.where(column == 0, 0.0, pltpu.roll(weighted, 1, 1))
                out_ref[pl.ds(begin + t, 8), g, :] = (lead + shifted) * factor
        return 0

    lax.fori_loop(0, tokens // step, tile, 0)


def per_device(n_head, n_ctx, queries, keys, span_start, tile_first):
    tokens, key_heads, heads, depth = queries.shape
    blocks = keys.shape[0]
    own = key_heads // n_head
    nsel = blocks * n_ctx
    vmem = pl.BlockSpec(memory_space=pltpu.VMEM)
    smem = pl.BlockSpec(memory_space=pltpu.SMEM)
    hbm = pl.BlockSpec(memory_space=pltpu.HBM)
    q_pack, k_pack = pl.pallas_call(
        partial(pack_kernel, n_head, n_ctx, key_heads, heads),
        out_shape=[
            jax.ShapeDtypeStruct((n_head, own, heads, tokens, depth), queries.dtype),
            jax.ShapeDtypeStruct((n_ctx, own, 4, blocks, depth), keys.dtype),
        ],
        in_specs=[hbm, hbm],
        out_specs=[vmem, vmem],
        scratch_shapes=[
            pltpu.VMEM((tokens * key_heads * heads, depth), queries.dtype),
            pltpu.VMEM((blocks * 4 * key_heads, depth), keys.dtype),
            pltpu.SemaphoreType.DMA((tokens // PACK,)),
            pltpu.SemaphoreType.DMA((blocks // PACK,)),
        ],
        compiler_params=pltpu.CompilerParams(vmem_limit_bytes=56 * 2 ** 20),
        name="pack",
    )(queries.reshape(-1, depth), keys.reshape(-1, depth))
    q_all = lax.all_to_all(q_pack, "head", 0, 0, tiled=True)
    k_all = lax.all_to_all(k_pack, "ctx", 0, 0, tiled=True)
    step = min(QTILE, max(PACK, QTILE * 1024 // (4 * nsel)))
    return pl.pallas_call(
        main_kernel,
        out_shape=jax.ShapeDtypeStruct((tokens, own, nsel), jnp.float32),
        in_specs=[smem, smem, vmem, vmem],
        out_specs=vmem,
        scratch_shapes=[
            pltpu.VMEM((own, 4, nsel, depth), keys.dtype),
            pltpu.VMEM((n_head * heads * step, 4 * nsel), jnp.float32),
        ],
        compiler_params=pltpu.CompilerParams(vmem_limit_bytes=32 * 2 ** 20),
        name="importance",
    )(span_start, tile_first, q_all, k_all)


def solution(mesh):
    placed = (
        P(("groups", "ctx"), None, "head", None),
        P(("groups", "ctx"), None, None, None),
        P("groups"),
        P(("groups", "ctx")),
    )
    return jax.shard_map(
        partial(per_device, mesh.shape["head"], mesh.shape["ctx"]),
        mesh=mesh,
        in_specs=placed,
        out_specs=P(("groups", "ctx"), "head", None),
        check_vma=False,
    )
```

```python
import math
from functools import partial

import jax
import jax.numpy as jnp
from jax import lax
from jax.experimental import pallas as pl
from jax.experimental.pallas import tpu as pltpu
from jax.sharding import PartitionSpec as P

QTILE = 64
PACK = 16
K_COPIES = 2
Q_COPIES = 3
LANES = 128
MASKED = -1e30
NT = (((1,), (1,)), ((), ()))


def pack_kernel(n_head, key_heads, heads, q_hbm, k_hbm, *refs):
    q_outs, (k_out, q_ref, k_ref, q_sems, k_sems) = refs[:n_head], refs[n_head:]
    me = lax.axis_index("head")
    own = key_heads // n_head
    width = own * heads
    tokens = q_outs[0].shape[2]
    blocks = k_out.shape[2]
    q_rows = PACK * key_heads * heads
    k_rows = PACK * 4 * key_heads
    k_copies, q_copies = [], []
    k_each, q_each = blocks // PACK // K_COPIES, tokens // PACK // Q_COPIES
    for n in range(K_COPIES):
        at = pl.ds(n * k_each * k_rows, k_each * k_rows)
        k_copies.append(pltpu.make_async_copy(k_hbm.at[at], k_ref.at[at], k_sems.at[n]))
    for n in range(Q_COPIES):
        at = pl.ds(n * q_each * q_rows, q_each * q_rows)
        q_copies.append(pltpu.make_async_copy(q_hbm.at[at], q_ref.at[at], q_sems.at[n]))
    for copy in k_copies + q_copies:
        copy.start()

    out_row = lax.broadcasted_iota(jnp.int32, (own * 4 * PACK, k_rows), 0)
    in_row = lax.broadcasted_iota(jnp.int32, (own * 4 * PACK, k_rows), 1)
    head = out_row // (4 * PACK)
    part = out_row // PACK % 4
    source = out_row % PACK * (4 * key_heads) + part * key_heads + me * own + head
    select = jnp.where(in_row == source, 1.0, 0.0).astype(jnp.bfloat16)
    for block in range(blocks // PACK):
        if block % k_each == 0:
            k_copies[block // k_each].wait()
        moved = jnp.dot(
            select, k_ref[block * k_rows:(block + 1) * k_rows, :], preferred_element_type=jnp.float32
        ).astype(jnp.bfloat16)
        for u in range(own * 4):
            k_out[u // 4, u % 4, block * PACK:(block + 1) * PACK, :] = moved[u * PACK:(u + 1) * PACK]

    out_row = lax.broadcasted_iota(jnp.int32, (n_head * width * PACK, q_rows), 0)
    in_row = lax.broadcasted_iota(jnp.int32, (n_head * width * PACK, q_rows), 1)
    step = out_row // (width * PACK)
    unit = out_row // PACK % width
    source = out_row % PACK * (key_heads * heads) + (step ^ me) * width + unit
    select = jnp.where(in_row == source, 1.0, 0.0).astype(jnp.bfloat16)
    for block in range(tokens // PACK):
        if block % q_each == 0:
            q_copies[block // q_each].wait()
        moved = jnp.dot(
            select, q_ref[block * q_rows:(block + 1) * q_rows, :], preferred_element_type=jnp.float32
        ).astype(jnp.bfloat16)
        for u in range(n_head * width):
            d, g, h = u // width, u % width // heads, u % heads
            q_outs[d][g, h, block * PACK:(block + 1) * PACK, :] = moved[u * PACK:(u + 1) * PACK]


def main_kernel(n_head, n_ctx, start_ref, first_ref, *refs):
    q_refs, k_refs = refs[:n_head], refs[n_head:n_head + n_ctx]
    out_ref, keys, scores = refs[n_head + n_ctx:]
    own, heads, tokens, depth = q_refs[0].shape
    local = k_refs[0].shape[2]
    nsel = local * n_ctx
    me = lax.axis_index("ctx")
    step = scores.shape[0] // (n_head * heads)
    scale = math.log2(math.e) / math.sqrt(depth)
    factor = nsel / (2.0 * n_head * heads)
    least_position = 16 * 4 * nsel * 7 // 8 - n_ctx * tokens
    most_first = nsel - 1

    for j in range(n_ctx):
        source = lax.rem(me + 1 + j, n_ctx)
        at = pl.ds(pl.multiple_of(source * local, local), local)
        keys[:, :, at, :] = k_refs[j][...]

    def tile(index, _):
        begin = pl.multiple_of(index * step, step)
        first = first_ref[begin // QTILE]
        position = start_ref[0] + me * tokens + begin
        for g in range(own):
            rows = jnp.concatenate(
                [q[g, h, pl.ds(begin, step), :] for q in q_refs for h in range(heads)], axis=0
            )
            for s in range(4):
                scores[:, s * nsel:(s + 1) * nsel] = lax.dot_general(
                    rows, keys[g, s], NT, preferred_element_type=jnp.float32
                )
            for t in range(0, step, 8):
                masks = []
                place = position + t + lax.broadcasted_iota(jnp.int32, (8, LANES), 0)
                for s in range(4):
                    for lane in range(0, nsel, LANES):
                        i = 4 * (lane + lax.broadcasted_iota(jnp.int32, (8, LANES), 1)) + s
                        mask = None
                        if 4 * lane <= most_first:
                            mask = i >= first
                        if 16 * (4 * (lane + LANES - 1) + s) + 31 > least_position:
                            below = 16 * i + 31 <= place
                            mask = below if mask is None else mask & below
                        masks.append(mask)
                lead_sum, rest_sum = None, None
                for h in range(n_head * heads):
                    at = h * step + t
                    pieces = []
                    for n, mask in enumerate(masks):
                        piece = scores[at:at + 8, n * LANES:(n + 1) * LANES]
                        pieces.append(piece if mask is None else jnp.where(mask, piece, MASKED))
                    top = pieces[0]
                    for piece in pieces[1:]:
                        top = jnp.maximum(top, piece)
                    top = jnp.max(top, axis=1, keepdims=True)
                    pieces = [jnp.exp2((piece - top) * scale) for piece in pieces]
                    width = nsel // LANES
                    lead = pieces[:width]
                    rest = [pieces[n + width] + pieces[n + 2 * width] + pieces[n + 3 * width] for n in range(width)]
                    total = lead[0] + rest[0]
                    for n in range(1, width):
                        total = total + (lead[n] + rest[n])
                    inverse = 1.0 / jnp.sum(total, axis=1, keepdims=True)
                    lead = [piece * inverse for piece in lead]
                    rest = [piece * inverse for piece in rest]
                    if lead_sum is None:
                        lead_sum, rest_sum = lead, rest
                    else:
                        lead_sum = [a + b for a, b in zip(lead_sum, lead)]
                        rest_sum = [a + b for a, b in zip(rest_sum, rest)]
                lead = jnp.concatenate(lead_sum, axis=1)
                weighted = lead + 2.0 * jnp.concatenate(rest_sum, axis=1)
                column = lax.broadcasted_iota(jnp.int32, (8, nsel), 1)
                shifted = jnp.where(column == 0, 0.0, pltpu.roll(weighted, 1, 1))
                out_ref[pl.ds(begin + t, 8), g, :] = (lead + shifted) * factor
        return 0

    lax.fori_loop(0, tokens // step, tile, 0)


def in_hbm(array):
    return pltpu.with_memory_space_constraint(array, pltpu.HBM)


def per_device(n_head, n_ctx, queries, keys, span_start, tile_first):
    tokens, key_heads, heads, depth = queries.shape
    blocks = keys.shape[0]
    own = key_heads // n_head
    nsel = blocks * n_ctx
    vmem = pl.BlockSpec(memory_space=pltpu.VMEM)
    smem = pl.BlockSpec(memory_space=pltpu.SMEM)
    hbm = pl.BlockSpec(memory_space=pltpu.HBM)
    q_part = jax.ShapeDtypeStruct((own, heads, tokens, depth), queries.dtype)
    k_part = jax.ShapeDtypeStruct((own, 4, blocks, depth), keys.dtype)
    packed = pl.pallas_call(
        partial(pack_kernel, n_head, key_heads, heads),
        out_shape=[q_part] * n_head + [k_part],
        in_specs=[hbm, hbm],
        out_specs=[vmem] * (n_head + 1),
        scratch_shapes=[
            pltpu.VMEM((tokens * key_heads * heads, depth), queries.dtype),
            pltpu.VMEM((blocks * 4 * key_heads, depth), keys.dtype),
            pltpu.SemaphoreType.DMA((Q_COPIES,)),
            pltpu.SemaphoreType.DMA((K_COPIES,)),
        ],
        compiler_params=pltpu.CompilerParams(vmem_limit_bytes=16 * 2 ** 20),
        name="pack",
    )(in_hbm(queries.reshape(-1, depth)), in_hbm(keys.reshape(-1, depth)))
    q_parts, k_parts = list(packed[:n_head]), [packed[n_head]] * n_ctx

    def send_keys(j):
        k_parts[j] = lax.ppermute(k_parts[0], "ctx", [(i, (i + j) % n_ctx) for i in range(n_ctx)])

    for d in range(1, n_head):
        q_parts[d] = lax.ppermute(q_parts[d], "head", [(i, i ^ d) for i in range(n_head)])
    for j in range(n_ctx - 1, 0, -1):
        send_keys(j)
    step = min(QTILE, max(PACK, QTILE * 1024 // (4 * nsel)))
    return pl.pallas_call(
        partial(main_kernel, n_head, n_ctx),
        out_shape=jax.ShapeDtypeStruct((tokens, own, nsel), jnp.float32),
        in_specs=[smem, smem] + [vmem] * (n_head + n_ctx),
        out_specs=vmem,
        scratch_shapes=[
            pltpu.VMEM((own, 4, nsel, depth), keys.dtype),
            pltpu.VMEM((n_head * heads * step, 4 * nsel), jnp.float32),
        ],
        compiler_params=pltpu.CompilerParams(vmem_limit_bytes=32 * 2 ** 20),
        name="importance",
    )(span_start, tile_first, *q_parts, *k_parts[::-1])


def solution(mesh):
    placed = (
        P(("groups", "ctx"), None, "head", None),
        P(("groups", "ctx"), None, None, None),
        P("groups"),
        P(("groups", "ctx")),
    )
    return jax.shard_map(
        partial(per_device, mesh.shape["head"], mesh.shape["ctx"]),
        mesh=mesh,
        in_specs=placed,
        out_specs=P(("groups", "ctx"), "head", None),
        check_vma=False,
    )
```

```python
import math
from functools import partial

import jax
import jax.numpy as jnp
from jax import lax
from jax.experimental import pallas as pl
from jax.experimental.pallas import tpu as pltpu
from jax.sharding import PartitionSpec as P

QTILE = 64
PACK = 16
K_COPIES = 2
Q_COPIES = 3
LANES = 128
CHUNK = 256
MASKED = -1e30
NT = (((1,), (1,)), ((), ()))


def pack_kernel(n_head, key_heads, heads, q_hbm, k_hbm, *refs):
    q_outs, (k_out, q_ref, k_ref, q_sems, k_sems) = refs[:n_head], refs[n_head:]
    me = lax.axis_index("head")
    own = key_heads // n_head
    width = own * heads
    tokens = q_outs[0].shape[2]
    blocks = k_out.shape[2]
    q_rows = PACK * key_heads * heads
    k_rows = PACK * 4 * key_heads
    k_copies, q_copies = [], []
    k_each, q_each = blocks // PACK // K_COPIES, tokens // PACK // Q_COPIES
    for n in range(K_COPIES):
        at = pl.ds(n * k_each * k_rows, k_each * k_rows)
        k_copies.append(pltpu.make_async_copy(k_hbm.at[at], k_ref.at[at], k_sems.at[n]))
    for n in range(Q_COPIES):
        at = pl.ds(n * q_each * q_rows, q_each * q_rows)
        q_copies.append(pltpu.make_async_copy(q_hbm.at[at], q_ref.at[at], q_sems.at[n]))
    for copy in k_copies + q_copies:
        copy.start()

    out_row = lax.broadcasted_iota(jnp.int32, (own * 4 * PACK, k_rows), 0)
    in_row = lax.broadcasted_iota(jnp.int32, (own * 4 * PACK, k_rows), 1)
    head = out_row // (4 * PACK)
    part = out_row // PACK % 4
    source = out_row % PACK * (4 * key_heads) + part * key_heads + me * own + head
    select = jnp.where(in_row == source, 1.0, 0.0).astype(jnp.bfloat16)
    for block in range(blocks // PACK):
        if block % k_each == 0:
            k_copies[block // k_each].wait()
        moved = jnp.dot(
            select, k_ref[block * k_rows:(block + 1) * k_rows, :], preferred_element_type=jnp.float32
        ).astype(jnp.bfloat16)
        for u in range(own * 4):
            k_out[u // 4, u % 4, block * PACK:(block + 1) * PACK, :] = moved[u * PACK:(u + 1) * PACK]

    out_row = lax.broadcasted_iota(jnp.int32, (n_head * width * PACK, q_rows), 0)
    in_row = lax.broadcasted_iota(jnp.int32, (n_head * width * PACK, q_rows), 1)
    step = out_row // (width * PACK)
    unit = out_row // PACK % width
    source = out_row % PACK * (key_heads * heads) + (step ^ me) * width + unit
    select = jnp.where(in_row == source, 1.0, 0.0).astype(jnp.bfloat16)
    for block in range(tokens // PACK):
        if block % q_each == 0:
            q_copies[block // q_each].wait()
        moved = jnp.dot(
            select, q_ref[block * q_rows:(block + 1) * q_rows, :], preferred_element_type=jnp.float32
        ).astype(jnp.bfloat16)
        for u in range(n_head * width):
            d, g, h = u // width, u % width // heads, u % heads
            q_outs[d][g, h, block * PACK:(block + 1) * PACK, :] = moved[u * PACK:(u + 1) * PACK]


def main_kernel(n_head, n_ctx, start_ref, first_ref, *refs):
    q_refs, k_refs = refs[:n_head], refs[n_head:n_head + n_ctx]
    out_ref, keys, scores, pooled, lined = refs[n_head + n_ctx:]
    own, heads, tokens, depth = q_refs[0].shape
    local = k_refs[0].shape[2]
    nsel = local * n_ctx
    me = lax.axis_index("ctx")
    scale = math.log2(math.e) / math.sqrt(depth)
    factor = nsel / (2.0 * n_head * heads)
    least_position = 16 * 4 * nsel * 7 // 8 - n_ctx * tokens
    most_first = nsel - 1
    chunks = n_head * heads * QTILE // CHUNK
    per_chunk = n_head // chunks

    for j in range(n_ctx):
        source = lax.rem(me + 1 + j, n_ctx)
        at = pl.ds(pl.multiple_of(source * local, local), local)
        keys[:, :, at, :] = k_refs[j][...]

    def tile(index, _):
        begin = pl.multiple_of(index * QTILE, QTILE)
        first = first_ref[index]
        lane = lax.broadcasted_iota(jnp.int32, (8, LANES), 1)
        row = lax.broadcasted_iota(jnp.int32, (8, LANES), 0)
        place = start_ref[0] + me * tokens + begin + lane % QTILE

        def visible(r, s):
            i = 4 * (r + row) + s
            mask = None
            if 4 * r + s <= most_first:
                mask = i >= first
            if 16 * (4 * (r + 7) + s) + 31 > least_position:
                below = 16 * i + 31 <= place
                mask = below if mask is None else mask & below
            return mask

        for g in range(own):
            weights = []
            for c in range(chunks):
                columns = jnp.concatenate(
                    [q[g, h, pl.ds(begin, QTILE), :] for q in q_refs[c * per_chunk:(c + 1) * per_chunk] for h in range(heads)],
                    axis=0,
                )
                tops = [None] * (CHUNK // LANES)
                for s in range(4):
                    piece = lax.dot_general(keys[g, s], columns, NT, preferred_element_type=jnp.float32)
                    for r in range(0, nsel, 8):
                        mask = visible(r, s)
                        for n in range(CHUNK // LANES):
                            part = piece[r:r + 8, n * LANES:(n + 1) * LANES]
                            if mask is not None:
                                part = jnp.where(mask, part, MASKED)
                            scores[c, s, r:r + 8, n * LANES:(n + 1) * LANES] = part
                            tops[n] = part if tops[n] is None else jnp.maximum(tops[n], part)
                for n in range(CHUNK // LANES):
                    total = None
                    at = (c * CHUNK // LANES + n) * LANES
                    for r in range(0, nsel, 8):
                        parts = [
                            jnp.exp2((scores[c, s, r:r + 8, n * LANES:(n + 1) * LANES] - tops[n]) * scale)
                            for s in range(4)
                        ]
                        rest = parts[1] + parts[2] + parts[3]
                        pooled[0, r:r + 8, at:at + LANES] = parts[0]
                        pooled[1, r:r + 8, at:at + LANES] = rest
                        both = parts[0] + rest
                        total = both if total is None else total + both
                    top = jnp.max(tops[n], axis=0, keepdims=True)
                    lowered = jnp.exp2((tops[n] - top) * scale)
                    weights.append(lowered * (factor / jnp.sum(total * lowered, axis=0, keepdims=True)))
            for r in range(0, nsel, 8):
                lead, rest = [
                    sum(
                        (pooled[p, r:r + 8, n * LANES:(n + 1) * LANES] * weights[n] for n in range(1, len(weights))),
                        pooled[p, r:r + 8, 0:LANES] * weights[0],
                    )
                    for p in range(2)
                ]
                lined[0, 8 + r:16 + r, :] = lead
                lined[1, 8 + r:16 + r, :] = lead + 2.0 * rest
            lined[1, 0:8, :] = jnp.zeros((8, LANES), jnp.float32)
            blocks = lined[0, 8:8 + nsel, :] + lined[1, 7:7 + nsel, :]
            turned = blocks.T
            out_ref[pl.ds(begin, QTILE), g, :] = turned[:QTILE] + turned[QTILE:]
        return 0

    lax.fori_loop(0, tokens // QTILE, tile, 0)


def in_hbm(array):
    return pltpu.with_memory_space_constraint(array, pltpu.HBM)


def per_device(n_head, n_ctx, queries, keys, span_start, tile_first):
    tokens, key_heads, heads, depth = queries.shape
    blocks = keys.shape[0]
    own = key_heads // n_head
    nsel = blocks * n_ctx
    vmem = pl.BlockSpec(memory_space=pltpu.VMEM)
    smem = pl.BlockSpec(memory_space=pltpu.SMEM)
    hbm = pl.BlockSpec(memory_space=pltpu.HBM)
    q_part = jax.ShapeDtypeStruct((own, heads, tokens, depth), queries.dtype)
    k_part = jax.ShapeDtypeStruct((own, 4, blocks, depth), keys.dtype)
    packed = pl.pallas_call(
        partial(pack_kernel, n_head, key_heads, heads),
        out_shape=[q_part] * n_head + [k_part],
        in_specs=[hbm, hbm],
        out_specs=[vmem] * (n_head + 1),
        scratch_shapes=[
            pltpu.VMEM((tokens * key_heads * heads, depth), queries.dtype),
            pltpu.VMEM((blocks * 4 * key_heads, depth), keys.dtype),
            pltpu.SemaphoreType.DMA((Q_COPIES,)),
            pltpu.SemaphoreType.DMA((K_COPIES,)),
        ],
        compiler_params=pltpu.CompilerParams(vmem_limit_bytes=16 * 2 ** 20),
        name="pack",
    )(in_hbm(queries.reshape(-1, depth)), in_hbm(keys.reshape(-1, depth)))
    q_parts, k_parts = list(packed[:n_head]), [packed[n_head]] * n_ctx

    def send_keys(j):
        k_parts[j] = lax.ppermute(k_parts[0], "ctx", [(i, (i + j) % n_ctx) for i in range(n_ctx)])

    for d in range(1, n_head):
        q_parts[d] = lax.ppermute(q_parts[d], "head", [(i, i ^ d) for i in range(n_head)])
    for j in range(n_ctx - 1, 0, -1):
        send_keys(j)
    columns = n_head * heads * QTILE
    return pl.pallas_call(
        partial(main_kernel, n_head, n_ctx),
        out_shape=jax.ShapeDtypeStruct((tokens, own, nsel), jnp.float32),
        in_specs=[smem, smem] + [vmem] * (n_head + n_ctx),
        out_specs=vmem,
        scratch_shapes=[
            pltpu.VMEM((own, 4, nsel, depth), keys.dtype),
            pltpu.VMEM((columns // CHUNK, 4, nsel, CHUNK), jnp.float32),
            pltpu.VMEM((2, nsel, columns), jnp.float32),
            pltpu.VMEM((2, 8 + nsel, LANES), jnp.float32),
        ],
        compiler_params=pltpu.CompilerParams(vmem_limit_bytes=44 * 2 ** 20),
        name="importance",
    )(span_start, tile_first, *q_parts, *k_parts[::-1])


def solution(mesh):
    placed = (
        P(("groups", "ctx"), None, "head", None),
        P(("groups", "ctx"), None, None, None),
        P("groups"),
        P(("groups", "ctx")),
    )
    return jax.shard_map(
        partial(per_device, mesh.shape["head"], mesh.shape["ctx"]),
        mesh=mesh,
        in_specs=placed,
        out_specs=P(("groups", "ctx"), "head", None),
        check_vma=False,
    )
```

```python
import math
from functools import partial

import jax
import jax.numpy as jnp
from jax import lax
from jax.experimental import pallas as pl
from jax.experimental.pallas import tpu as pltpu
from jax.sharding import PartitionSpec as P

QTILE = 64
PACK = 16
LANES = 128
CHUNK = 256
MASKED = -1e30
NT = (((1,), (1,)), ((), ()))


def pack_keys_kernel(n_head, key_heads, k_hbm, k_out, k_ref, sem):
    copy = pltpu.make_async_copy(k_hbm, k_ref, sem)
    copy.start()
    me = lax.axis_index("head")
    own = key_heads // n_head
    blocks = k_out.shape[2]
    rows = PACK * 4 * key_heads
    out_row = lax.broadcasted_iota(jnp.int32, (own * 4 * PACK, rows), 0)
    in_row = lax.broadcasted_iota(jnp.int32, (own * 4 * PACK, rows), 1)
    head = out_row // (4 * PACK)
    part = out_row // PACK % 4
    source = out_row % PACK * (4 * key_heads) + part * key_heads + me * own + head
    select = jnp.where(in_row == source, 1.0, 0.0).astype(jnp.bfloat16)
    copy.wait()
    for block in range(blocks // PACK):
        moved = jnp.dot(
            select, k_ref[block * rows:(block + 1) * rows, :], preferred_element_type=jnp.float32
        ).astype(jnp.bfloat16)
        for u in range(own * 4):
            k_out[u // 4, u % 4, block * PACK:(block + 1) * PACK, :] = moved[u * PACK:(u + 1) * PACK]


def pack_queries_kernel(n_head, key_heads, heads, q_ref, *q_outs):
    me = lax.axis_index("head")
    width = key_heads // n_head * heads
    tokens = q_outs[0].shape[2]
    rows = PACK * key_heads * heads
    out_row = lax.broadcasted_iota(jnp.int32, (n_head * width * PACK, rows), 0)
    in_row = lax.broadcasted_iota(jnp.int32, (n_head * width * PACK, rows), 1)
    step = out_row // (width * PACK)
    unit = out_row // PACK % width
    source = out_row % PACK * (key_heads * heads) + (step ^ me) * width + unit
    select = jnp.where(in_row == source, 1.0, 0.0).astype(jnp.bfloat16)
    for block in range(tokens // PACK):
        moved = jnp.dot(
            select, q_ref[block * rows:(block + 1) * rows, :], preferred_element_type=jnp.float32
        ).astype(jnp.bfloat16)
        for u in range(n_head * width):
            d, g, h = u // width, u % width // heads, u % heads
            q_outs[d][g, h, block * PACK:(block + 1) * PACK, :] = moved[u * PACK:(u + 1) * PACK]


def main_kernel(n_head, n_ctx, start_ref, first_ref, *refs):
    q_refs, k_refs = refs[:n_head], refs[n_head:n_head + n_ctx]
    out_ref, keys, scores, pooled, lined = refs[n_head + n_ctx:]
    own, heads, tokens, depth = q_refs[0].shape
    local = k_refs[0].shape[2]
    nsel = local * n_ctx
    me = lax.axis_index("ctx")
    scale = math.log2(math.e) / math.sqrt(depth)
    factor = nsel / (2.0 * n_head * heads)
    least_position = 16 * 4 * nsel * 7 // 8 - n_ctx * tokens
    most_first = nsel - 1
    chunks = n_head * heads * QTILE // CHUNK
    per_chunk = n_head // chunks

    span = min(nsel, 256)
    spans = nsel // span

    def over_spans(body, carry):
        if spans == 1:
            return body(0, carry)
        return lax.fori_loop(0, spans, lambda n, c: body(pl.multiple_of(n * span, span), c), carry)

    for j in range(n_ctx):
        at = pl.ds(pl.multiple_of((me ^ j ^ (j >> 1)) * local, local), local)
        keys[:, :, at, :] = k_refs[j][...]

    def tile(index, _):
        begin = pl.multiple_of(index * QTILE, QTILE)
        first = first_ref[index]
        lane = lax.broadcasted_iota(jnp.int32, (8, LANES), 1)
        row = lax.broadcasted_iota(jnp.int32, (8, LANES), 0)
        place = start_ref[0] + me * tokens + begin + lane % QTILE

        def visible(base, r, s):
            i = 4 * (base + r + row) + s
            mask = None
            if spans > 1 or 4 * r + s <= most_first:
                mask = i >= first
            if spans > 1 or 16 * (4 * (r + 7) + s) + 31 > least_position:
                below = 16 * i + 31 <= place
                mask = below if mask is None else mask & below
            return mask

        for g in range(own):
            weights = []
            for c in range(chunks):
                columns = jnp.concatenate(
                    [q[g, h, pl.ds(begin, QTILE), :] for q in q_refs[c * per_chunk:(c + 1) * per_chunk] for h in range(heads)],
                    axis=0,
                )

                def scores_span(base, tops):
                    tops = list(tops)
                    rows = jnp.concatenate([keys[g, s, pl.ds(base, span), :] for s in range(4)], axis=0)
                    piece = lax.dot_general(rows, columns, NT, preferred_element_type=jnp.float32)
                    for s in range(4):
                        for r in range(0, span, 8):
                            mask = visible(base, r, s)
                            for n in range(CHUNK // LANES):
                                part = piece[s * span + r:s * span + r + 8, n * LANES:(n + 1) * LANES]
                                if mask is not None:
                                    part = jnp.where(mask, part, MASKED)
                                scores[c, s, pl.ds(base + r, 8), n * LANES:(n + 1) * LANES] = part
                                tops[n] = jnp.maximum(tops[n], part)
                    return tuple(tops)

                tops = over_spans(scores_span, (jnp.full((8, LANES), MASKED, jnp.float32),) * (CHUNK // LANES))
                for n in range(CHUNK // LANES):
                    at = (c * CHUNK // LANES + n) * LANES

                    def exps_span(base, total):
                        for r in range(0, span, 8):
                            here = pl.ds(base + r, 8)
                            parts = [
                                jnp.exp2((scores[c, s, here, n * LANES:(n + 1) * LANES] - tops[n]) * scale)
                                for s in range(4)
                            ]
                            rest = parts[1] + parts[2] + parts[3]
                            pooled[0, here, at:at + LANES] = parts[0]
                            pooled[1, here, at:at + LANES] = rest
                            total = total + (parts[0] + rest)
                        return total

                    total = over_spans(exps_span, jnp.zeros((8, LANES), jnp.float32))
                    top = jnp.max(tops[n], axis=0, keepdims=True)
                    lowered = jnp.exp2((tops[n] - top) * scale)
                    weights.append(lowered * (factor / jnp.sum(total * lowered, axis=0, keepdims=True)))

            def sums_span(base, _):
                for r in range(0, span, 8):
                    lead, rest = [
                        sum(
                            (pooled[p, pl.ds(base + r, 8), n * LANES:(n + 1) * LANES] * weights[n] for n in range(1, len(weights))),
                            pooled[p, pl.ds(base + r, 8), 0:LANES] * weights[0],
                        )
                        for p in range(2)
                    ]
                    lined[0, pl.ds(base + 8 + r, 8), :] = lead
                    lined[1, pl.ds(base + 8 + r, 8), :] = lead + 2.0 * rest
                return 0

            lined[1, 0:8, :] = jnp.zeros((8, LANES), jnp.float32)
            over_spans(sums_span, 0)
            blocks = lined[0, 8:8 + nsel, :] + lined[1, 7:7 + nsel, :]
            turned = blocks.T
            out_ref[pl.ds(begin, QTILE), g, :] = turned[:QTILE] + turned[QTILE:]
        return 0

    lax.fori_loop(0, tokens // QTILE, tile, 0)


def in_hbm(array):
    return pltpu.with_memory_space_constraint(array, pltpu.HBM)


def per_device(n_head, n_ctx, queries, keys, span_start, tile_first):
    tokens, key_heads, heads, depth = queries.shape
    blocks = keys.shape[0]
    own = key_heads // n_head
    nsel = blocks * n_ctx
    vmem = pl.BlockSpec(memory_space=pltpu.VMEM)
    smem = pl.BlockSpec(memory_space=pltpu.SMEM)
    hbm = pl.BlockSpec(memory_space=pltpu.HBM)
    q_part = jax.ShapeDtypeStruct((own, heads, tokens, depth), queries.dtype)
    k_part = jax.ShapeDtypeStruct((own, 4, blocks, depth), keys.dtype)
    k_own = pl.pallas_call(
        partial(pack_keys_kernel, n_head, key_heads),
        out_shape=k_part,
        in_specs=[hbm],
        out_specs=vmem,
        scratch_shapes=[pltpu.VMEM((blocks * 4 * key_heads, depth), keys.dtype), pltpu.SemaphoreType.DMA],
        compiler_params=pltpu.CompilerParams(vmem_limit_bytes=16 * 2 ** 20),
        name="pack_keys",
    )(in_hbm(keys.reshape(-1, depth)))
    q_parts = pl.pallas_call(
        partial(pack_queries_kernel, n_head, key_heads, heads),
        out_shape=[q_part] * n_head,
        in_specs=[vmem],
        out_specs=[vmem] * n_head,
        compiler_params=pltpu.CompilerParams(vmem_limit_bytes=16 * 2 ** 20),
        name="pack_queries",
    )(queries.reshape(-1, depth))
    q_parts, k_parts = list(q_parts), [k_own]
    for d in range(1, n_head):
        q_parts[d] = lax.ppermute(q_parts[d], "head", [(i, i ^ d) for i in range(n_head)])
    for j in range(1, n_ctx):
        k_parts.append(lax.ppermute(k_own, "ctx", [(i, i ^ j ^ (j >> 1)) for i in range(n_ctx)]))
    columns = n_head * heads * QTILE
    return pl.pallas_call(
        partial(main_kernel, n_head, n_ctx),
        out_shape=jax.ShapeDtypeStruct((tokens, own, nsel), jnp.float32),
        in_specs=[smem, smem] + [vmem] * (n_head + n_ctx),
        out_specs=vmem,
        scratch_shapes=[
            pltpu.VMEM((own, 4, nsel, depth), keys.dtype),
            pltpu.VMEM((columns // CHUNK, 4, nsel, CHUNK), jnp.float32),
            pltpu.VMEM((2, nsel, columns), jnp.float32),
            pltpu.VMEM((2, 8 + nsel, LANES), jnp.float32),
        ],
        compiler_params=pltpu.CompilerParams(vmem_limit_bytes=44 * 2 ** 20),
        name="importance",
    )(span_start, tile_first, *q_parts, *k_parts)


def solution(mesh):
    placed = (
        P(("groups", "ctx"), None, "head", None),
        P(("groups", "ctx"), None, None, None),
        P("groups"),
        P(("groups", "ctx")),
    )
    return jax.shard_map(
        partial(per_device, mesh.shape["head"], mesh.shape["ctx"]),
        mesh=mesh,
        in_specs=placed,
        out_specs=P(("groups", "ctx"), "head", None),
        check_vma=False,
    )
```

```python
import math
from functools import partial

import jax
import jax.numpy as jnp
from jax import lax
from jax.experimental import pallas as pl
from jax.experimental.pallas import tpu as pltpu
from jax.sharding import PartitionSpec as P

QTILE = 64
PACK = 16
K_COPIES = 2
Q_COPIES = 3
LANES = 128
CHUNK = 512
MASKED = -1e30
NT = (((1,), (1,)), ((), ()))


def pack_kernel(n_head, key_heads, heads, q_hbm, k_hbm, *refs):
    q_outs, (k_out, q_ref, k_ref, q_sems, k_sems) = refs[:n_head], refs[n_head:]
    me = lax.axis_index("head")
    own = key_heads // n_head
    width = own * heads
    tokens = q_outs[0].shape[2]
    blocks = k_out.shape[2]
    q_rows = PACK * key_heads * heads
    k_rows = PACK * 4 * key_heads
    k_copies, q_copies = [], []
    k_each, q_each = blocks // PACK // K_COPIES, tokens // PACK // Q_COPIES
    for n in range(K_COPIES):
        at = pl.ds(n * k_each * k_rows, k_each * k_rows)
        k_copies.append(pltpu.make_async_copy(k_hbm.at[at], k_ref.at[at], k_sems.at[n]))
    for n in range(Q_COPIES):
        at = pl.ds(n * q_each * q_rows, q_each * q_rows)
        q_copies.append(pltpu.make_async_copy(q_hbm.at[at], q_ref.at[at], q_sems.at[n]))
    for copy in k_copies + q_copies:
        copy.start()

    out_row = lax.broadcasted_iota(jnp.int32, (own * 4 * PACK, k_rows), 0)
    in_row = lax.broadcasted_iota(jnp.int32, (own * 4 * PACK, k_rows), 1)
    head = out_row // (4 * PACK)
    part = out_row // PACK % 4
    source = out_row % PACK * (4 * key_heads) + part * key_heads + me * own + head
    select = jnp.where(in_row == source, 1.0, 0.0).astype(jnp.bfloat16)
    for block in range(blocks // PACK):
        if block % k_each == 0:
            k_copies[block // k_each].wait()
        moved = jnp.dot(
            select, k_ref[block * k_rows:(block + 1) * k_rows, :], preferred_element_type=jnp.float32
        ).astype(jnp.bfloat16)
        for u in range(own * 4):
            k_out[u // 4, u % 4, block * PACK:(block + 1) * PACK, :] = moved[u * PACK:(u + 1) * PACK]

    out_row = lax.broadcasted_iota(jnp.int32, (n_head * width * PACK, q_rows), 0)
    in_row = lax.broadcasted_iota(jnp.int32, (n_head * width * PACK, q_rows), 1)
    step = out_row // (width * PACK)
    unit = out_row // PACK % width
    source = out_row % PACK * (key_heads * heads) + (step ^ me) * width + unit
    select = jnp.where(in_row == source, 1.0, 0.0).astype(jnp.bfloat16)
    for block in range(tokens // PACK):
        if block % q_each == 0:
            q_copies[block // q_each].wait()
        moved = jnp.dot(
            select, q_ref[block * q_rows:(block + 1) * q_rows, :], preferred_element_type=jnp.float32
        ).astype(jnp.bfloat16)
        for u in range(n_head * width):
            d, g, h = u // width, u % width // heads, u % heads
            q_outs[d][g, h, block * PACK:(block + 1) * PACK, :] = moved[u * PACK:(u + 1) * PACK]


def main_kernel(n_head, n_ctx, start_ref, first_ref, *refs):
    q_refs, k_refs = refs[:n_head], refs[n_head:n_head + n_ctx]
    out_ref, keys, scores, pooled, lined = refs[n_head + n_ctx:]
    own, heads, tokens, depth = q_refs[0].shape
    local = k_refs[0].shape[2]
    nsel = local * n_ctx
    me = lax.axis_index("ctx")
    scale = math.log2(math.e) / math.sqrt(depth)
    factor = nsel / (2.0 * n_head * heads)
    least_position = 16 * 4 * nsel * 7 // 8 - n_ctx * tokens
    most_first = nsel - 1
    chunks = n_head * heads * QTILE // CHUNK
    per_chunk = n_head // chunks

    span = min(nsel, 256)
    spans = nsel // span

    def over_spans(body, carry):
        if spans == 1:
            return body(0, carry)
        return lax.fori_loop(0, spans, lambda n, c: body(pl.multiple_of(n * span, span), c), carry)

    for j in range(n_ctx):
        at = pl.ds(pl.multiple_of((me ^ j) * local, local), local)
        keys[:, :, at, :] = k_refs[j][...]

    def tile(index, _):
        begin = pl.multiple_of(index * QTILE, QTILE)
        first = first_ref[index]
        lane = lax.broadcasted_iota(jnp.int32, (8, LANES), 1)
        row = lax.broadcasted_iota(jnp.int32, (8, LANES), 0)
        place = start_ref[0] + me * tokens + begin + lane % QTILE

        def visible(base, r, s):
            i = 4 * (base + r + row) + s
            mask = None
            if spans > 1 or 4 * r + s <= most_first:
                mask = i >= first
            if spans > 1 or 16 * (4 * (r + 7) + s) + 31 > least_position:
                below = 16 * i + 31 <= place
                mask = below if mask is None else mask & below
            return mask

        for g in range(own):
            weights = []
            for c in range(chunks):
                columns = jnp.concatenate(
                    [q[g, h, pl.ds(begin, QTILE), :] for q in q_refs[c * per_chunk:(c + 1) * per_chunk] for h in range(heads)],
                    axis=0,
                )

                def scores_span(base, tops):
                    tops = list(tops)
                    rows = jnp.concatenate([keys[g, s, pl.ds(base, span), :] for s in range(4)], axis=0)
                    piece = lax.dot_general(rows, columns, NT, preferred_element_type=jnp.float32)
                    for s in range(4):
                        for r in range(0, span, 8):
                            mask = visible(base, r, s)
                            for n in range(CHUNK // LANES):
                                part = piece[s * span + r:s * span + r + 8, n * LANES:(n + 1) * LANES]
                                if mask is not None:
                                    part = jnp.where(mask, part, MASKED)
                                scores[c, s, pl.ds(base + r, 8), n * LANES:(n + 1) * LANES] = part
                                tops[n] = jnp.maximum(tops[n], part)
                    return tuple(tops)

                tops = over_spans(scores_span, (jnp.full((8, LANES), MASKED, jnp.float32),) * (CHUNK // LANES))
                for n in range(CHUNK // LANES):
                    at = (c * CHUNK // LANES + n) * LANES

                    def exps_span(base, total):
                        for r in range(0, span, 8):
                            here = pl.ds(base + r, 8)
                            parts = [
                                jnp.exp2((scores[c, s, here, n * LANES:(n + 1) * LANES] - tops[n]) * scale)
                                for s in range(4)
                            ]
                            rest = parts[1] + parts[2] + parts[3]
                            pooled[0, here, at:at + LANES] = parts[0]
                            pooled[1, here, at:at + LANES] = rest
                            total = total + (parts[0] + rest)
                        return total

                    total = over_spans(exps_span, jnp.zeros((8, LANES), jnp.float32))
                    top = jnp.max(tops[n], axis=0, keepdims=True)
                    lowered = jnp.exp2((tops[n] - top) * scale)
                    weights.append(lowered * (factor / jnp.sum(total * lowered, axis=0, keepdims=True)))

            def sums_span(base, _):
                for r in range(0, span, 8):
                    lead, rest = [
                        sum(
                            (pooled[p, pl.ds(base + r, 8), n * LANES:(n + 1) * LANES] * weights[n] for n in range(1, len(weights))),
                            pooled[p, pl.ds(base + r, 8), 0:LANES] * weights[0],
                        )
                        for p in range(2)
                    ]
                    lined[0, pl.ds(base + 8 + r, 8), :] = lead
                    lined[1, pl.ds(base + 8 + r, 8), :] = lead + 2.0 * rest
                return 0

            lined[1, 0:8, :] = jnp.zeros((8, LANES), jnp.float32)
            over_spans(sums_span, 0)
            blocks = lined[0, 8:8 + nsel, :] + lined[1, 7:7 + nsel, :]
            turned = blocks.T
            out_ref[pl.ds(begin, QTILE), g, :] = turned[:QTILE] + turned[QTILE:]
        return 0

    lax.fori_loop(0, tokens // QTILE, tile, 0)


def in_hbm(array):
    return pltpu.with_memory_space_constraint(array, pltpu.HBM)


def per_device(n_head, n_ctx, queries, keys, span_start, tile_first):
    tokens, key_heads, heads, depth = queries.shape
    blocks = keys.shape[0]
    own = key_heads // n_head
    nsel = blocks * n_ctx
    vmem = pl.BlockSpec(memory_space=pltpu.VMEM)
    smem = pl.BlockSpec(memory_space=pltpu.SMEM)
    hbm = pl.BlockSpec(memory_space=pltpu.HBM)
    q_part = jax.ShapeDtypeStruct((own, heads, tokens, depth), queries.dtype)
    k_part = jax.ShapeDtypeStruct((own, 4, blocks, depth), keys.dtype)
    packed = pl.pallas_call(
        partial(pack_kernel, n_head, key_heads, heads),
        out_shape=[q_part] * n_head + [k_part],
        in_specs=[hbm, hbm],
        out_specs=[vmem] * (n_head + 1),
        scratch_shapes=[
            pltpu.VMEM((tokens * key_heads * heads, depth), queries.dtype),
            pltpu.VMEM((blocks * 4 * key_heads, depth), keys.dtype),
            pltpu.SemaphoreType.DMA((Q_COPIES,)),
            pltpu.SemaphoreType.DMA((K_COPIES,)),
        ],
        compiler_params=pltpu.CompilerParams(vmem_limit_bytes=16 * 2 ** 20),
        name="pack",
    )(in_hbm(queries.reshape(-1, depth)), in_hbm(keys.reshape(-1, depth)))
    q_parts, k_parts = list(packed[:n_head]), [packed[n_head]]

    def swap(array, axis, size, bit):
        return lax.ppermute(array, axis, [(i, i ^ bit) for i in range(size)])

    for d in range(1, n_head):
        q_parts[d] = swap(q_parts[d], "head", n_head, d)
    bit = n_ctx // 2
    k_parts = {0: packed[n_head]}
    while bit:
        for j in list(k_parts):
            k_parts[j | bit] = swap(k_parts[j], "ctx", n_ctx, bit)
        bit //= 2
    k_parts = [k_parts[j] for j in range(n_ctx)]
    columns = n_head * heads * QTILE
    return pl.pallas_call(
        partial(main_kernel, n_head, n_ctx),
        out_shape=jax.ShapeDtypeStruct((tokens, own, nsel), jnp.float32),
        in_specs=[smem, smem] + [vmem] * (n_head + n_ctx),
        out_specs=vmem,
        scratch_shapes=[
            pltpu.VMEM((own, 4, nsel, depth), keys.dtype),
            pltpu.VMEM((columns // CHUNK, 4, nsel, CHUNK), jnp.float32),
            pltpu.VMEM((2, nsel, columns), jnp.float32),
            pltpu.VMEM((2, 8 + nsel, LANES), jnp.float32),
        ],
        compiler_params=pltpu.CompilerParams(vmem_limit_bytes=44 * 2 ** 20),
        name="importance",
    )(span_start, tile_first, *q_parts, *k_parts)


def solution(mesh):
    placed = (
        P(("groups", "ctx"), None, "head", None),
        P(("groups", "ctx"), None, None, None),
        P("groups"),
        P(("groups", "ctx")),
    )
    return jax.shard_map(
        partial(per_device, mesh.shape["head"], mesh.shape["ctx"]),
        mesh=mesh,
        in_specs=placed,
        out_specs=P(("groups", "ctx"), "head", None),
        check_vma=False,
    )
```

```python
import math
from functools import partial

import jax
import jax.numpy as jnp
from jax import lax
from jax.experimental import pallas as pl
from jax.experimental.pallas import tpu as pltpu
from jax.sharding import PartitionSpec as P

QTILE = 64
PACK = 16
K_COPIES = 2
Q_COPIES = 3
LANES = 128
CHUNK = 512
SPAN_ROWS = 256
MASKED = -1e30
NT = (((1,), (1,)), ((), ()))


def pack_kernel(n_head, key_heads, heads, q_hbm, k_hbm, *refs):
    q_outs, (k_out, q_ref, k_ref, q_sems, k_sems) = refs[:n_head], refs[n_head:]
    me = lax.axis_index("head")
    own = key_heads // n_head
    width = own * heads
    tokens = q_outs[0].shape[2]
    blocks = k_out.shape[2]
    q_rows = PACK * key_heads * heads
    k_rows = PACK * 4 * key_heads
    k_copies, q_copies = [], []
    k_each, q_each = blocks // PACK // K_COPIES, tokens // PACK // Q_COPIES
    for n in range(K_COPIES):
        at = pl.ds(n * k_each * k_rows, k_each * k_rows)
        k_copies.append(pltpu.make_async_copy(k_hbm.at[at], k_ref.at[at], k_sems.at[n]))
    for n in range(Q_COPIES):
        at = pl.ds(n * q_each * q_rows, q_each * q_rows)
        q_copies.append(pltpu.make_async_copy(q_hbm.at[at], q_ref.at[at], q_sems.at[n]))
    for copy in k_copies + q_copies:
        copy.start()

    out_row = lax.broadcasted_iota(jnp.int32, (own * 4 * PACK, k_rows), 0)
    in_row = lax.broadcasted_iota(jnp.int32, (own * 4 * PACK, k_rows), 1)
    head = out_row // (4 * PACK)
    part = out_row // PACK % 4
    source = out_row % PACK * (4 * key_heads) + part * key_heads + me * own + head
    select = jnp.where(in_row == source, 1.0, 0.0).astype(jnp.bfloat16)
    for block in range(blocks // PACK):
        if block % k_each == 0:
            k_copies[block // k_each].wait()
        moved = jnp.dot(
            select, k_ref[block * k_rows:(block + 1) * k_rows, :], preferred_element_type=jnp.float32
        ).astype(jnp.bfloat16)
        for u in range(own * 4):
            k_out[u // 4, u % 4, block * PACK:(block + 1) * PACK, :] = moved[u * PACK:(u + 1) * PACK]

    out_row = lax.broadcasted_iota(jnp.int32, (n_head * width * PACK, q_rows), 0)
    in_row = lax.broadcasted_iota(jnp.int32, (n_head * width * PACK, q_rows), 1)
    step = out_row // (width * PACK)
    unit = out_row // PACK % width
    source = out_row % PACK * (key_heads * heads) + (step ^ me) * width + unit
    select = jnp.where(in_row == source, 1.0, 0.0).astype(jnp.bfloat16)
    for block in range(tokens // PACK):
        if block % q_each == 0:
            q_copies[block // q_each].wait()
        moved = jnp.dot(
            select, q_ref[block * q_rows:(block + 1) * q_rows, :], preferred_element_type=jnp.float32
        ).astype(jnp.bfloat16)
        for u in range(n_head * width):
            d, g, h = u // width, u % width // heads, u % heads
            q_outs[d][g, h, block * PACK:(block + 1) * PACK, :] = moved[u * PACK:(u + 1) * PACK]


def gather_keys(n_ctx, k_refs, keys):
    me = lax.axis_index("ctx")
    local = k_refs[0].shape[2]
    for j in range(n_ctx):
        at = pl.ds(pl.multiple_of((me ^ j) * local, local), local)
        keys[:, :, at, :] = k_refs[j][...]


def limits(n_ctx, tokens, begin, start_ref):
    lane = lax.broadcasted_iota(jnp.int32, (8, LANES), 1)
    row = lax.broadcasted_iota(jnp.int32, (8, LANES), 0)
    place = start_ref[0] + lax.axis_index("ctx") * tokens + begin + lane % QTILE
    return 4 * row, place - 31 - 64 * row


def visible(nsel, span_tokens, r, s, first, row4, reach, base=None):
    least_position = 16 * 4 * nsel * 7 // 8 - span_tokens
    most_first = nsel - 1
    at = r if base is None else base + r
    mask = None
    if base is not None or 4 * r + s <= most_first:
        mask = row4 >= first - (4 * at + s)
    if base is not None or 16 * (4 * (r + 7) + s) + 31 > least_position:
        below = reach >= 64 * at + 16 * s
        mask = below if mask is None else mask & below
    return mask


def tile_columns(q_refs, g, begin):
    return jnp.concatenate(
        [q[g, h, pl.ds(begin, QTILE), :] for q in q_refs for h in range(q.shape[1])], axis=0
    )


def interleave(*stages):
    lengths = [length for length, _ in stages]
    done = [0] * len(stages)
    for tick in range(1, max(lengths) + 1):
        for n, (length, stage) in enumerate(stages):
            while done[n] * max(lengths) < tick * length:
                next(stage, None)
                done[n] += 1
    for _, stage in stages:
        for _ in stage:
            pass


def unit_kernel(n_head, n_ctx, start_ref, first_ref, *refs):
    q_refs, k_refs = refs[:n_head], refs[n_head:n_head + n_ctx]
    out_ref, keys, scores, pooled, lined = refs[n_head + n_ctx:]
    own, heads, tokens, depth = q_refs[0].shape
    nsel = keys.shape[2]
    scale = math.log2(math.e) / math.sqrt(depth)
    factor = nsel / (2.0 * n_head * heads)
    tiles_n = n_head * heads * QTILE // LANES
    block = 64
    gather_keys(n_ctx, k_refs, keys)
    units = [(t, g) for t in range(tokens // QTILE) for g in range(own)]
    tops, weights = {}, {}

    def products(u):
        t, g = units[u]
        columns = tile_columns(q_refs, g, t * QTILE)
        row4, reach = limits(n_ctx, tokens, t * QTILE, start_ref)
        first = first_ref[t]
        top = [None] * tiles_n
        for base in range(0, nsel, block):
            rows = jnp.concatenate([keys[g, s, base:base + block, :] for s in range(4)], axis=0)
            piece = lax.dot_general(rows, columns, NT, preferred_element_type=jnp.float32)
            for s in range(4):
                for r in range(0, block, 8):
                    mask = visible(nsel, n_ctx * tokens, base + r, s, first, row4, reach)
                    for n in range(tiles_n):
                        part = piece[s * block + r:s * block + r + 8, n * LANES:(n + 1) * LANES]
                        if mask is not None:
                            part = jnp.where(mask, part, MASKED)
                        scores[u % 2, s, base + r:base + r + 8, n * LANES:(n + 1) * LANES] = part
                        top[n] = part if top[n] is None else jnp.maximum(top[n], part)
                yield
        tops[u] = top

    def exponentials(u):
        weights[u] = []
        for n in range(tiles_n):
            top, total = tops[u][n], None
            at = slice(n * LANES, (n + 1) * LANES)
            for r in range(0, nsel, 8):
                parts = [jnp.exp2((scores[u % 2, s, r:r + 8, at] - top) * scale) for s in range(4)]
                rest = parts[1] + parts[2] + parts[3]
                pooled[u % 2, 0, r:r + 8, at] = parts[0]
                pooled[u % 2, 1, r:r + 8, at] = rest
                both = parts[0] + rest
                total = both if total is None else total + both
                if r % 32 == 24:
                    yield
            peak = jnp.max(top, axis=0, keepdims=True)
            lowered = jnp.exp2((top - peak) * scale)
            weights[u].append(lowered * (factor / jnp.sum(total * lowered, axis=0, keepdims=True)))

    def sums(u):
        t, g = units[u]
        lined[u % 2, 1, 0:8, :] = jnp.zeros((8, LANES), jnp.float32)
        for r in range(0, nsel, 8):
            lead, rest = None, None
            for n in range(tiles_n):
                at = slice(n * LANES, (n + 1) * LANES)
                first, second = pooled[u % 2, 0, r:r + 8, at] * weights[u][n], pooled[u % 2, 1, r:r + 8, at] * weights[u][n]
                lead = first if lead is None else lead + first
                rest = second if rest is None else rest + second
            lined[u % 2, 0, 8 + r:16 + r, :] = lead
            lined[u % 2, 1, 8 + r:16 + r, :] = lead + 2.0 * rest
            if r % 16 == 8:
                yield
        turned = (lined[u % 2, 0, 8:8 + nsel, :] + lined[u % 2, 1, 7:7 + nsel, :]).T
        out_ref[t * QTILE:(t + 1) * QTILE, g, :] = turned[:QTILE] + turned[QTILE:]
        yield

    for step in range(len(units) + 2):
        stages = []
        if step < len(units):
            stages.append((4 * nsel // block, products(step)))
        if 0 <= step - 1 < len(units):
            stages.append((tiles_n * nsel // 32, exponentials(step - 1)))
        if step >= 2:
            stages.append((nsel // 16 + 1, sums(step - 2)))
        interleave(*stages)


def span_kernel(n_head, n_ctx, start_ref, first_ref, *refs):
    q_refs, k_refs = refs[:n_head], refs[n_head:n_head + n_ctx]
    out_ref, keys, scores, pooled, lined = refs[n_head + n_ctx:]
    own, heads, tokens, depth = q_refs[0].shape
    nsel = keys.shape[2]
    scale = math.log2(math.e) / math.sqrt(depth)
    factor = nsel / (2.0 * n_head * heads)
    chunks = n_head * heads * QTILE // CHUNK
    per_chunk = n_head // chunks

    span = SPAN_ROWS
    spans = nsel // span

    def over_spans(body, carry):
        return lax.fori_loop(0, spans, lambda n, c: body(pl.multiple_of(n * span, span), c), carry)

    gather_keys(n_ctx, k_refs, keys)

    def tile(index, _):
        begin = pl.multiple_of(index * QTILE, QTILE)
        first = first_ref[index]
        row4, reach = limits(n_ctx, tokens, begin, start_ref)

        for g in range(own):
            weights = []
            for c in range(chunks):
                columns = tile_columns(q_refs[c * per_chunk:(c + 1) * per_chunk], g, begin)

                def scores_span(base, tops):
                    tops = list(tops)
                    rows = jnp.concatenate([keys[g, s, pl.ds(base, span), :] for s in range(4)], axis=0)
                    piece = lax.dot_general(rows, columns, NT, preferred_element_type=jnp.float32)
                    for s in range(4):
                        for r in range(0, span, 8):
                            mask = visible(nsel, n_ctx * tokens, r, s, first, row4, reach, base)
                            for n in range(CHUNK // LANES):
                                part = piece[s * span + r:s * span + r + 8, n * LANES:(n + 1) * LANES]
                                if mask is not None:
                                    part = jnp.where(mask, part, MASKED)
                                scores[0, s, pl.ds(base + r, 8), n * LANES:(n + 1) * LANES] = part
                                tops[n] = jnp.maximum(tops[n], part)
                    return tuple(tops)

                tops = over_spans(scores_span, (jnp.full((8, LANES), MASKED, jnp.float32),) * (CHUNK // LANES))
                for n in range(CHUNK // LANES):
                    at = (c * CHUNK // LANES + n) * LANES

                    def exps_span(base, total):
                        for r in range(0, span, 8):
                            here = pl.ds(base + r, 8)
                            parts = [
                                jnp.exp2((scores[0, s, here, n * LANES:(n + 1) * LANES] - tops[n]) * scale)
                                for s in range(4)
                            ]
                            rest = parts[1] + parts[2] + parts[3]
                            pooled[0, 0, here, at:at + LANES] = parts[0]
                            pooled[0, 1, here, at:at + LANES] = rest
                            total = total + (parts[0] + rest)
                        return total

                    total = over_spans(exps_span, jnp.zeros((8, LANES), jnp.float32))
                    top = jnp.max(tops[n], axis=0, keepdims=True)
                    lowered = jnp.exp2((tops[n] - top) * scale)
                    weights.append(lowered * (factor / jnp.sum(total * lowered, axis=0, keepdims=True)))

            def sums_span(base, _):
                for r in range(0, span, 8):
                    lead, rest = [
                        sum(
                            (pooled[0, p, pl.ds(base + r, 8), n * LANES:(n + 1) * LANES] * weights[n] for n in range(1, len(weights))),
                            pooled[0, p, pl.ds(base + r, 8), 0:LANES] * weights[0],
                        )
                        for p in range(2)
                    ]
                    lined[0, 0, pl.ds(base + 8 + r, 8), :] = lead
                    lined[0, 1, pl.ds(base + 8 + r, 8), :] = lead + 2.0 * rest
                return 0

            lined[0, 1, 0:8, :] = jnp.zeros((8, LANES), jnp.float32)
            over_spans(sums_span, 0)
            blocks = lined[0, 0, 8:8 + nsel, :] + lined[0, 1, 7:7 + nsel, :]
            turned = blocks.T
            out_ref[pl.ds(begin, QTILE), g, :] = turned[:QTILE] + turned[QTILE:]
        return 0

    lax.fori_loop(0, tokens // QTILE, tile, 0)


def in_hbm(array):
    return pltpu.with_memory_space_constraint(array, pltpu.HBM)


def per_device(n_head, n_ctx, queries, keys, span_start, tile_first):
    tokens, key_heads, heads, depth = queries.shape
    blocks = keys.shape[0]
    own = key_heads // n_head
    nsel = blocks * n_ctx
    vmem = pl.BlockSpec(memory_space=pltpu.VMEM)
    smem = pl.BlockSpec(memory_space=pltpu.SMEM)
    hbm = pl.BlockSpec(memory_space=pltpu.HBM)
    q_part = jax.ShapeDtypeStruct((own, heads, tokens, depth), queries.dtype)
    k_part = jax.ShapeDtypeStruct((own, 4, blocks, depth), keys.dtype)
    packed = pl.pallas_call(
        partial(pack_kernel, n_head, key_heads, heads),
        out_shape=[q_part] * n_head + [k_part],
        in_specs=[hbm, hbm],
        out_specs=[vmem] * (n_head + 1),
        scratch_shapes=[
            pltpu.VMEM((tokens * key_heads * heads, depth), queries.dtype),
            pltpu.VMEM((blocks * 4 * key_heads, depth), keys.dtype),
            pltpu.SemaphoreType.DMA((Q_COPIES,)),
            pltpu.SemaphoreType.DMA((K_COPIES,)),
        ],
        compiler_params=pltpu.CompilerParams(vmem_limit_bytes=16 * 2 ** 20),
        name="pack",
    )(in_hbm(queries.reshape(-1, depth)), in_hbm(keys.reshape(-1, depth)))
    q_parts, k_parts = list(packed[:n_head]), [packed[n_head]]

    def swap(array, axis, size, bit):
        return lax.ppermute(array, axis, [(i, i ^ bit) for i in range(size)])

    for d in range(1, n_head):
        q_parts[d] = swap(q_parts[d], "head", n_head, d)
    bit = n_ctx // 2
    k_parts = {0: packed[n_head]}
    while bit:
        for j in list(k_parts):
            k_parts[j | bit] = swap(k_parts[j], "ctx", n_ctx, bit)
        bit //= 2
    k_parts = [k_parts[j] for j in range(n_ctx)]
    columns = n_head * heads * QTILE
    buffers = 2 if nsel <= SPAN_ROWS else 1
    return pl.pallas_call(
        partial(unit_kernel if buffers == 2 else span_kernel, n_head, n_ctx),
        out_shape=jax.ShapeDtypeStruct((tokens, own, nsel), jnp.float32),
        in_specs=[smem, smem] + [vmem] * (n_head + n_ctx),
        out_specs=vmem,
        scratch_shapes=[
            pltpu.VMEM((own, 4, nsel, depth), keys.dtype),
            pltpu.VMEM((buffers, 4, nsel, columns), jnp.float32),
            pltpu.VMEM((buffers, 2, nsel, columns), jnp.float32),
            pltpu.VMEM((buffers, 2, 8 + nsel, LANES), jnp.float32),
        ],
        compiler_params=pltpu.CompilerParams(vmem_limit_bytes=(20 if buffers == 2 else 52) * 2 ** 20),
        name="importance",
    )(span_start, tile_first, *q_parts, *k_parts)


def solution(mesh):
    placed = (
        P(("groups", "ctx"), None, "head", None),
        P(("groups", "ctx"), None, None, None),
        P("groups"),
        P(("groups", "ctx")),
    )
    return jax.shard_map(
        partial(per_device, mesh.shape["head"], mesh.shape["ctx"]),
        mesh=mesh,
        in_specs=placed,
        out_specs=P(("groups", "ctx"), "head", None),
        check_vma=False,
    )
```

```python
import math
from functools import partial

import jax
import jax.numpy as jnp
from jax import lax
from jax.experimental import pallas as pl
from jax.experimental.pallas import tpu as pltpu
from jax.sharding import PartitionSpec as P

QTILE = 64
PACK = 16
K_COPIES = 2
Q_COPIES = 3
LANES = 128
CHUNK = 512
SPAN_ROWS = 256
MASKED = -1e30
NT = (((1,), (1,)), ((), ()))


def pack_kernel(n_head, key_heads, heads, q_hbm, k_hbm, *refs):
    me = lax.axis_index("head")
    own = key_heads // n_head
    q_outs, k_outs = refs[:n_head * own], refs[n_head * own:(n_head + 1) * own]
    q_ref, k_ref, q_sems, k_sems = refs[(n_head + 1) * own:]
    width = own * heads
    tokens = q_outs[0].shape[1]
    blocks = k_outs[0].shape[1]
    q_rows = PACK * key_heads * heads
    k_rows = PACK * 4 * key_heads
    k_copies, q_copies = [], []
    k_each, q_each = blocks // PACK // K_COPIES, tokens // PACK // Q_COPIES
    for n in range(K_COPIES):
        at = pl.ds(n * k_each * k_rows, k_each * k_rows)
        k_copies.append(pltpu.make_async_copy(k_hbm.at[at], k_ref.at[at], k_sems.at[n]))
    for n in range(Q_COPIES):
        at = pl.ds(n * q_each * q_rows, q_each * q_rows)
        q_copies.append(pltpu.make_async_copy(q_hbm.at[at], q_ref.at[at], q_sems.at[n]))
    for copy in k_copies + q_copies:
        copy.start()

    out_row = lax.broadcasted_iota(jnp.int32, (own * 4 * PACK, k_rows), 0)
    in_row = lax.broadcasted_iota(jnp.int32, (own * 4 * PACK, k_rows), 1)
    head = out_row // (4 * PACK)
    part = out_row // PACK % 4
    source = out_row % PACK * (4 * key_heads) + part * key_heads + me * own + head
    select = jnp.where(in_row == source, 1.0, 0.0).astype(jnp.bfloat16)
    for block in range(blocks // PACK):
        if block % k_each == 0:
            k_copies[block // k_each].wait()
        moved = jnp.dot(
            select, k_ref[block * k_rows:(block + 1) * k_rows, :], preferred_element_type=jnp.float32
        ).astype(jnp.bfloat16)
        for u in range(own * 4):
            k_outs[u // 4][u % 4, block * PACK:(block + 1) * PACK, :] = moved[u * PACK:(u + 1) * PACK]

    out_row = lax.broadcasted_iota(jnp.int32, (n_head * width * PACK, q_rows), 0)
    in_row = lax.broadcasted_iota(jnp.int32, (n_head * width * PACK, q_rows), 1)
    step = out_row // (width * PACK)
    unit = out_row // PACK % width
    source = out_row % PACK * (key_heads * heads) + (step ^ me) * width + unit
    select = jnp.where(in_row == source, 1.0, 0.0).astype(jnp.bfloat16)
    for block in range(tokens // PACK):
        if block % q_each == 0:
            q_copies[block // q_each].wait()
        moved = jnp.dot(
            select, q_ref[block * q_rows:(block + 1) * q_rows, :], preferred_element_type=jnp.float32
        ).astype(jnp.bfloat16)
        for u in range(n_head * width):
            d, g, h = u // width, u % width // heads, u % heads
            q_outs[g * n_head + d][h, block * PACK:(block + 1) * PACK, :] = moved[u * PACK:(u + 1) * PACK]


def gather_keys(n_ctx, k_refs, keys):
    me = lax.axis_index("ctx")
    local = k_refs[0].shape[1]
    for j in range(n_ctx):
        at = pl.ds(pl.multiple_of((me ^ j) * local, local), local)
        keys[:, at, :] = k_refs[j][...]


def limits(n_ctx, tokens, begin, start_ref):
    lane = lax.broadcasted_iota(jnp.int32, (8, LANES), 1)
    row = lax.broadcasted_iota(jnp.int32, (8, LANES), 0)
    place = start_ref[0] + lax.axis_index("ctx") * tokens + begin + lane % QTILE
    return 4 * row, place - 31 - 64 * row


def visible(nsel, span_tokens, r, s, first, row4, reach, base=None):
    least_position = 16 * 4 * nsel * 7 // 8 - span_tokens
    most_first = nsel - 1
    at = r if base is None else base + r
    mask = None
    if base is not None or 4 * r + s <= most_first:
        mask = row4 >= first - (4 * at + s)
    if base is not None or 16 * (4 * (r + 7) + s) + 31 > least_position:
        below = reach >= 64 * at + 16 * s
        mask = below if mask is None else mask & below
    return mask


def tile_columns(q_refs, begin):
    return jnp.concatenate(
        [q[h, pl.ds(begin, QTILE), :] for q in q_refs for h in range(q.shape[0])], axis=0
    )


def take_refs(n_head, n_ctx, refs):
    q_refs, k_refs, refs = refs[:n_head], refs[n_head:n_head + n_ctx], refs[n_head + n_ctx:]
    earlier, (out_ref, keys, scores, pooled, lined) = refs[:-5], refs[-5:]
    return q_refs, k_refs, earlier, out_ref, keys, scores, pooled, lined


def put(out_ref, g, rows, value):
    if len(out_ref.shape) == 2:
        out_ref[rows, :] = value
    else:
        out_ref[rows, g, :] = value


def interleave(*stages):
    lengths = [length for length, _ in stages]
    done = [0] * len(stages)
    for tick in range(1, max(lengths) + 1):
        for n, (length, stage) in enumerate(stages):
            while done[n] * max(lengths) < tick * length:
                next(stage, None)
                done[n] += 1
    for _, stage in stages:
        for _ in stage:
            pass


def unit_kernel(n_head, n_ctx, start_ref, first_ref, *refs):
    q_refs, k_refs, earlier, out_ref, keys, scores, pooled, lined = take_refs(n_head, n_ctx, refs)
    heads, tokens, depth = q_refs[0].shape
    nsel, g = keys.shape[1], len(earlier)
    scale = math.log2(math.e) / math.sqrt(depth)
    factor = nsel / (2.0 * n_head * heads)
    tiles_n = n_head * heads * QTILE // LANES
    block = 64
    gather_keys(n_ctx, k_refs, keys)
    for n, ref in enumerate(earlier):
        put(out_ref, n, slice(None), ref[...])
    units = list(range(tokens // QTILE))
    tops, weights = {}, {}

    def products(u):
        t = units[u]
        columns = tile_columns(q_refs, t * QTILE)
        row4, reach = limits(n_ctx, tokens, t * QTILE, start_ref)
        first = first_ref[t]
        top = [None] * tiles_n
        for base in range(0, nsel, block):
            rows = jnp.concatenate([keys[s, base:base + block, :] for s in range(4)], axis=0)
            piece = lax.dot_general(rows, columns, NT, preferred_element_type=jnp.float32)
            for s in range(4):
                for r in range(0, block, 8):
                    mask = visible(nsel, n_ctx * tokens, base + r, s, first, row4, reach)
                    for n in range(tiles_n):
                        part = piece[s * block + r:s * block + r + 8, n * LANES:(n + 1) * LANES]
                        if mask is not None:
                            part = jnp.where(mask, part, MASKED)
                        scores[u % 2, s, base + r:base + r + 8, n * LANES:(n + 1) * LANES] = part
                        top[n] = part if top[n] is None else jnp.maximum(top[n], part)
                yield
        tops[u] = top

    def exponentials(u):
        weights[u] = []
        for n in range(tiles_n):
            top, total = tops[u][n], None
            at = slice(n * LANES, (n + 1) * LANES)
            for r in range(0, nsel, 8):
                parts = [jnp.exp2((scores[u % 2, s, r:r + 8, at] - top) * scale) for s in range(4)]
                rest = parts[1] + parts[2] + parts[3]
                pooled[u % 2, 0, r:r + 8, at] = parts[0]
                pooled[u % 2, 1, r:r + 8, at] = rest
                both = parts[0] + rest
                total = both if total is None else total + both
                if r % 32 == 24:
                    yield
            peak = jnp.max(top, axis=0, keepdims=True)
            lowered = jnp.exp2((top - peak) * scale)
            weights[u].append(lowered * (factor / jnp.sum(total * lowered, axis=0, keepdims=True)))

    def sums(u):
        t = units[u]
        lined[u % 2, 1, 0:8, :] = jnp.zeros((8, LANES), jnp.float32)
        for r in range(0, nsel, 8):
            lead, rest = None, None
            for n in range(tiles_n):
                at = slice(n * LANES, (n + 1) * LANES)
                first, second = pooled[u % 2, 0, r:r + 8, at] * weights[u][n], pooled[u % 2, 1, r:r + 8, at] * weights[u][n]
                lead = first if lead is None else lead + first
                rest = second if rest is None else rest + second
            lined[u % 2, 0, 8 + r:16 + r, :] = lead
            lined[u % 2, 1, 8 + r:16 + r, :] = lead + 2.0 * rest
            if r % 16 == 8:
                yield
        turned = (lined[u % 2, 0, 8:8 + nsel, :] + lined[u % 2, 1, 7:7 + nsel, :]).T
        put(out_ref, g, slice(t * QTILE, (t + 1) * QTILE), turned[:QTILE] + turned[QTILE:])
        yield

    for step in range(len(units) + 2):
        stages = []
        if step < len(units):
            stages.append((4 * nsel // block, products(step)))
        if 0 <= step - 1 < len(units):
            stages.append((tiles_n * nsel // 32, exponentials(step - 1)))
        if step >= 2:
            stages.append((nsel // 16 + 1, sums(step - 2)))
        interleave(*stages)


def span_kernel(n_head, n_ctx, start_ref, first_ref, *refs):
    q_refs, k_refs, earlier, out_ref, keys, scores, pooled, lined = take_refs(n_head, n_ctx, refs)
    heads, tokens, depth = q_refs[0].shape
    nsel, g = keys.shape[1], len(earlier)
    scale = math.log2(math.e) / math.sqrt(depth)
    factor = nsel / (2.0 * n_head * heads)
    chunks = n_head * heads * QTILE // CHUNK
    per_chunk = n_head // chunks

    span = SPAN_ROWS
    spans = nsel // span

    def over_spans(body, carry):
        return lax.fori_loop(0, spans, lambda n, c: body(pl.multiple_of(n * span, span), c), carry)

    gather_keys(n_ctx, k_refs, keys)
    for n, ref in enumerate(earlier):
        put(out_ref, n, slice(None), ref[...])

    def tile(index, _):
        begin = pl.multiple_of(index * QTILE, QTILE)
        first = first_ref[index]
        row4, reach = limits(n_ctx, tokens, begin, start_ref)

        weights = []
        for c in range(chunks):
            columns = tile_columns(q_refs[c * per_chunk:(c + 1) * per_chunk], begin)

            def scores_span(base, tops):
                tops = list(tops)
                rows = jnp.concatenate([keys[s, pl.ds(base, span), :] for s in range(4)], axis=0)
                piece = lax.dot_general(rows, columns, NT, preferred_element_type=jnp.float32)
                for s in range(4):
                    for r in range(0, span, 8):
                        mask = visible(nsel, n_ctx * tokens, r, s, first, row4, reach, base)
                        for n in range(CHUNK // LANES):
                            part = piece[s * span + r:s * span + r + 8, n * LANES:(n + 1) * LANES]
                            if mask is not None:
                                part = jnp.where(mask, part, MASKED)
                            scores[0, s, pl.ds(base + r, 8), n * LANES:(n + 1) * LANES] = part
                            tops[n] = jnp.maximum(tops[n], part)
                return tuple(tops)

            tops = over_spans(scores_span, (jnp.full((8, LANES), MASKED, jnp.float32),) * (CHUNK // LANES))
            for n in range(CHUNK // LANES):
                at = (c * CHUNK // LANES + n) * LANES

                def exps_span(base, total):
                    for r in range(0, span, 8):
                        here = pl.ds(base + r, 8)
                        parts = [
                            jnp.exp2((scores[0, s, here, n * LANES:(n + 1) * LANES] - tops[n]) * scale)
                            for s in range(4)
                        ]
                        rest = parts[1] + parts[2] + parts[3]
                        pooled[0, 0, here, at:at + LANES] = parts[0]
                        pooled[0, 1, here, at:at + LANES] = rest
                        total = total + (parts[0] + rest)
                    return total

                total = over_spans(exps_span, jnp.zeros((8, LANES), jnp.float32))
                top = jnp.max(tops[n], axis=0, keepdims=True)
                lowered = jnp.exp2((tops[n] - top) * scale)
                weights.append(lowered * (factor / jnp.sum(total * lowered, axis=0, keepdims=True)))

        def sums_span(base, _):
            for r in range(0, span, 8):
                lead, rest = [
                    sum(
                        (pooled[0, p, pl.ds(base + r, 8), n * LANES:(n + 1) * LANES] * weights[n] for n in range(1, len(weights))),
                        pooled[0, p, pl.ds(base + r, 8), 0:LANES] * weights[0],
                    )
                    for p in range(2)
                ]
                lined[0, 0, pl.ds(base + 8 + r, 8), :] = lead
                lined[0, 1, pl.ds(base + 8 + r, 8), :] = lead + 2.0 * rest
            return 0

        lined[0, 1, 0:8, :] = jnp.zeros((8, LANES), jnp.float32)
        over_spans(sums_span, 0)
        blocks = lined[0, 0, 8:8 + nsel, :] + lined[0, 1, 7:7 + nsel, :]
        turned = blocks.T
        put(out_ref, g, pl.ds(begin, QTILE), turned[:QTILE] + turned[QTILE:])
        return 0

    lax.fori_loop(0, tokens // QTILE, tile, 0)


def in_hbm(array):
    return pltpu.with_memory_space_constraint(array, pltpu.HBM)


def per_device(n_head, n_ctx, queries, keys, span_start, tile_first):
    tokens, key_heads, heads, depth = queries.shape
    blocks = keys.shape[0]
    own = key_heads // n_head
    nsel = blocks * n_ctx
    vmem = pl.BlockSpec(memory_space=pltpu.VMEM)
    smem = pl.BlockSpec(memory_space=pltpu.SMEM)
    hbm = pl.BlockSpec(memory_space=pltpu.HBM)
    q_part = jax.ShapeDtypeStruct((heads, tokens, depth), queries.dtype)
    k_part = jax.ShapeDtypeStruct((4, blocks, depth), keys.dtype)
    packed = pl.pallas_call(
        partial(pack_kernel, n_head, key_heads, heads),
        out_shape=[q_part] * (n_head * own) + [k_part] * own,
        in_specs=[hbm, hbm],
        out_specs=[vmem] * ((n_head + 1) * own),
        scratch_shapes=[
            pltpu.VMEM((tokens * key_heads * heads, depth), queries.dtype),
            pltpu.VMEM((blocks * 4 * key_heads, depth), keys.dtype),
            pltpu.SemaphoreType.DMA((Q_COPIES,)),
            pltpu.SemaphoreType.DMA((K_COPIES,)),
        ],
        compiler_params=pltpu.CompilerParams(vmem_limit_bytes=16 * 2 ** 20),
        name="pack",
    )(in_hbm(queries.reshape(-1, depth)), in_hbm(keys.reshape(-1, depth)))

    def swap(array, axis, size, bit):
        return lax.ppermute(array, axis, [(i, i ^ bit) for i in range(size)])

    columns = n_head * heads * QTILE
    buffers = 2 if nsel <= SPAN_ROWS else 1
    done = []
    for g in range(own):
        q_parts = list(packed[g * n_head:(g + 1) * n_head])
        for d in range(1, n_head):
            q_parts[d] = swap(q_parts[d], "head", n_head, d)
        k_parts = {0: packed[n_head * own + g]}
        bit = n_ctx // 2
        while bit:
            for j in list(k_parts):
                k_parts[j | bit] = swap(k_parts[j], "ctx", n_ctx, bit)
            bit //= 2
        last = g == own - 1
        done.append(pl.pallas_call(
            partial(unit_kernel if buffers == 2 else span_kernel, n_head, n_ctx),
            out_shape=jax.ShapeDtypeStruct((tokens, own, nsel) if last else (tokens, nsel), jnp.float32),
            in_specs=[smem, smem] + [vmem] * (n_head + n_ctx + len(done)),
            out_specs=vmem,
            scratch_shapes=[
                pltpu.VMEM((4, nsel, depth), keys.dtype),
                pltpu.VMEM((buffers, 4, nsel, columns), jnp.float32),
                pltpu.VMEM((buffers, 2, nsel, columns), jnp.float32),
                pltpu.VMEM((buffers, 2, 8 + nsel, LANES), jnp.float32),
            ],
            compiler_params=pltpu.CompilerParams(vmem_limit_bytes=(20 if buffers == 2 else 52) * 2 ** 20),
            cost_estimate=pl.CostEstimate(
                flops=2 * columns * tokens // QTILE * 4 * nsel * depth,
                bytes_accessed=4 * tokens * nsel,
                transcendentals=columns * tokens // QTILE * 4 * nsel,
            ),
            name="importance",
        )(span_start, tile_first, *q_parts, *[k_parts[j] for j in range(n_ctx)], *done))
    return done[-1]


def solution(mesh):
    placed = (
        P(("groups", "ctx"), None, "head", None),
        P(("groups", "ctx"), None, None, None),
        P("groups"),
        P(("groups", "ctx")),
    )
    return jax.shard_map(
        partial(per_device, mesh.shape["head"], mesh.shape["ctx"]),
        mesh=mesh,
        in_specs=placed,
        out_specs=P(("groups", "ctx"), "head", None),
        check_vma=False,
    )
```

```python
import math
from functools import partial

import jax
import jax.numpy as jnp
from jax import lax
from jax.experimental import pallas as pl
from jax.experimental.pallas import tpu as pltpu
from jax.sharding import PartitionSpec as P

QTILE = 64
PACK = 16
K_COPIES = 2
Q_COPIES = 3
LANES = 128
CHUNK = 512
SPAN_ROWS = 256
BLOCK = 64
SAFE = 64.0
MASKED = -1e30
NT = (((1,), (1,)), ((), ()))


def pack_kernel(n_head, key_heads, heads, q_hbm, k_hbm, *refs):
    q_outs, (k_out, q_ref, k_ref, q_sems, k_sems) = refs[:n_head], refs[n_head:]
    me = lax.axis_index("head")
    own = key_heads // n_head
    width = own * heads
    tokens = q_outs[0].shape[2]
    blocks = k_out.shape[2]
    q_rows = PACK * key_heads * heads
    k_rows = PACK * 4 * key_heads
    k_copies, q_copies = [], []
    k_each, q_each = blocks // PACK // K_COPIES, tokens // PACK // Q_COPIES
    for n in range(K_COPIES):
        at = pl.ds(n * k_each * k_rows, k_each * k_rows)
        k_copies.append(pltpu.make_async_copy(k_hbm.at[at], k_ref.at[at], k_sems.at[n]))
    for n in range(Q_COPIES):
        at = pl.ds(n * q_each * q_rows, q_each * q_rows)
        q_copies.append(pltpu.make_async_copy(q_hbm.at[at], q_ref.at[at], q_sems.at[n]))
    for copy in k_copies + q_copies:
        copy.start()

    out_row = lax.broadcasted_iota(jnp.int32, (own * 4 * PACK, k_rows), 0)
    in_row = lax.broadcasted_iota(jnp.int32, (own * 4 * PACK, k_rows), 1)
    head = out_row // (4 * PACK)
    part = out_row // PACK % 4
    source = out_row % PACK * (4 * key_heads) + part * key_heads + me * own + head
    select = jnp.where(in_row == source, 1.0, 0.0).astype(jnp.bfloat16)
    for block in range(blocks // PACK):
        if block % k_each == 0:
            k_copies[block // k_each].wait()
        moved = jnp.dot(
            select, k_ref[block * k_rows:(block + 1) * k_rows, :], preferred_element_type=jnp.float32
        ).astype(jnp.bfloat16)
        for u in range(own * 4):
            k_out[u // 4, u % 4, block * PACK:(block + 1) * PACK, :] = moved[u * PACK:(u + 1) * PACK]

    out_row = lax.broadcasted_iota(jnp.int32, (n_head * width * PACK, q_rows), 0)
    in_row = lax.broadcasted_iota(jnp.int32, (n_head * width * PACK, q_rows), 1)
    step = out_row // (width * PACK)
    unit = out_row // PACK % width
    source = out_row % PACK * (key_heads * heads) + (step ^ me) * width + unit
    select = jnp.where(in_row == source, 1.0, 0.0).astype(jnp.bfloat16)
    for block in range(tokens // PACK):
        if block % q_each == 0:
            q_copies[block // q_each].wait()
        moved = jnp.dot(
            select, q_ref[block * q_rows:(block + 1) * q_rows, :], preferred_element_type=jnp.float32
        ).astype(jnp.bfloat16)
        for u in range(n_head * width):
            d, g, h = u // width, u % width // heads, u % heads
            q_outs[d][g, h, block * PACK:(block + 1) * PACK, :] = moved[u * PACK:(u + 1) * PACK]


def gather_keys(n_ctx, k_refs, keys):
    me = lax.axis_index("ctx")
    local = k_refs[0].shape[2]
    for j in range(n_ctx):
        at = pl.ds(pl.multiple_of((me ^ j) * local, local), local)
        keys[:, :, at, :] = k_refs[j][...]


def limits(n_ctx, tokens, begin, start_ref):
    lane = lax.broadcasted_iota(jnp.int32, (8, LANES), 1)
    row = lax.broadcasted_iota(jnp.int32, (8, LANES), 0)
    place = start_ref[0] + lax.axis_index("ctx") * tokens + begin + lane % QTILE
    return 4 * row, place - 31 - 64 * row


def visible(nsel, span_tokens, r, s, first, row4, reach, base=None):
    least_position = 16 * 4 * nsel * 7 // 8 - span_tokens
    most_first = nsel - 1
    at = r if base is None else base + r
    mask = None
    if base is not None or 4 * r + s <= most_first:
        mask = row4 >= first - (4 * at + s)
    if base is not None or 16 * (4 * (r + 7) + s) + 31 > least_position:
        below = reach >= 64 * at + 16 * s
        mask = below if mask is None else mask & below
    return mask


def tile_columns(q_refs, g, begin):
    return jnp.concatenate(
        [q[g, h, pl.ds(begin, QTILE), :] for q in q_refs for h in range(q.shape[1])], axis=0
    )


def interleave(*stages):
    lengths = [length for length, _ in stages]
    done = [0] * len(stages)
    for tick in range(1, max(lengths) + 1):
        for n, (length, stage) in enumerate(stages):
            while done[n] * max(lengths) < tick * length:
                next(stage, None)
                done[n] += 1
    for _, stage in stages:
        for _ in stage:
            pass


def unit_kernel(n_head, n_ctx, start_ref, first_ref, *refs):
    q_refs, k_refs = refs[:n_head], refs[n_head:n_head + n_ctx]
    out_ref, keys, scores, pooled, lined = refs[n_head + n_ctx:]
    own, heads, tokens, depth = q_refs[0].shape
    nsel = keys.shape[2]
    scale = math.log2(math.e) / math.sqrt(depth)
    factor = nsel / (2.0 * n_head * heads)
    tiles_n = n_head * heads * QTILE // LANES
    gather_keys(n_ctx, k_refs, keys)
    units = [(t, g) for t in range(tokens // QTILE) for g in range(own)]
    weights, tops = {}, []

    def exponentials(u):
        t, g = units[u]
        columns = tile_columns(q_refs, g, t * QTILE)
        row4, reach = limits(n_ctx, tokens, t * QTILE, start_ref)
        first = first_ref[t]
        top, total = [None] * tiles_n, [None] * tiles_n
        for base in range(0, nsel, BLOCK):
            rows = jnp.concatenate([keys[g, s, base:base + BLOCK, :] for s in range(4)], axis=0)
            piece = lax.dot_general(rows, columns, NT, preferred_element_type=jnp.float32)
            for r in range(0, BLOCK, 8):
                masks = [visible(nsel, n_ctx * tokens, base + r, s, first, row4, reach) for s in range(4)]
                for n in range(tiles_n):
                    at = slice(n * LANES, (n + 1) * LANES)
                    parts = []
                    for s, mask in enumerate(masks):
                        part = piece[s * BLOCK + r:s * BLOCK + r + 8, at]
                        if mask is not None:
                            part = jnp.where(mask, part, MASKED)
                        top[n] = part if top[n] is None else jnp.maximum(top[n], part)
                        parts.append(jnp.exp2(part * scale))
                    rest = parts[1] + parts[2] + parts[3]
                    pooled[u % 2, 0, base + r:base + r + 8, at] = parts[0]
                    pooled[u % 2, 1, base + r:base + r + 8, at] = rest
                    both = parts[0] + rest
                    total[n] = both if total[n] is None else total[n] + both
                yield
        weights[u] = [factor / jnp.sum(part, axis=0, keepdims=True) for part in total]
        for part in top:
            tops.append(jnp.abs(jnp.max(part, axis=0, keepdims=True)))

    def sums(u):
        t, g = units[u]
        lined[u % 2, 1, 0:8, :] = jnp.zeros((8, LANES), jnp.float32)
        for r in range(0, nsel, 8):
            lead, rest = None, None
            for n in range(tiles_n):
                at = slice(n * LANES, (n + 1) * LANES)
                first, second = pooled[u % 2, 0, r:r + 8, at] * weights[u][n], pooled[u % 2, 1, r:r + 8, at] * weights[u][n]
                lead = first if lead is None else lead + first
                rest = second if rest is None else rest + second
            lined[u % 2, 0, 8 + r:16 + r, :] = lead
            lined[u % 2, 1, 8 + r:16 + r, :] = lead + 2.0 * rest
            yield
        turned = (lined[u % 2, 0, 8:8 + nsel, :] + lined[u % 2, 1, 7:7 + nsel, :]).T
        out_ref[t * QTILE:(t + 1) * QTILE, g, :] = turned[:QTILE] + turned[QTILE:]
        yield

    for step in range(len(units) + 1):
        stages = []
        if step < len(units):
            stages.append((nsel // 8, exponentials(step)))
        if step >= 1:
            stages.append((nsel // 8 + 1, sums(step - 1)))
        interleave(*stages)

    worst = tops[0]
    for part in tops[1:]:
        worst = jnp.maximum(worst, part)

    @pl.when(jnp.max(worst) * scale > SAFE)
    def _():
        shifted(n_head, n_ctx, start_ref, first_ref, *refs)


def span_kernel(n_head, n_ctx, start_ref, first_ref, *refs):
    gather_keys(n_ctx, refs[n_head:n_head + n_ctx], refs[n_head + n_ctx + 1])
    shifted(n_head, n_ctx, start_ref, first_ref, *refs)


def shifted(n_head, n_ctx, start_ref, first_ref, *refs):
    q_refs, k_refs = refs[:n_head], refs[n_head:n_head + n_ctx]
    out_ref, keys, scores, pooled, lined = refs[n_head + n_ctx:]
    own, heads, tokens, depth = q_refs[0].shape
    nsel = keys.shape[2]
    scale = math.log2(math.e) / math.sqrt(depth)
    factor = nsel / (2.0 * n_head * heads)
    chunks = n_head * heads * QTILE // CHUNK
    per_chunk = n_head // chunks

    span = SPAN_ROWS
    spans = nsel // span

    def over_spans(body, carry):
        return lax.fori_loop(0, spans, lambda n, c: body(pl.multiple_of(n * span, span), c), carry)

    def tile(index, _):
        begin = pl.multiple_of(index * QTILE, QTILE)
        first = first_ref[index]
        row4, reach = limits(n_ctx, tokens, begin, start_ref)

        for g in range(own):
            weights = []
            for c in range(chunks):
                columns = tile_columns(q_refs[c * per_chunk:(c + 1) * per_chunk], g, begin)

                def scores_span(base, tops):
                    tops = list(tops)
                    rows = jnp.concatenate([keys[g, s, pl.ds(base, span), :] for s in range(4)], axis=0)
                    piece = lax.dot_general(rows, columns, NT, preferred_element_type=jnp.float32)
                    for s in range(4):
                        for r in range(0, span, 8):
                            mask = visible(nsel, n_ctx * tokens, r, s, first, row4, reach, base)
                            for n in range(CHUNK // LANES):
                                part = piece[s * span + r:s * span + r + 8, n * LANES:(n + 1) * LANES]
                                if mask is not None:
                                    part = jnp.where(mask, part, MASKED)
                                scores[0, s, pl.ds(base + r, 8), n * LANES:(n + 1) * LANES] = part
                                tops[n] = jnp.maximum(tops[n], part)
                    return tuple(tops)

                tops = over_spans(scores_span, (jnp.full((8, LANES), MASKED, jnp.float32),) * (CHUNK // LANES))
                for n in range(CHUNK // LANES):
                    at = (c * CHUNK // LANES + n) * LANES

                    def exps_span(base, total):
                        for r in range(0, span, 8):
                            here = pl.ds(base + r, 8)
                            parts = [
                                jnp.exp2((scores[0, s, here, n * LANES:(n + 1) * LANES] - tops[n]) * scale)
                                for s in range(4)
                            ]
                            rest = parts[1] + parts[2] + parts[3]
                            pooled[0, 0, here, at:at + LANES] = parts[0]
                            pooled[0, 1, here, at:at + LANES] = rest
                            total = total + (parts[0] + rest)
                        return total

                    total = over_spans(exps_span, jnp.zeros((8, LANES), jnp.float32))
                    top = jnp.max(tops[n], axis=0, keepdims=True)
                    lowered = jnp.exp2((tops[n] - top) * scale)
                    weights.append(lowered * (factor / jnp.sum(total * lowered, axis=0, keepdims=True)))

            def sums_span(base, _):
                for r in range(0, span, 8):
                    lead, rest = [
                        sum(
                            (pooled[0, p, pl.ds(base + r, 8), n * LANES:(n + 1) * LANES] * weights[n] for n in range(1, len(weights))),
                            pooled[0, p, pl.ds(base + r, 8), 0:LANES] * weights[0],
                        )
                        for p in range(2)
                    ]
                    lined[0, 0, pl.ds(base + 8 + r, 8), :] = lead
                    lined[0, 1, pl.ds(base + 8 + r, 8), :] = lead + 2.0 * rest
                return 0

            lined[0, 1, 0:8, :] = jnp.zeros((8, LANES), jnp.float32)
            over_spans(sums_span, 0)
            blocks = lined[0, 0, 8:8 + nsel, :] + lined[0, 1, 7:7 + nsel, :]
            turned = blocks.T
            out_ref[pl.ds(begin, QTILE), g, :] = turned[:QTILE] + turned[QTILE:]
        return 0

    lax.fori_loop(0, tokens // QTILE, tile, 0)


def in_hbm(array):
    return pltpu.with_memory_space_constraint(array, pltpu.HBM)


def per_device(n_head, n_ctx, queries, keys, span_start, tile_first):
    tokens, key_heads, heads, depth = queries.shape
    blocks = keys.shape[0]
    own = key_heads // n_head
    nsel = blocks * n_ctx
    vmem = pl.BlockSpec(memory_space=pltpu.VMEM)
    smem = pl.BlockSpec(memory_space=pltpu.SMEM)
    hbm = pl.BlockSpec(memory_space=pltpu.HBM)
    q_part = jax.ShapeDtypeStruct((own, heads, tokens, depth), queries.dtype)
    k_part = jax.ShapeDtypeStruct((own, 4, blocks, depth), keys.dtype)
    packed = pl.pallas_call(
        partial(pack_kernel, n_head, key_heads, heads),
        out_shape=[q_part] * n_head + [k_part],
        in_specs=[hbm, hbm],
        out_specs=[vmem] * (n_head + 1),
        scratch_shapes=[
            pltpu.VMEM((tokens * key_heads * heads, depth), queries.dtype),
            pltpu.VMEM((blocks * 4 * key_heads, depth), keys.dtype),
            pltpu.SemaphoreType.DMA((Q_COPIES,)),
            pltpu.SemaphoreType.DMA((K_COPIES,)),
        ],
        compiler_params=pltpu.CompilerParams(vmem_limit_bytes=16 * 2 ** 20),
        name="pack",
    )(in_hbm(queries.reshape(-1, depth)), in_hbm(keys.reshape(-1, depth)))
    q_parts, k_parts = list(packed[:n_head]), [packed[n_head]]

    def swap(array, axis, size, bit):
        return lax.ppermute(array, axis, [(i, i ^ bit) for i in range(size)])

    for d in range(1, n_head):
        q_parts[d] = swap(q_parts[d], "head", n_head, d)
    bit = n_ctx // 2
    k_parts = {0: packed[n_head]}
    while bit:
        for j in list(k_parts):
            k_parts[j | bit] = swap(k_parts[j], "ctx", n_ctx, bit)
        bit //= 2
    k_parts = [k_parts[j] for j in range(n_ctx)]
    columns = n_head * heads * QTILE
    buffers = 2 if nsel <= SPAN_ROWS else 1
    return pl.pallas_call(
        partial(unit_kernel if buffers == 2 else span_kernel, n_head, n_ctx),
        out_shape=jax.ShapeDtypeStruct((tokens, own, nsel), jnp.float32),
        in_specs=[smem, smem] + [vmem] * (n_head + n_ctx),
        out_specs=vmem,
        scratch_shapes=[
            pltpu.VMEM((own, 4, nsel, depth), keys.dtype),
            pltpu.VMEM((1, 4, nsel, columns), jnp.float32),
            pltpu.VMEM((buffers, 2, nsel, columns), jnp.float32),
            pltpu.VMEM((buffers, 2, 8 + nsel, LANES), jnp.float32),
        ],
        compiler_params=pltpu.CompilerParams(vmem_limit_bytes=(20 if buffers == 2 else 52) * 2 ** 20),
        name="importance",
    )(span_start, tile_first, *q_parts, *k_parts)


def solution(mesh):
    placed = (
        P(("groups", "ctx"), None, "head", None),
        P(("groups", "ctx"), None, None, None),
        P("groups"),
        P(("groups", "ctx")),
    )
    return jax.shard_map(
        partial(per_device, mesh.shape["head"], mesh.shape["ctx"]),
        mesh=mesh,
        in_specs=placed,
        out_specs=P(("groups", "ctx"), "head", None),
        check_vma=False,
    )
```

```python
import math
from functools import partial

import jax
import jax.numpy as jnp
from jax import lax
from jax.experimental import pallas as pl
from jax.experimental.pallas import tpu as pltpu
from jax.sharding import PartitionSpec as P

QTILE = 64
PACK = 16
K_COPIES = 2
Q_COPIES = 3
LANES = 128
CHUNK = 512
SPAN_ROWS = 256
BLOCK = 64
SAFE = 2.0 ** 64
MASKED = -1e30
NT = (((1,), (1,)), ((), ()))


def pack_kernel(n_head, key_heads, heads, q_hbm, k_hbm, *refs):
    q_outs, (k_out, q_ref, k_ref, q_sems, k_sems) = refs[:n_head], refs[n_head:]
    me = lax.axis_index("head")
    own = key_heads // n_head
    width = own * heads
    tokens = q_outs[0].shape[2]
    blocks = k_out.shape[2]
    q_rows = PACK * key_heads * heads
    k_rows = PACK * 4 * key_heads
    k_copies, q_copies = [], []
    k_each, q_each = blocks // PACK // K_COPIES, tokens // PACK // Q_COPIES
    for n in range(K_COPIES):
        at = pl.ds(n * k_each * k_rows, k_each * k_rows)
        k_copies.append(pltpu.make_async_copy(k_hbm.at[at], k_ref.at[at], k_sems.at[n]))
    for n in range(Q_COPIES):
        at = pl.ds(n * q_each * q_rows, q_each * q_rows)
        q_copies.append(pltpu.make_async_copy(q_hbm.at[at], q_ref.at[at], q_sems.at[n]))
    for copy in k_copies + q_copies:
        copy.start()

    out_row = lax.broadcasted_iota(jnp.int32, (own * 4 * PACK, k_rows), 0)
    in_row = lax.broadcasted_iota(jnp.int32, (own * 4 * PACK, k_rows), 1)
    head = out_row // (4 * PACK)
    part = out_row // PACK % 4
    source = out_row % PACK * (4 * key_heads) + part * key_heads + me * own + head
    select = jnp.where(in_row == source, 1.0, 0.0).astype(jnp.bfloat16)
    for block in range(blocks // PACK):
        if block % k_each == 0:
            k_copies[block // k_each].wait()
        moved = jnp.dot(
            select, k_ref[block * k_rows:(block + 1) * k_rows, :], preferred_element_type=jnp.float32
        ).astype(jnp.bfloat16)
        for u in range(own * 4):
            k_out[u // 4, u % 4, block * PACK:(block + 1) * PACK, :] = moved[u * PACK:(u + 1) * PACK]

    out_row = lax.broadcasted_iota(jnp.int32, (n_head * width * PACK, q_rows), 0)
    in_row = lax.broadcasted_iota(jnp.int32, (n_head * width * PACK, q_rows), 1)
    step = out_row // (width * PACK)
    unit = out_row // PACK % width
    source = out_row % PACK * (key_heads * heads) + (step ^ me) * width + unit
    select = jnp.where(in_row == source, 1.0, 0.0).astype(jnp.bfloat16)
    for block in range(tokens // PACK):
        if block % q_each == 0:
            q_copies[block // q_each].wait()
        moved = jnp.dot(
            select, q_ref[block * q_rows:(block + 1) * q_rows, :], preferred_element_type=jnp.float32
        ).astype(jnp.bfloat16)
        for u in range(n_head * width):
            d, g, h = u // width, u % width // heads, u % heads
            q_outs[d][g, h, block * PACK:(block + 1) * PACK, :] = moved[u * PACK:(u + 1) * PACK]


def gather_keys(n_ctx, k_refs, keys):
    me = lax.axis_index("ctx")
    local = k_refs[0].shape[2]
    for j in range(n_ctx):
        at = pl.ds(pl.multiple_of((me ^ j) * local, local), local)
        keys[:, :, at, :] = k_refs[j][...]


def limits(n_ctx, tokens, begin, start_ref):
    lane = lax.broadcasted_iota(jnp.int32, (8, LANES), 1)
    row = lax.broadcasted_iota(jnp.int32, (8, LANES), 0)
    place = start_ref[0] + lax.axis_index("ctx") * tokens + begin + lane % QTILE
    return 4 * row, place - 31 - 64 * row


def visible(nsel, span_tokens, r, s, first, row4, reach, base=None):
    least_position = 16 * 4 * nsel * 7 // 8 - span_tokens
    most_first = nsel - 1
    at = r if base is None else base + r
    mask = None
    if base is not None or 4 * r + s <= most_first:
        mask = row4 >= first - (4 * at + s)
    if base is not None or 16 * (4 * (r + 7) + s) + 31 > least_position:
        below = reach >= 64 * at + 16 * s
        mask = below if mask is None else mask & below
    return mask


def tile_columns(q_refs, g, begin):
    return jnp.concatenate(
        [q[g, h, pl.ds(begin, QTILE), :] for q in q_refs for h in range(q.shape[1])], axis=0
    )


def interleave(*stages):
    lengths = [length for length, _ in stages]
    done = [0] * len(stages)
    for tick in range(1, max(lengths) + 1):
        for n, (length, stage) in enumerate(stages):
            while done[n] * max(lengths) < tick * length:
                next(stage, None)
                done[n] += 1
    for _, stage in stages:
        for _ in stage:
            pass


def unit_kernel(n_head, n_ctx, start_ref, first_ref, *refs):
    q_refs, k_refs = refs[:n_head], refs[n_head:n_head + n_ctx]
    out_hbm, keys, scores, pooled, lined, out_ref, sems = refs[n_head + n_ctx:]
    own, heads, tokens, depth = q_refs[0].shape
    nsel = keys.shape[2]
    scale = math.log2(math.e) / math.sqrt(depth)
    factor = nsel / (2.0 * n_head * heads)
    tiles_n = n_head * heads * QTILE // LANES
    gather_keys(n_ctx, k_refs, keys)
    units = [(t, g) for t in range(tokens // QTILE) for g in range(own)]
    weights, totals = {}, []
    sent = [
        pltpu.make_async_copy(out_ref.at[pl.ds(t * QTILE, QTILE)], out_hbm.at[pl.ds(t * QTILE, QTILE)], sems.at[t])
        for t in range(tokens // QTILE)
    ]

    def exponentials(u):
        t, g = units[u]
        columns = tile_columns(q_refs, g, t * QTILE)
        row4, reach = limits(n_ctx, tokens, t * QTILE, start_ref)
        first = first_ref[t]
        total = [None] * tiles_n
        for base in range(0, nsel, BLOCK):
            rows = jnp.concatenate([keys[g, s, base:base + BLOCK, :] for s in range(4)], axis=0)
            piece = lax.dot_general(rows, columns, NT, preferred_element_type=jnp.float32)
            for r in range(0, BLOCK, 8):
                masks = [visible(nsel, n_ctx * tokens, base + r, s, first, row4, reach) for s in range(4)]
                for n in range(tiles_n):
                    at = slice(n * LANES, (n + 1) * LANES)
                    parts = []
                    for s, mask in enumerate(masks):
                        part = piece[s * BLOCK + r:s * BLOCK + r + 8, at]
                        if mask is not None:
                            part = jnp.where(mask, part, MASKED)
                        parts.append(jnp.exp2(part * scale))
                    rest = parts[1] + parts[2] + parts[3]
                    pooled[u % 2, 0, base + r:base + r + 8, at] = parts[0]
                    pooled[u % 2, 1, base + r:base + r + 8, at] = rest
                    both = parts[0] + rest
                    total[n] = both if total[n] is None else total[n] + both
                yield
        total = [jnp.sum(part, axis=0, keepdims=True) for part in total]
        weights[u] = [factor / part for part in total]
        totals.extend(total)

    def sums(u):
        t, g = units[u]
        lined[u % 2, 1, 0:8, :] = jnp.zeros((8, LANES), jnp.float32)
        for r in range(0, nsel, 8):
            lead, rest = None, None
            for n in range(tiles_n):
                at = slice(n * LANES, (n + 1) * LANES)
                first, second = pooled[u % 2, 0, r:r + 8, at] * weights[u][n], pooled[u % 2, 1, r:r + 8, at] * weights[u][n]
                lead = first if lead is None else lead + first
                rest = second if rest is None else rest + second
            lined[u % 2, 0, 8 + r:16 + r, :] = lead
            lined[u % 2, 1, 8 + r:16 + r, :] = lead + 2.0 * rest
            yield
        turned = (lined[u % 2, 0, 8:8 + nsel, :] + lined[u % 2, 1, 7:7 + nsel, :]).T
        out_ref[t * QTILE:(t + 1) * QTILE, g, :] = turned[:QTILE] + turned[QTILE:]
        if g == own - 1:
            sent[t].start()
        yield

    for step in range(len(units) + 1):
        stages = []
        if step < len(units):
            stages.append((nsel // 8, exponentials(step)))
        if step >= 1:
            stages.append((nsel // 8 + 1, sums(step - 1)))
        interleave(*stages)

    least, most = totals[0], totals[0]
    for part in totals[1:]:
        least, most = jnp.minimum(least, part), jnp.maximum(most, part)
    safe = (jnp.min(least) >= 1.0 / SAFE) & (jnp.max(most) <= SAFE)
    for copy in sent:
        copy.wait()

    @pl.when(jnp.logical_not(safe))
    def _():
        shifted(n_head, n_ctx, start_ref, first_ref, q_refs, out_ref, keys, scores, pooled, lined)
        for copy in sent:
            copy.start()
        for copy in sent:
            copy.wait()


def span_kernel(n_head, n_ctx, start_ref, first_ref, *refs):
    out_ref, keys, scores, pooled, lined = refs[n_head + n_ctx:]
    gather_keys(n_ctx, refs[n_head:n_head + n_ctx], keys)
    shifted(n_head, n_ctx, start_ref, first_ref, refs[:n_head], out_ref, keys, scores, pooled, lined)


def shifted(n_head, n_ctx, start_ref, first_ref, q_refs, out_ref, keys, scores, pooled, lined):
    own, heads, tokens, depth = q_refs[0].shape
    nsel = keys.shape[2]
    scale = math.log2(math.e) / math.sqrt(depth)
    factor = nsel / (2.0 * n_head * heads)
    chunks = n_head * heads * QTILE // CHUNK
    per_chunk = n_head // chunks

    span = SPAN_ROWS
    spans = nsel // span

    def over_spans(body, carry):
        return lax.fori_loop(0, spans, lambda n, c: body(pl.multiple_of(n * span, span), c), carry)

    def tile(index, _):
        begin = pl.multiple_of(index * QTILE, QTILE)
        first = first_ref[index]
        row4, reach = limits(n_ctx, tokens, begin, start_ref)

        for g in range(own):
            weights = []
            for c in range(chunks):
                columns = tile_columns(q_refs[c * per_chunk:(c + 1) * per_chunk], g, begin)

                def scores_span(base, tops):
                    tops = list(tops)
                    rows = jnp.concatenate([keys[g, s, pl.ds(base, span), :] for s in range(4)], axis=0)
                    piece = lax.dot_general(rows, columns, NT, preferred_element_type=jnp.float32)
                    for s in range(4):
                        for r in range(0, span, 8):
                            mask = visible(nsel, n_ctx * tokens, r, s, first, row4, reach, base)
                            for n in range(CHUNK // LANES):
                                part = piece[s * span + r:s * span + r + 8, n * LANES:(n + 1) * LANES]
                                if mask is not None:
                                    part = jnp.where(mask, part, MASKED)
                                scores[0, s, pl.ds(base + r, 8), n * LANES:(n + 1) * LANES] = part
                                tops[n] = jnp.maximum(tops[n], part)
                    return tuple(tops)

                tops = over_spans(scores_span, (jnp.full((8, LANES), MASKED, jnp.float32),) * (CHUNK // LANES))
                for n in range(CHUNK // LANES):
                    at = (c * CHUNK // LANES + n) * LANES

                    def exps_span(base, total):
                        for r in range(0, span, 8):
                            here = pl.ds(base + r, 8)
                            parts = [
                                jnp.exp2((scores[0, s, here, n * LANES:(n + 1) * LANES] - tops[n]) * scale)
                                for s in range(4)
                            ]
                            rest = parts[1] + parts[2] + parts[3]
                            pooled[0, 0, here, at:at + LANES] = parts[0]
                            pooled[0, 1, here, at:at + LANES] = rest
                            total = total + (parts[0] + rest)
                        return total

                    total = over_spans(exps_span, jnp.zeros((8, LANES), jnp.float32))
                    top = jnp.max(tops[n], axis=0, keepdims=True)
                    lowered = jnp.exp2((tops[n] - top) * scale)
                    weights.append(lowered * (factor / jnp.sum(total * lowered, axis=0, keepdims=True)))

            def sums_span(base, _):
                for r in range(0, span, 8):
                    lead, rest = [
                        sum(
                            (pooled[0, p, pl.ds(base + r, 8), n * LANES:(n + 1) * LANES] * weights[n] for n in range(1, len(weights))),
                            pooled[0, p, pl.ds(base + r, 8), 0:LANES] * weights[0],
                        )
                        for p in range(2)
                    ]
                    lined[0, 0, pl.ds(base + 8 + r, 8), :] = lead
                    lined[0, 1, pl.ds(base + 8 + r, 8), :] = lead + 2.0 * rest
                return 0

            lined[0, 1, 0:8, :] = jnp.zeros((8, LANES), jnp.float32)
            over_spans(sums_span, 0)
            blocks = lined[0, 0, 8:8 + nsel, :] + lined[0, 1, 7:7 + nsel, :]
            turned = blocks.T
            out_ref[pl.ds(begin, QTILE), g, :] = turned[:QTILE] + turned[QTILE:]
        return 0

    lax.fori_loop(0, tokens // QTILE, tile, 0)


def in_hbm(array):
    return pltpu.with_memory_space_constraint(array, pltpu.HBM)


def per_device(n_head, n_ctx, queries, keys, span_start, tile_first):
    tokens, key_heads, heads, depth = queries.shape
    blocks = keys.shape[0]
    own = key_heads // n_head
    nsel = blocks * n_ctx
    vmem = pl.BlockSpec(memory_space=pltpu.VMEM)
    smem = pl.BlockSpec(memory_space=pltpu.SMEM)
    hbm = pl.BlockSpec(memory_space=pltpu.HBM)
    q_part = jax.ShapeDtypeStruct((own, heads, tokens, depth), queries.dtype)
    k_part = jax.ShapeDtypeStruct((own, 4, blocks, depth), keys.dtype)
    packed = pl.pallas_call(
        partial(pack_kernel, n_head, key_heads, heads),
        out_shape=[q_part] * n_head + [k_part],
        in_specs=[hbm, hbm],
        out_specs=[vmem] * (n_head + 1),
        scratch_shapes=[
            pltpu.VMEM((tokens * key_heads * heads, depth), queries.dtype),
            pltpu.VMEM((blocks * 4 * key_heads, depth), keys.dtype),
            pltpu.SemaphoreType.DMA((Q_COPIES,)),
            pltpu.SemaphoreType.DMA((K_COPIES,)),
        ],
        compiler_params=pltpu.CompilerParams(vmem_limit_bytes=16 * 2 ** 20),
        name="pack",
    )(in_hbm(queries.reshape(-1, depth)), in_hbm(keys.reshape(-1, depth)))
    q_parts, k_parts = list(packed[:n_head]), [packed[n_head]]

    def swap(array, axis, size, bit):
        return lax.ppermute(array, axis, [(i, i ^ bit) for i in range(size)])

    for d in range(1, n_head):
        q_parts[d] = swap(q_parts[d], "head", n_head, d)
    bit = n_ctx // 2
    k_parts = {0: packed[n_head]}
    while bit:
        for j in list(k_parts):
            k_parts[j | bit] = swap(k_parts[j], "ctx", n_ctx, bit)
        bit //= 2
    k_parts = [k_parts[j] for j in range(n_ctx)]
    columns = n_head * heads * QTILE
    buffers = 2 if nsel <= SPAN_ROWS else 1
    staging = []
    if buffers == 2:
        staging = [pltpu.VMEM((tokens, own, nsel), jnp.float32), pltpu.SemaphoreType.DMA((tokens // QTILE,))]
    return pl.pallas_call(
        partial(unit_kernel if buffers == 2 else span_kernel, n_head, n_ctx),
        out_shape=jax.ShapeDtypeStruct((tokens, own, nsel), jnp.float32),
        in_specs=[smem, smem] + [vmem] * (n_head + n_ctx),
        out_specs=hbm if buffers == 2 else vmem,
        scratch_shapes=[
            pltpu.VMEM((own, 4, nsel, depth), keys.dtype),
            pltpu.VMEM((1, 4, nsel, columns), jnp.float32),
            pltpu.VMEM((buffers, 2, nsel, columns), jnp.float32),
            pltpu.VMEM((buffers, 2, 8 + nsel, LANES), jnp.float32),
        ] + staging,
        compiler_params=pltpu.CompilerParams(vmem_limit_bytes=(20 if buffers == 2 else 52) * 2 ** 20),
        name="importance",
    )(span_start, tile_first, *q_parts, *k_parts)


def solution(mesh):
    placed = (
        P(("groups", "ctx"), None, "head", None),
        P(("groups", "ctx"), None, None, None),
        P("groups"),
        P(("groups", "ctx")),
    )
    return jax.shard_map(
        partial(per_device, mesh.shape["head"], mesh.shape["ctx"]),
        mesh=mesh,
        in_specs=placed,
        out_specs=P(("groups", "ctx"), "head", None),
        check_vma=False,
    )
```

```python
import math
from functools import partial

import jax
import jax.numpy as jnp
from jax import lax
from jax.experimental import pallas as pl
from jax.experimental.pallas import tpu as pltpu
from jax.sharding import PartitionSpec as P

QTILE = 64
PACK = 16
K_COPIES = 2
Q_COPIES = 3
LANES = 128
CHUNK = 512
SPAN_ROWS = 256
BLOCK = 64
SAFE = 2.0 ** 64
MASKED = -1e30
NT = (((1,), (1,)), ((), ()))


def pack_kernel(n_head, key_heads, heads, q_hbm, k_hbm, *refs):
    q_outs, (k_out, q_ref, k_ref, q_sems, k_sems) = refs[:n_head], refs[n_head:]
    me = lax.axis_index("head")
    own = key_heads // n_head
    width = own * heads
    tokens = q_outs[0].shape[2]
    blocks = k_out.shape[2]
    q_rows = PACK * key_heads * heads
    k_rows = PACK * 4 * key_heads
    k_copies, q_copies = [], []
    k_each, q_each = blocks // PACK // K_COPIES, tokens // PACK // Q_COPIES
    for n in range(K_COPIES):
        at = pl.ds(n * k_each * k_rows, k_each * k_rows)
        k_copies.append(pltpu.make_async_copy(k_hbm.at[at], k_ref.at[at], k_sems.at[n]))
    for n in range(Q_COPIES):
        at = pl.ds(n * q_each * q_rows, q_each * q_rows)
        q_copies.append(pltpu.make_async_copy(q_hbm.at[at], q_ref.at[at], q_sems.at[n]))
    for copy in k_copies + q_copies:
        copy.start()

    out_row = lax.broadcasted_iota(jnp.int32, (own * 4 * PACK, k_rows), 0)
    in_row = lax.broadcasted_iota(jnp.int32, (own * 4 * PACK, k_rows), 1)
    head = out_row // (4 * PACK)
    part = out_row // PACK % 4
    source = out_row % PACK * (4 * key_heads) + part * key_heads + me * own + head
    select = jnp.where(in_row == source, 1.0, 0.0).astype(jnp.bfloat16)
    for block in range(blocks // PACK):
        if block % k_each == 0:
            k_copies[block // k_each].wait()
        moved = jnp.dot(
            select, k_ref[block * k_rows:(block + 1) * k_rows, :], preferred_element_type=jnp.float32
        ).astype(jnp.bfloat16)
        for u in range(own * 4):
            k_out[u // 4, u % 4, block * PACK:(block + 1) * PACK, :] = moved[u * PACK:(u + 1) * PACK]

    out_row = lax.broadcasted_iota(jnp.int32, (n_head * width * PACK, q_rows), 0)
    in_row = lax.broadcasted_iota(jnp.int32, (n_head * width * PACK, q_rows), 1)
    step = out_row // (width * PACK)
    unit = out_row // PACK % width
    source = out_row % PACK * (key_heads * heads) + (step ^ me) * width + unit
    select = jnp.where(in_row == source, 1.0, 0.0).astype(jnp.bfloat16)
    for block in range(tokens // PACK):
        if block % q_each == 0:
            q_copies[block // q_each].wait()
        moved = jnp.dot(
            select, q_ref[block * q_rows:(block + 1) * q_rows, :], preferred_element_type=jnp.float32
        ).astype(jnp.bfloat16)
        for u in range(n_head * width):
            d, g, h = u // width, u % width // heads, u % heads
            q_outs[d][g, h, block * PACK:(block + 1) * PACK, :] = moved[u * PACK:(u + 1) * PACK]


def gather_keys(n_ctx, k_refs, keys):
    me = lax.axis_index("ctx")
    local = k_refs[0].shape[2]
    for j in range(n_ctx):
        at = pl.ds(pl.multiple_of((me ^ j) * local, local), local)
        keys[:, :, at, :] = k_refs[j][...]


def limits(n_ctx, tokens, begin, start_ref):
    lane = lax.broadcasted_iota(jnp.int32, (8, LANES), 1)
    row = lax.broadcasted_iota(jnp.int32, (8, LANES), 0)
    place = start_ref[0] + lax.axis_index("ctx") * tokens + begin + lane % QTILE
    return 4 * row, place - 31 - 64 * row


def visible(nsel, span_tokens, r, s, first, row4, reach, base=None):
    least_position = 16 * 4 * nsel * 7 // 8 - span_tokens
    most_first = nsel - 1
    at = r if base is None else base + r
    mask = None
    if base is not None or 4 * r + s <= most_first:
        mask = row4 >= first - (4 * at + s)
    if base is not None or 16 * (4 * (r + 7) + s) + 31 > least_position:
        below = reach >= 64 * at + 16 * s
        mask = below if mask is None else mask & below
    return mask


def tile_columns(q_refs, g, begin):
    return jnp.concatenate(
        [q[g][h, pl.ds(begin, QTILE), :] for q in q_refs for h in range(q[g].shape[0])], axis=0
    )


def interleave(*stages):
    lengths = [length for length, _ in stages]
    done = [0] * len(stages)
    for tick in range(1, max(lengths) + 1):
        for n, (length, stage) in enumerate(stages):
            while done[n] * max(lengths) < tick * length:
                next(stage, None)
                done[n] += 1
    for _, stage in stages:
        for _ in stage:
            pass


def pooled_exponentials(q_refs, k_refs, t, spans, scale, masks_at, put, totals):
    own = len(q_refs[0])
    for sources, j in spans:
        pieces = []
        for g in range(own):
            rows = jnp.concatenate([k_refs[j][g, s] for s in range(4)], axis=0)
            columns = tile_columns([q_refs[n] for n in sources], g, t * QTILE)
            pieces.append(lax.dot_general(rows, columns, NT, preferred_element_type=jnp.float32))
        for r in range(0, BLOCK, 8):
            masks = masks_at(t, j, r)
            for g in range(own):
                for at, n in enumerate(sources):
                    parts = []
                    for s in range(4):
                        part = pieces[g][s * BLOCK + r:s * BLOCK + r + 8, at * LANES:(at + 1) * LANES]
                        parts.append(jnp.exp2(jnp.where(masks[s], part, MASKED) * scale))
                    rest = parts[1] + parts[2] + parts[3]
                    put(g, n, j, r, parts[0], rest)
                    both = parts[0] + rest
                    totals[g, n] = totals[g, n] + both if (g, n) in totals else both
            yield


def mask_maker(n_ctx, tokens, start_ref, first_ref):
    me = lax.axis_index("ctx")

    def masks_at(t, j, r):
        row4, reach = limits(n_ctx, tokens, t * QTILE, start_ref)
        first = first_ref[t]
        at = (me ^ j) * BLOCK + r
        return [(row4 >= first - (4 * at + s)) & (reach >= 64 * at + 16 * s) for s in range(4)]

    return masks_at


def early_kernel(n_ctx, start_ref, first_ref, *refs):
    q_refs, k_refs, (pooled, total_ref) = refs[:3], refs[3:6], refs[6:]
    own, heads, tokens, depth = q_refs[0].shape
    q_refs = [[ref.at[g] for g in range(own)] for ref in q_refs]
    scale = math.log2(math.e) / math.sqrt(depth)
    masks_at = mask_maker(n_ctx, tokens, start_ref, first_ref)
    for t in range(tokens // QTILE):
        def put(g, n, j, r, lead, rest):
            pooled[t, g, 0, j * BLOCK + r:j * BLOCK + r + 8, n * LANES:(n + 1) * LANES] = lead
            pooled[t, g, 1, j * BLOCK + r:j * BLOCK + r + 8, n * LANES:(n + 1) * LANES] = rest

        totals = {}
        for _ in pooled_exponentials(q_refs, k_refs, t, [((0, 1, 2), j) for j in range(3)], scale, masks_at, put, totals):
            pass
        for (g, n), total in totals.items():
            total_ref[t, g, :, n * LANES:(n + 1) * LANES] = total


def late_kernel(n_head, n_ctx, start_ref, first_ref, *refs):
    raw_q, k_refs, (early, early_total) = refs[:n_head], refs[n_head:n_head + n_ctx], refs[n_head + n_ctx:-9]
    out_hbm, keys, scores, pooled, lined, far, corner, out_ref, sems = refs[-9:]
    own, heads, tokens, depth = raw_q[0].shape
    q_refs = [[ref.at[g] for g in range(own)] for ref in raw_q]
    nsel = keys.shape[2]
    scale = math.log2(math.e) / math.sqrt(depth)
    factor = nsel / (2.0 * n_head * heads)
    me = lax.axis_index("ctx")
    masks_at = mask_maker(n_ctx, tokens, start_ref, first_ref)
    tiles = tokens // QTILE
    last = n_ctx - 1
    weights, totals = {}, []
    sent = [
        pltpu.make_async_copy(out_ref.at[pl.ds(t * QTILE, QTILE)], out_hbm.at[pl.ds(t * QTILE, QTILE)], sems.at[t])
        for t in range(tiles)
    ]

    def exponentials(t):
        def put(g, n, j, r, lead, rest):
            if n == last:
                far[t % 2, g, 0, j * BLOCK + r:j * BLOCK + r + 8, :] = lead
                far[t % 2, g, 1, j * BLOCK + r:j * BLOCK + r + 8, :] = rest
            else:
                corner[t % 2, g, 0, r:r + 8, n * LANES:(n + 1) * LANES] = lead
                corner[t % 2, g, 1, r:r + 8, n * LANES:(n + 1) * LANES] = rest

        sums = {}
        spans = [((last,), j) for j in range(last)] + [(tuple(range(n_head)), last)]
        yield from pooled_exponentials(q_refs, k_refs, t, spans, scale, masks_at, put, sums)
        for (g, n), total in sums.items():
            if n < last:
                total = total + early_total[t, g, :, n * LANES:(n + 1) * LANES]
            total = jnp.sum(total, axis=0, keepdims=True)
            weights[t, g, n] = factor / total
            totals.append(total)

    def sums(t):
        for g in range(own):
            lined[t % 2, g, 1, 0:8, :] = jnp.zeros((8, LANES), jnp.float32)
            for j in range(n_ctx):
                for r in range(0, BLOCK, 8):
                    both = []
                    for p in range(2):
                        value = far[t % 2, g, p, j * BLOCK + r:j * BLOCK + r + 8, :] * weights[t, g, last]
                        for n in range(last):
                            at = slice(n * LANES, (n + 1) * LANES)
                            if j == last:
                                part = corner[t % 2, g, p, r:r + 8, at]
                            else:
                                part = early[t, g, p, j * BLOCK + r:j * BLOCK + r + 8, at]
                            value = value + part * weights[t, g, n]
                        both.append(value)
                    here = pl.ds(pl.multiple_of(8 + (me ^ j) * BLOCK + r, 8), 8)
                    lined[t % 2, g, 0, here, :] = both[0]
                    lined[t % 2, g, 1, here, :] = both[0] + 2.0 * both[1]
                    yield
            turned = (lined[t % 2, g, 0, 8:8 + nsel, :] + lined[t % 2, g, 1, 7:7 + nsel, :]).T
            out_ref[t * QTILE:(t + 1) * QTILE, g, :] = turned[:QTILE] + turned[QTILE:]
            yield
        sent[t].start()

    for step in range(tiles + 1):
        stages = []
        if step < tiles:
            stages.append((nsel // 8, exponentials(step)))
        if step >= 1:
            stages.append((own * (nsel // 8 + 1), sums(step - 1)))
        interleave(*stages)

    least, most = totals[0], totals[0]
    for part in totals[1:]:
        least, most = jnp.minimum(least, part), jnp.maximum(most, part)
    safe = (jnp.min(least) >= 1.0 / SAFE) & (jnp.max(most) <= SAFE)
    for copy in sent:
        copy.wait()

    @pl.when(jnp.logical_not(safe))
    def _():
        gather_keys(n_ctx, k_refs, keys)
        shifted(n_head, n_ctx, start_ref, first_ref, raw_q, out_ref, keys, scores, pooled, lined.at[:, 0])
        for copy in sent:
            copy.start()
        for copy in sent:
            copy.wait()


def span_kernel(n_head, n_ctx, start_ref, first_ref, *refs):
    out_ref, keys, scores, pooled, lined = refs[n_head + n_ctx:]
    gather_keys(n_ctx, refs[n_head:n_head + n_ctx], keys)
    shifted(n_head, n_ctx, start_ref, first_ref, refs[:n_head], out_ref, keys, scores, pooled, lined)


def shifted(n_head, n_ctx, start_ref, first_ref, raw_q, out_ref, keys, scores, pooled, lined):
    own, heads, tokens, depth = raw_q[0].shape
    q_refs = [[ref.at[g] for g in range(own)] for ref in raw_q]
    nsel = keys.shape[2]
    scale = math.log2(math.e) / math.sqrt(depth)
    factor = nsel / (2.0 * n_head * heads)
    chunks = n_head * heads * QTILE // CHUNK
    per_chunk = n_head // chunks

    span = SPAN_ROWS
    spans = nsel // span

    def over_spans(body, carry):
        return lax.fori_loop(0, spans, lambda n, c: body(pl.multiple_of(n * span, span), c), carry)

    def tile(index, _):
        begin = pl.multiple_of(index * QTILE, QTILE)
        first = first_ref[index]
        row4, reach = limits(n_ctx, tokens, begin, start_ref)

        for g in range(own):
            weights = []
            for c in range(chunks):
                columns = tile_columns(q_refs[c * per_chunk:(c + 1) * per_chunk], g, begin)

                def scores_span(base, tops):
                    tops = list(tops)
                    rows = jnp.concatenate([keys[g, s, pl.ds(base, span), :] for s in range(4)], axis=0)
                    piece = lax.dot_general(rows, columns, NT, preferred_element_type=jnp.float32)
                    for s in range(4):
                        for r in range(0, span, 8):
                            mask = visible(nsel, n_ctx * tokens, r, s, first, row4, reach, base)
                            for n in range(CHUNK // LANES):
                                part = piece[s * span + r:s * span + r + 8, n * LANES:(n + 1) * LANES]
                                if mask is not None:
                                    part = jnp.where(mask, part, MASKED)
                                scores[0, s, pl.ds(base + r, 8), n * LANES:(n + 1) * LANES] = part
                                tops[n] = jnp.maximum(tops[n], part)
                    return tuple(tops)

                tops = over_spans(scores_span, (jnp.full((8, LANES), MASKED, jnp.float32),) * (CHUNK // LANES))
                for n in range(CHUNK // LANES):
                    at = (c * CHUNK // LANES + n) * LANES

                    def exps_span(base, total):
                        for r in range(0, span, 8):
                            here = pl.ds(base + r, 8)
                            parts = [
                                jnp.exp2((scores[0, s, here, n * LANES:(n + 1) * LANES] - tops[n]) * scale)
                                for s in range(4)
                            ]
                            rest = parts[1] + parts[2] + parts[3]
                            pooled[0, 0, here, at:at + LANES] = parts[0]
                            pooled[0, 1, here, at:at + LANES] = rest
                            total = total + (parts[0] + rest)
                        return total

                    total = over_spans(exps_span, jnp.zeros((8, LANES), jnp.float32))
                    top = jnp.max(tops[n], axis=0, keepdims=True)
                    lowered = jnp.exp2((tops[n] - top) * scale)
                    weights.append(lowered * (factor / jnp.sum(total * lowered, axis=0, keepdims=True)))

            def sums_span(base, _):
                for r in range(0, span, 8):
                    lead, rest = [
                        sum(
                            (pooled[0, p, pl.ds(base + r, 8), n * LANES:(n + 1) * LANES] * weights[n] for n in range(1, len(weights))),
                            pooled[0, p, pl.ds(base + r, 8), 0:LANES] * weights[0],
                        )
                        for p in range(2)
                    ]
                    lined[0, 0, pl.ds(base + 8 + r, 8), :] = lead
                    lined[0, 1, pl.ds(base + 8 + r, 8), :] = lead + 2.0 * rest
                return 0

            lined[0, 1, 0:8, :] = jnp.zeros((8, LANES), jnp.float32)
            over_spans(sums_span, 0)
            blocks = lined[0, 0, 8:8 + nsel, :] + lined[0, 1, 7:7 + nsel, :]
            turned = blocks.T
            out_ref[pl.ds(begin, QTILE), g, :] = turned[:QTILE] + turned[QTILE:]
        return 0

    lax.fori_loop(0, tokens // QTILE, tile, 0)


def in_hbm(array):
    return pltpu.with_memory_space_constraint(array, pltpu.HBM)


def per_device(n_head, n_ctx, queries, keys, span_start, tile_first):
    tokens, key_heads, heads, depth = queries.shape
    blocks = keys.shape[0]
    own = key_heads // n_head
    nsel = blocks * n_ctx
    vmem = pl.BlockSpec(memory_space=pltpu.VMEM)
    smem = pl.BlockSpec(memory_space=pltpu.SMEM)
    hbm = pl.BlockSpec(memory_space=pltpu.HBM)
    q_part = jax.ShapeDtypeStruct((own, heads, tokens, depth), queries.dtype)
    k_part = jax.ShapeDtypeStruct((own, 4, blocks, depth), keys.dtype)
    packed = pl.pallas_call(
        partial(pack_kernel, n_head, key_heads, heads),
        out_shape=[q_part] * n_head + [k_part],
        in_specs=[hbm, hbm],
        out_specs=[vmem] * (n_head + 1),
        scratch_shapes=[
            pltpu.VMEM((tokens * key_heads * heads, depth), queries.dtype),
            pltpu.VMEM((blocks * 4 * key_heads, depth), keys.dtype),
            pltpu.SemaphoreType.DMA((Q_COPIES,)),
            pltpu.SemaphoreType.DMA((K_COPIES,)),
        ],
        compiler_params=pltpu.CompilerParams(vmem_limit_bytes=16 * 2 ** 20),
        name="pack",
    )(in_hbm(queries.reshape(-1, depth)), in_hbm(keys.reshape(-1, depth)))
    q_parts, k_parts = list(packed[:n_head]), [packed[n_head]]

    def swap(array, axis, size, bit):
        return lax.ppermute(array, axis, [(i, i ^ bit) for i in range(size)])

    for d in range(1, n_head):
        q_parts[d] = swap(q_parts[d], "head", n_head, d)
    bit = n_ctx // 2
    k_parts = {0: packed[n_head]}
    while bit:
        for j in list(k_parts):
            k_parts[j | bit] = swap(k_parts[j], "ctx", n_ctx, bit)
        bit //= 2
    k_parts = [k_parts[j] for j in range(n_ctx)]
    columns = n_head * heads * QTILE
    tiles = tokens // QTILE
    limit = pltpu.CompilerParams(vmem_limit_bytes=20 * 2 ** 20)
    scratch = [
        pltpu.VMEM((own, 4, nsel, depth), keys.dtype),
        pltpu.VMEM((1, 4, nsel, columns), jnp.float32),
        pltpu.VMEM((1, 2, nsel, columns), jnp.float32),
    ]
    result = jax.ShapeDtypeStruct((tokens, own, nsel), jnp.float32)
    if (n_ctx, n_head, blocks, heads * QTILE) != (4, 4, BLOCK, LANES):
        return pl.pallas_call(
            partial(span_kernel, n_head, n_ctx),
            out_shape=result,
            in_specs=[smem, smem] + [vmem] * (n_head + n_ctx),
            out_specs=vmem,
            scratch_shapes=scratch + [pltpu.VMEM((1, 2, 8 + nsel, LANES), jnp.float32)],
            compiler_params=pltpu.CompilerParams(vmem_limit_bytes=52 * 2 ** 20),
            name="importance",
        )(span_start, tile_first, *q_parts, *k_parts)
    most = 3 * LANES
    early = pl.pallas_call(
        partial(early_kernel, n_ctx),
        out_shape=[
            jax.ShapeDtypeStruct((tiles, own, 2, 3 * BLOCK, most), jnp.float32),
            jax.ShapeDtypeStruct((tiles, own, 8, most), jnp.float32),
        ],
        in_specs=[smem, smem] + [vmem] * 6,
        out_specs=[vmem, vmem],
        compiler_params=limit,
        name="early",
    )(span_start, tile_first, *q_parts[:3], *k_parts[:3])
    return pl.pallas_call(
        partial(late_kernel, n_head, n_ctx),
        out_shape=result,
        in_specs=[smem, smem] + [vmem] * (n_head + n_ctx + 2),
        out_specs=hbm,
        scratch_shapes=scratch + [
            pltpu.VMEM((2, own, 2, 8 + nsel, LANES), jnp.float32),
            pltpu.VMEM((2, own, 2, nsel, LANES), jnp.float32),
            pltpu.VMEM((2, own, 2, BLOCK, most), jnp.float32),
            pltpu.VMEM((tokens, own, nsel), jnp.float32),
            pltpu.SemaphoreType.DMA((tiles,)),
        ],
        compiler_params=limit,
        name="late",
    )(span_start, tile_first, *q_parts, *k_parts, *early)


def solution(mesh):
    placed = (
        P(("groups", "ctx"), None, "head", None),
        P(("groups", "ctx"), None, None, None),
        P("groups"),
        P(("groups", "ctx")),
    )
    return jax.shard_map(
        partial(per_device, mesh.shape["head"], mesh.shape["ctx"]),
        mesh=mesh,
        in_specs=placed,
        out_specs=P(("groups", "ctx"), "head", None),
        check_vma=False,
    )
```

```python
import math
from functools import partial

import jax
import jax.numpy as jnp
from jax import lax
from jax.experimental import pallas as pl
from jax.experimental.pallas import tpu as pltpu
from jax.sharding import PartitionSpec as P

QTILE = 64
PACK = 16
K_COPIES = 2
Q_COPIES = 3
LANES = 128
CHUNK = 512
SPAN_ROWS = 256
BLOCK = 64
SAFE = 2.0 ** 64
MASKED = -1e30
NT = (((1,), (1,)), ((), ()))


def pack_kernel(n_head, key_heads, heads, q_hbm, k_hbm, first_hbm, *refs):
    q_outs, (k_out, spread, q_ref, k_ref, first, q_sems, k_sems, sem) = refs[:n_head], refs[n_head:]
    first_copy = pltpu.make_async_copy(first_hbm, first, sem)
    me = lax.axis_index("head")
    own = key_heads // n_head
    width = own * heads
    tokens = q_outs[0].shape[2]
    blocks = k_out.shape[2]
    q_rows = PACK * key_heads * heads
    k_rows = PACK * 4
    k_copies, q_copies = [], []
    k_each, q_each = blocks // PACK // K_COPIES, tokens // PACK // Q_COPIES
    for n in range(K_COPIES):
        at = pl.ds(n * k_each * k_rows, k_each * k_rows)
        k_copies.append(pltpu.make_async_copy(k_hbm.at[at, me], k_ref.at[at], k_sems.at[n]))
    for n in range(Q_COPIES):
        at = pl.ds(n * q_each * q_rows, q_each * q_rows)
        q_copies.append(pltpu.make_async_copy(q_hbm.at[at], q_ref.at[at], q_sems.at[n]))
    for copy in k_copies + q_copies + [first_copy]:
        copy.start()

    out_row = lax.broadcasted_iota(jnp.int32, (own * k_rows, own * k_rows), 0)
    in_row = lax.broadcasted_iota(jnp.int32, (own * k_rows, own * k_rows), 1)
    source = (out_row % PACK * 4 + out_row // PACK % 4) * own + out_row // k_rows
    select = jnp.where(in_row == source, 1.0, 0.0).astype(jnp.bfloat16)
    for block in range(blocks // PACK):
        if block % k_each == 0:
            k_copies[block // k_each].wait()
        rows = k_ref[block * k_rows:(block + 1) * k_rows].reshape(own * k_rows, k_ref.shape[2])
        moved = jnp.dot(select, rows, preferred_element_type=jnp.float32).astype(jnp.bfloat16)
        for u in range(own * 4):
            k_out[u // 4, u % 4, block * PACK:(block + 1) * PACK, :] = moved[u * PACK:(u + 1) * PACK]

    first_copy.wait()
    for t in range(first_hbm.shape[0]):
        spread[t] = jnp.full((8, LANES), first[t], jnp.int32)

    out_row = lax.broadcasted_iota(jnp.int32, (n_head * width * PACK, q_rows), 0)
    in_row = lax.broadcasted_iota(jnp.int32, (n_head * width * PACK, q_rows), 1)
    step = out_row // (width * PACK)
    unit = out_row // PACK % width
    source = out_row % PACK * (key_heads * heads) + (step ^ me) * width + unit
    select = jnp.where(in_row == source, 1.0, 0.0).astype(jnp.bfloat16)
    for block in range(tokens // PACK):
        if block % q_each == 0:
            q_copies[block // q_each].wait()
        moved = jnp.dot(
            select, q_ref[block * q_rows:(block + 1) * q_rows, :], preferred_element_type=jnp.float32
        ).astype(jnp.bfloat16)
        for u in range(n_head * width):
            d, g, h = u // width, u % width // heads, u % heads
            q_outs[d][g, h, block * PACK:(block + 1) * PACK, :] = moved[u * PACK:(u + 1) * PACK]


def gather_keys(n_ctx, k_refs, keys):
    me = lax.axis_index("ctx")
    local = k_refs[0].shape[2]
    for j in range(n_ctx):
        at = pl.ds(pl.multiple_of((me ^ j) * local, local), local)
        keys[:, :, at, :] = k_refs[j][...]


def limits(n_ctx, tokens, begin, start):
    lane = lax.broadcasted_iota(jnp.int32, (8, LANES), 1)
    row = lax.broadcasted_iota(jnp.int32, (8, LANES), 0)
    place = start + lax.axis_index("ctx") * tokens + begin + lane % QTILE
    return 4 * row, place - 31 - 64 * row


def visible(nsel, span_tokens, r, s, first, row4, reach, base=None):
    least_position = 16 * 4 * nsel * 7 // 8 - span_tokens
    most_first = nsel - 1
    at = r if base is None else base + r
    mask = None
    if base is not None or 4 * r + s <= most_first:
        mask = row4 >= first - (4 * at + s)
    if base is not None or 16 * (4 * (r + 7) + s) + 31 > least_position:
        below = reach >= 64 * at + 16 * s
        mask = below if mask is None else mask & below
    return mask


def tile_columns(q_refs, g, begin):
    return jnp.concatenate(
        [q[g][h, pl.ds(begin, QTILE), :] for q in q_refs for h in range(q[g].shape[0])], axis=0
    )


def interleave(*stages):
    lengths = [length for length, _ in stages]
    done = [0] * len(stages)
    for tick in range(1, max(lengths) + 1):
        for n, (length, stage) in enumerate(stages):
            while done[n] * max(lengths) < tick * length:
                next(stage, None)
                done[n] += 1
    for _, stage in stages:
        for _ in stage:
            pass


def pooled_exponentials(q_refs, k_refs, t, group, spans, scale, masks_at, put, totals):
    for sources, j in spans:
        pieces = {}
        for g in group:
            rows = jnp.concatenate([k_refs[j][g, s] for s in range(4)], axis=0)
            columns = tile_columns([q_refs[n] for n in sources], g, t * QTILE)
            pieces[g] = lax.dot_general(rows, columns, NT, preferred_element_type=jnp.float32)
        for r in range(0, BLOCK, 8):
            masks = masks_at(t, j, r)
            for g in group:
                for at, n in enumerate(sources):
                    parts = []
                    for s in range(4):
                        part = pieces[g][s * BLOCK + r:s * BLOCK + r + 8, at * LANES:(at + 1) * LANES]
                        parts.append(jnp.exp2(jnp.where(masks[s], part, MASKED) * scale))
                    rest = parts[1] + parts[2] + parts[3]
                    put(g, n, j, r, parts[0], rest)
                    both = parts[0] + rest
                    totals[g, n] = totals[g, n] + both if (g, n) in totals else both
            yield


def mask_maker(n_ctx, tokens, start, spread):
    me = lax.axis_index("ctx")
    tiles = tokens // QTILE
    edges = [limits(n_ctx, tokens, t * QTILE, start) for t in range(tiles)]
    edges = [(row4 - spread[t], reach) for t, (row4, reach) in enumerate(edges)]

    def masks_at(t, j, r):
        low, high = edges[t]
        at = (me ^ j) * BLOCK + r
        return [(low >= -(4 * at + s)) & (high >= 64 * at + 16 * s) for s in range(4)]

    return masks_at


def early_kernel(n_ctx, start_ref, spread, *refs):
    q_refs, k_refs, (pooled, total_ref) = refs[:3], refs[3:6], refs[6:]
    own, heads, tokens, depth = q_refs[0].shape
    q_refs = [[ref.at[g] for g in range(own)] for ref in q_refs]
    scale = math.log2(math.e) / math.sqrt(depth)
    masks_at = mask_maker(n_ctx, tokens, start_ref[0], spread)
    for t in range(tokens // QTILE):
        def put(g, n, j, r, lead, rest):
            pooled[t, g, 0, j * BLOCK + r:j * BLOCK + r + 8, n * LANES:(n + 1) * LANES] = lead
            pooled[t, g, 1, j * BLOCK + r:j * BLOCK + r + 8, n * LANES:(n + 1) * LANES] = rest

        totals = {}
        spans = [((0, 1, 2), j) for j in range(3)]
        for _ in pooled_exponentials(q_refs, k_refs, t, range(own), spans, scale, masks_at, put, totals):
            pass
        for (g, n), total in totals.items():
            total_ref[t, g, :, n * LANES:(n + 1) * LANES] = total


def late_kernel(n_head, n_ctx, start_ref, first_hbm, spread, *refs):
    raw_q, k_refs, (early, early_total) = refs[:n_head], refs[n_head:n_head + n_ctx], refs[n_head + n_ctx:-10]
    out_hbm, keys, scores, pooled, lined, far, corner, out_ref, first_ref, sems = refs[-10:]
    own, heads, tokens, depth = raw_q[0].shape
    q_refs = [[ref.at[g] for g in range(own)] for ref in raw_q]
    nsel = keys.shape[2]
    scale = math.log2(math.e) / math.sqrt(depth)
    factor = nsel / (2.0 * n_head * heads)
    me = lax.axis_index("ctx")
    masks_at = mask_maker(n_ctx, tokens, start_ref[0], spread)
    tiles = tokens // QTILE
    last = n_ctx - 1
    weights, totals = {}, []
    sent = [
        pltpu.make_async_copy(out_ref.at[pl.ds(t * QTILE, QTILE)], out_hbm.at[pl.ds(t * QTILE, QTILE)], sems.at[t])
        for t in range(tiles)
    ]

    units = [(t, g) for t in range(tiles) for g in range(own)]

    def exponentials(u):
        t, g = units[u]

        def put(_, n, j, r, lead, rest):
            if n == last:
                far[u % 2, 0, j * BLOCK + r:j * BLOCK + r + 8, :] = lead
                far[u % 2, 1, j * BLOCK + r:j * BLOCK + r + 8, :] = rest
            else:
                corner[u % 2, 0, r:r + 8, n * LANES:(n + 1) * LANES] = lead
                corner[u % 2, 1, r:r + 8, n * LANES:(n + 1) * LANES] = rest

        found = {}
        spans = [((last,), j) for j in range(last)] + [(tuple(range(n_head)), last)]
        yield from pooled_exponentials(q_refs, k_refs, t, [g], spans, scale, masks_at, put, found)
        for (_, n), total in found.items():
            if n < last:
                total = total + early_total[t, g, :, n * LANES:(n + 1) * LANES]
            total = jnp.sum(total, axis=0, keepdims=True)
            weights[u, n] = factor / total
            totals.append(total)

    def sums(u):
        t, g = units[u]
        lined[u % 2, 1, 0:8, :] = jnp.zeros((8, LANES), jnp.float32)
        for j in range(n_ctx):
            for r in range(0, BLOCK, 8):
                both = []
                for p in range(2):
                    value = far[u % 2, p, j * BLOCK + r:j * BLOCK + r + 8, :] * weights[u, last]
                    for n in range(last):
                        at = slice(n * LANES, (n + 1) * LANES)
                        if j == last:
                            part = corner[u % 2, p, r:r + 8, at]
                        else:
                            part = early[t, g, p, j * BLOCK + r:j * BLOCK + r + 8, at]
                        value = value + part * weights[u, n]
                    both.append(value)
                here = pl.ds(pl.multiple_of(8 + (me ^ j) * BLOCK + r, 8), 8)
                lined[u % 2, 0, here, :] = both[0]
                lined[u % 2, 1, here, :] = both[0] + 2.0 * both[1]
                yield
        turned = (lined[u % 2, 0, 8:8 + nsel, :] + lined[u % 2, 1, 7:7 + nsel, :]).T
        out_ref[t * QTILE:(t + 1) * QTILE, g, :] = turned[:QTILE] + turned[QTILE:]
        if g == own - 1:
            sent[t].start()
        yield

    for step in range(len(units) + 1):
        stages = []
        if step < len(units):
            stages.append((nsel // 8, exponentials(step)))
        if step >= 1:
            stages.append((nsel // 8 + 1, sums(step - 1)))
        interleave(*stages)

    least, most = totals[0], totals[0]
    for part in totals[1:]:
        least, most = jnp.minimum(least, part), jnp.maximum(most, part)
    safe = (jnp.min(least) >= 1.0 / SAFE) & (jnp.max(most) <= SAFE)
    for copy in sent:
        copy.wait()

    @pl.when(jnp.logical_not(safe))
    def _():
        first_copy = pltpu.make_async_copy(first_hbm, first_ref, sems.at[0])
        first_copy.start()
        first_copy.wait()
        gather_keys(n_ctx, k_refs, keys)
        shifted(n_head, n_ctx, start_ref, first_ref, raw_q, out_ref, keys, scores, pooled, lined)
        for copy in sent:
            copy.start()
        for copy in sent:
            copy.wait()


def span_kernel(n_head, n_ctx, start_ref, first_ref, *refs):
    out_ref, keys, scores, pooled, lined = refs[n_head + n_ctx:]
    gather_keys(n_ctx, refs[n_head:n_head + n_ctx], keys)
    shifted(n_head, n_ctx, start_ref, first_ref, refs[:n_head], out_ref, keys, scores, pooled, lined)


def shifted(n_head, n_ctx, start_ref, first_ref, raw_q, out_ref, keys, scores, pooled, lined):
    own, heads, tokens, depth = raw_q[0].shape
    q_refs = [[ref.at[g] for g in range(own)] for ref in raw_q]
    nsel = keys.shape[2]
    scale = math.log2(math.e) / math.sqrt(depth)
    factor = nsel / (2.0 * n_head * heads)
    chunks = n_head * heads * QTILE // CHUNK
    per_chunk = n_head // chunks

    span = SPAN_ROWS
    spans = nsel // span

    def over_spans(body, carry):
        return lax.fori_loop(0, spans, lambda n, c: body(pl.multiple_of(n * span, span), c), carry)

    def tile(index, _):
        begin = pl.multiple_of(index * QTILE, QTILE)
        first = first_ref[index]
        row4, reach = limits(n_ctx, tokens, begin, start_ref[0])

        for g in range(own):
            weights = []
            for c in range(chunks):
                columns = tile_columns(q_refs[c * per_chunk:(c + 1) * per_chunk], g, begin)

                def scores_span(base, tops):
                    tops = list(tops)
                    rows = jnp.concatenate([keys[g, s, pl.ds(base, span), :] for s in range(4)], axis=0)
                    piece = lax.dot_general(rows, columns, NT, preferred_element_type=jnp.float32)
                    for s in range(4):
                        for r in range(0, span, 8):
                            mask = visible(nsel, n_ctx * tokens, r, s, first, row4, reach, base)
                            for n in range(CHUNK // LANES):
                                part = piece[s * span + r:s * span + r + 8, n * LANES:(n + 1) * LANES]
                                if mask is not None:
                                    part = jnp.where(mask, part, MASKED)
                                scores[0, s, pl.ds(base + r, 8), n * LANES:(n + 1) * LANES] = part
                                tops[n] = jnp.maximum(tops[n], part)
                    return tuple(tops)

                tops = over_spans(scores_span, (jnp.full((8, LANES), MASKED, jnp.float32),) * (CHUNK // LANES))
                for n in range(CHUNK // LANES):
                    at = (c * CHUNK // LANES + n) * LANES

                    def exps_span(base, total):
                        for r in range(0, span, 8):
                            here = pl.ds(base + r, 8)
                            parts = [
                                jnp.exp2((scores[0, s, here, n * LANES:(n + 1) * LANES] - tops[n]) * scale)
                                for s in range(4)
                            ]
                            rest = parts[1] + parts[2] + parts[3]
                            pooled[0, 0, here, at:at + LANES] = parts[0]
                            pooled[0, 1, here, at:at + LANES] = rest
                            total = total + (parts[0] + rest)
                        return total

                    total = over_spans(exps_span, jnp.zeros((8, LANES), jnp.float32))
                    top = jnp.max(tops[n], axis=0, keepdims=True)
                    lowered = jnp.exp2((tops[n] - top) * scale)
                    weights.append(lowered * (factor / jnp.sum(total * lowered, axis=0, keepdims=True)))

            def sums_span(base, _):
                for r in range(0, span, 8):
                    lead, rest = [
                        sum(
                            (pooled[0, p, pl.ds(base + r, 8), n * LANES:(n + 1) * LANES] * weights[n] for n in range(1, len(weights))),
                            pooled[0, p, pl.ds(base + r, 8), 0:LANES] * weights[0],
                        )
                        for p in range(2)
                    ]
                    lined[0, 0, pl.ds(base + 8 + r, 8), :] = lead
                    lined[0, 1, pl.ds(base + 8 + r, 8), :] = lead + 2.0 * rest
                return 0

            lined[0, 1, 0:8, :] = jnp.zeros((8, LANES), jnp.float32)
            over_spans(sums_span, 0)
            blocks = lined[0, 0, 8:8 + nsel, :] + lined[0, 1, 7:7 + nsel, :]
            turned = blocks.T
            out_ref[pl.ds(begin, QTILE), g, :] = turned[:QTILE] + turned[QTILE:]
        return 0

    lax.fori_loop(0, tokens // QTILE, tile, 0)


def in_hbm(array):
    return pltpu.with_memory_space_constraint(array, pltpu.HBM)


def per_device(n_head, n_ctx, queries, keys, span_start, tile_first):
    tokens, key_heads, heads, depth = queries.shape
    blocks = keys.shape[0]
    own = key_heads // n_head
    nsel = blocks * n_ctx
    vmem = pl.BlockSpec(memory_space=pltpu.VMEM)
    smem = pl.BlockSpec(memory_space=pltpu.SMEM)
    hbm = pl.BlockSpec(memory_space=pltpu.HBM)
    q_part = jax.ShapeDtypeStruct((own, heads, tokens, depth), queries.dtype)
    k_part = jax.ShapeDtypeStruct((own, 4, blocks, depth), keys.dtype)
    packed = pl.pallas_call(
        partial(pack_kernel, n_head, key_heads, heads),
        out_shape=[q_part] * n_head + [k_part, jax.ShapeDtypeStruct((tokens // QTILE, 8, LANES), jnp.int32)],
        in_specs=[hbm] * 3,
        out_specs=[vmem] * (n_head + 2),
        scratch_shapes=[
            pltpu.VMEM((tokens * key_heads * heads, depth), queries.dtype),
            pltpu.VMEM((blocks * 4, own, depth), keys.dtype),
            pltpu.SMEM(tile_first.shape, jnp.int32),
            pltpu.SemaphoreType.DMA((Q_COPIES,)),
            pltpu.SemaphoreType.DMA((K_COPIES,)),
            pltpu.SemaphoreType.DMA,
        ],
        compiler_params=pltpu.CompilerParams(vmem_limit_bytes=16 * 2 ** 20),
        name="pack",
    )(in_hbm(queries.reshape(-1, depth)), in_hbm(keys.reshape(-1, n_head, own, depth)), in_hbm(tile_first))
    q_parts, k_parts = list(packed[:n_head]), [packed[n_head]]

    def swap(array, axis, size, bit):
        return lax.ppermute(array, axis, [(i, i ^ bit) for i in range(size)])

    for d in range(1, n_head):
        q_parts[d] = swap(q_parts[d], "head", n_head, d)
    bit = n_ctx // 2
    k_parts = {0: packed[n_head]}
    while bit:
        for j in list(k_parts):
            k_parts[j | bit] = swap(k_parts[j], "ctx", n_ctx, bit)
        bit //= 2
    k_parts = [k_parts[j] for j in range(n_ctx)]
    columns = n_head * heads * QTILE
    tiles = tokens // QTILE
    limit = pltpu.CompilerParams(vmem_limit_bytes=20 * 2 ** 20)
    scratch = [
        pltpu.VMEM((own, 4, nsel, depth), keys.dtype),
        pltpu.VMEM((1, 4, nsel, columns), jnp.float32),
        pltpu.VMEM((1, 2, nsel, columns), jnp.float32),
    ]
    result = jax.ShapeDtypeStruct((tokens, own, nsel), jnp.float32)
    if (n_ctx, n_head, blocks, heads * QTILE) != (4, 4, BLOCK, LANES):
        return pl.pallas_call(
            partial(span_kernel, n_head, n_ctx),
            out_shape=result,
            in_specs=[smem, smem] + [vmem] * (n_head + n_ctx),
            out_specs=vmem,
            scratch_shapes=scratch + [pltpu.VMEM((1, 2, 8 + nsel, LANES), jnp.float32)],
            compiler_params=pltpu.CompilerParams(vmem_limit_bytes=52 * 2 ** 20),
            name="importance",
        )(span_start, tile_first, *q_parts, *k_parts)
    most = 3 * LANES
    early = pl.pallas_call(
        partial(early_kernel, n_ctx),
        out_shape=[
            jax.ShapeDtypeStruct((tiles, own, 2, 3 * BLOCK, most), jnp.float32),
            jax.ShapeDtypeStruct((tiles, own, 8, most), jnp.float32),
        ],
        in_specs=[smem] + [vmem] * 7,
        out_specs=[vmem, vmem],
        compiler_params=limit,
        name="early",
    )(span_start, packed[n_head + 1], *q_parts[:3], *k_parts[:3])
    return pl.pallas_call(
        partial(late_kernel, n_head, n_ctx),
        out_shape=result,
        in_specs=[smem, hbm] + [vmem] * (n_head + n_ctx + 3),
        out_specs=hbm,
        scratch_shapes=scratch + [
            pltpu.VMEM((2, 2, 8 + nsel, LANES), jnp.float32),
            pltpu.VMEM((2, 2, nsel, LANES), jnp.float32),
            pltpu.VMEM((2, 2, BLOCK, most), jnp.float32),
            pltpu.VMEM((tokens, own, nsel), jnp.float32),
            pltpu.SMEM(tile_first.shape, jnp.int32),
            pltpu.SemaphoreType.DMA((tiles,)),
        ],
        compiler_params=limit,
        name="late",
    )(span_start, in_hbm(tile_first), packed[n_head + 1], *q_parts, *k_parts, *early)


def solution(mesh):
    placed = (
        P(("groups", "ctx"), None, "head", None),
        P(("groups", "ctx"), None, None, None),
        P("groups"),
        P(("groups", "ctx")),
    )
    return jax.shard_map(
        partial(per_device, mesh.shape["head"], mesh.shape["ctx"]),
        mesh=mesh,
        in_specs=placed,
        out_specs=P(("groups", "ctx"), "head", None),
        check_vma=False,
    )
```

```python
import math
from functools import partial

import jax
import jax.numpy as jnp
from jax import lax
from jax.experimental import pallas as pl
from jax.experimental.pallas import tpu as pltpu
from jax.sharding import PartitionSpec as P

QTILE = 64
PACK = 16
K_COPIES = 2
Q_COPIES = 3
LANES = 128
CHUNK = 512
SPAN_ROWS = 256
BLOCK = 64
SAFE = 2.0 ** 64
MASKED = -1e30
NT = (((1,), (1,)), ((), ()))


def pack_kernel(n_head, key_heads, heads, q_hbm, k_hbm, first_hbm, *refs):
    q_outs, (k_out, spread, q_ref, k_ref, first, q_sems, k_sems, sem) = refs[:n_head], refs[n_head:]
    first_copy = pltpu.make_async_copy(first_hbm, first, sem)
    me = lax.axis_index("head")
    own = key_heads // n_head
    width = own * heads
    tokens = q_outs[0].shape[2]
    blocks = k_out.shape[2]
    q_rows = PACK * key_heads * heads
    k_rows = PACK * 4
    k_copies, q_copies = [], []
    k_each, q_each = blocks // PACK // K_COPIES, tokens // PACK // Q_COPIES
    for n in range(K_COPIES):
        at = pl.ds(n * k_each * k_rows, k_each * k_rows)
        k_copies.append(pltpu.make_async_copy(k_hbm.at[at, me], k_ref.at[at], k_sems.at[n]))
    for n in range(Q_COPIES):
        at = pl.ds(n * q_each * q_rows, q_each * q_rows)
        q_copies.append(pltpu.make_async_copy(q_hbm.at[at], q_ref.at[at], q_sems.at[n]))
    for copy in k_copies + q_copies + [first_copy]:
        copy.start()

    def bits(value, low, count):
        return (value >> low.bit_length() - 1) & (count - 1)

    out_row = lax.broadcasted_iota(jnp.int32, (own * k_rows, own * k_rows), 0)
    in_row = lax.broadcasted_iota(jnp.int32, (own * k_rows, own * k_rows), 1)
    source = (bits(out_row, 1, PACK) * 4 + bits(out_row, PACK, 4)) * own + bits(out_row, k_rows, own)
    k_select = jnp.where(in_row == source, 1.0, 0.0).astype(jnp.bfloat16)
    out_row = lax.broadcasted_iota(jnp.int32, (n_head * width * PACK, q_rows), 0)
    in_row = lax.broadcasted_iota(jnp.int32, (n_head * width * PACK, q_rows), 1)
    unit = (bits(out_row, width * PACK, n_head) ^ me) * width + bits(out_row, PACK, width)
    q_select = jnp.where(in_row == bits(out_row, 1, PACK) * (key_heads * heads) + unit, 1.0, 0.0).astype(jnp.bfloat16)

    first_copy.wait()
    for t in range(first_hbm.shape[0]):
        spread[t] = jnp.full((8, LANES), first[t], jnp.int32)
    for block in range(blocks // PACK):
        if block % k_each == 0:
            k_copies[block // k_each].wait()
        rows = k_ref[block * k_rows:(block + 1) * k_rows].reshape(own * k_rows, k_ref.shape[2])
        moved = jnp.dot(k_select, rows, preferred_element_type=jnp.float32).astype(jnp.bfloat16)
        for u in range(own * 4):
            k_out[u // 4, u % 4, block * PACK:(block + 1) * PACK, :] = moved[u * PACK:(u + 1) * PACK]
    for block in range(tokens // PACK):
        if block % q_each == 0:
            q_copies[block // q_each].wait()
        moved = jnp.dot(
            q_select, q_ref[block * q_rows:(block + 1) * q_rows, :], preferred_element_type=jnp.float32
        ).astype(jnp.bfloat16)
        for d in range(n_head):
            for u in range(width):
                at = (d * width + u) * PACK
                q_outs[d][u // heads, u % heads, block * PACK:(block + 1) * PACK, :] = moved[at:at + PACK]


def gather_keys(n_ctx, k_refs, keys):
    me = lax.axis_index("ctx")
    local = k_refs[0].shape[2]
    for j in range(n_ctx):
        at = pl.ds(pl.multiple_of((me ^ j) * local, local), local)
        keys[:, :, at, :] = k_refs[j][...]


def limits(n_ctx, tokens, begin, start):
    lane = lax.broadcasted_iota(jnp.int32, (8, LANES), 1)
    row = lax.broadcasted_iota(jnp.int32, (8, LANES), 0)
    place = start + lax.axis_index("ctx") * tokens + begin + lane % QTILE
    return 4 * row, place - 31 - 64 * row


def visible(nsel, span_tokens, r, s, first, row4, reach, base=None):
    least_position = 16 * 4 * nsel * 7 // 8 - span_tokens
    most_first = nsel - 1
    at = r if base is None else base + r
    mask = None
    if base is not None or 4 * r + s <= most_first:
        mask = row4 >= first - (4 * at + s)
    if base is not None or 16 * (4 * (r + 7) + s) + 31 > least_position:
        below = reach >= 64 * at + 16 * s
        mask = below if mask is None else mask & below
    return mask


def tile_columns(q_refs, g, begin):
    return jnp.concatenate(
        [q[g][h, pl.ds(begin, QTILE), :] for q in q_refs for h in range(q[g].shape[0])], axis=0
    )


def interleave(*stages):
    lengths = [length for length, _ in stages]
    done = [0] * len(stages)
    for tick in range(1, max(lengths) + 1):
        for n, (length, stage) in enumerate(stages):
            while done[n] * max(lengths) < tick * length:
                next(stage, None)
                done[n] += 1
    for _, stage in stages:
        for _ in stage:
            pass


def pooled_exponentials(q_refs, k_refs, t, group, spans, scale, masks_at, put, totals):
    for sources, j in spans:
        pieces = {}
        for g in group:
            rows = jnp.concatenate([k_refs[j][g, s] for s in range(4)], axis=0)
            columns = tile_columns([q_refs[n] for n in sources], g, t * QTILE)
            pieces[g] = lax.dot_general(rows, columns, NT, preferred_element_type=jnp.float32)
        for r in range(0, BLOCK, 8):
            masks = masks_at(t, j, r)
            for g in group:
                for at, n in enumerate(sources):
                    parts = []
                    for s in range(4):
                        part = pieces[g][s * BLOCK + r:s * BLOCK + r + 8, at * LANES:(at + 1) * LANES]
                        parts.append(jnp.exp2(jnp.where(masks[s], part, MASKED) * scale))
                    rest = parts[1] + parts[2] + parts[3]
                    put(g, n, j, r, parts[0], rest)
                    both = parts[0] + rest
                    totals[g, n] = totals[g, n] + both if (g, n) in totals else both
            yield


def mask_maker(n_ctx, tokens, start, spread):
    me = lax.axis_index("ctx")
    tiles = tokens // QTILE
    edges = [limits(n_ctx, tokens, t * QTILE, start) for t in range(tiles)]
    edges = [(row4 - spread[t], reach) for t, (row4, reach) in enumerate(edges)]

    def masks_at(t, j, r):
        low, high = edges[t]
        at = (me ^ j) * BLOCK + r
        return [(low >= -(4 * at + s)) & (high >= 64 * at + 16 * s) for s in range(4)]

    return masks_at


def early_kernel(n_ctx, n_before, start_ref, spread, *refs):
    refs = refs[n_before:]
    q_refs, k_refs, (pooled, total_ref) = refs[:-2 - n_ctx + 1], refs[-2 - n_ctx + 1:-2], refs[-2:]
    own, heads, tokens, depth = q_refs[0].shape
    q_refs = [[ref.at[g] for g in range(own)] for ref in q_refs]
    scale = math.log2(math.e) / math.sqrt(depth)
    masks_at = mask_maker(n_ctx, tokens, start_ref[0], spread)
    for t in range(tokens // QTILE):
        def put(g, n, j, r, lead, rest):
            pooled[t, g, 0, j * BLOCK + r:j * BLOCK + r + 8, n * LANES:(n + 1) * LANES] = lead
            pooled[t, g, 1, j * BLOCK + r:j * BLOCK + r + 8, n * LANES:(n + 1) * LANES] = rest

        totals = {}
        spans = [(tuple(range(len(q_refs))), j) for j in range(n_ctx - 1)]
        for _ in pooled_exponentials(q_refs, k_refs, t, range(own), spans, scale, masks_at, put, totals):
            pass
        for (g, n), total in totals.items():
            total_ref[t, g, :, n * LANES:(n + 1) * LANES] = total


def late_kernel(n_head, n_ctx, start_ref, first_hbm, spread, *refs):
    raw_q, k_refs, early = refs[:n_head], refs[n_head:n_head + n_ctx], refs[n_head + n_ctx:-9]
    out_hbm, keys, scores, pooled, lined, corner, out_ref, first_ref, sems = refs[-9:]
    own, heads, tokens, depth = raw_q[0].shape
    q_refs = [[ref.at[g] for g in range(own)] for ref in raw_q]
    nsel = keys.shape[2]
    scale = math.log2(math.e) / math.sqrt(depth)
    factor = nsel / (2.0 * n_head * heads)
    me = lax.axis_index("ctx")
    masks_at = mask_maker(n_ctx, tokens, start_ref[0], spread)
    tiles = tokens // QTILE
    last = n_ctx - 1
    weights, totals = {}, []
    sent = [
        pltpu.make_async_copy(out_ref.at[pl.ds(t * QTILE, QTILE)], out_hbm.at[pl.ds(t * QTILE, QTILE)], sems.at[t])
        for t in range(tiles)
    ]

    units = [(t, g) for t in range(tiles) for g in range(own)]

    def earlier(n):
        kept, total = early[:2] if n < n_head - 1 else early[2:]
        n = n if n < n_head - 1 else 0
        return kept, slice(n * LANES, (n + 1) * LANES), total

    def exponentials(u):
        t, g = units[u]

        def put(_, n, j, r, lead, rest):
            corner[u % 2, 0, r:r + 8, n * LANES:(n + 1) * LANES] = lead
            corner[u % 2, 1, r:r + 8, n * LANES:(n + 1) * LANES] = rest

        found = {}
        spans = [(tuple(range(n_head)), last)]
        yield from pooled_exponentials(q_refs, k_refs, t, [g], spans, scale, masks_at, put, found)
        for (_, n), total in found.items():
            _, at_n, early_total = earlier(n)
            total = jnp.sum(total + early_total[t, g, :, at_n], axis=0, keepdims=True)
            weights[u, n] = factor / total
            totals.append(total)

    def sums(u):
        t, g = units[u]
        lined[u % 2, 1, 0:8, :] = jnp.zeros((8, LANES), jnp.float32)
        for j in range(n_ctx):
            for r in range(0, BLOCK, 8):
                both = []
                for p in range(2):
                    value = None
                    for n in range(n_head):
                        if j == last:
                            part = corner[u % 2, p, r:r + 8, n * LANES:(n + 1) * LANES]
                        else:
                            kept, at_n, _ = earlier(n)
                            part = kept[t, g, p, j * BLOCK + r:j * BLOCK + r + 8, at_n]
                        part = part * weights[u, n]
                        value = part if value is None else value + part
                    both.append(value)
                here = pl.ds(pl.multiple_of(8 + (me ^ j) * BLOCK + r, 8), 8)
                lined[u % 2, 0, here, :] = both[0]
                lined[u % 2, 1, here, :] = both[0] + 2.0 * both[1]
                yield
        turned = (lined[u % 2, 0, 8:8 + nsel, :] + lined[u % 2, 1, 7:7 + nsel, :]).T
        out_ref[t * QTILE:(t + 1) * QTILE, g, :] = turned[:QTILE] + turned[QTILE:]
        if g == own - 1:
            sent[t].start()
        yield

    for step in range(len(units) + 1):
        stages = []
        if step < len(units):
            stages.append((BLOCK // 8, exponentials(step)))
        if step >= 1:
            stages.append((nsel // 8 + 1, sums(step - 1)))
        interleave(*stages)

    least, most = totals[0], totals[0]
    for part in totals[1:]:
        least, most = jnp.minimum(least, part), jnp.maximum(most, part)
    safe = (jnp.min(least) >= 1.0 / SAFE) & (jnp.max(most) <= SAFE)
    for copy in sent:
        copy.wait()

    @pl.when(jnp.logical_not(safe))
    def _():
        first_copy = pltpu.make_async_copy(first_hbm, first_ref, sems.at[0])
        first_copy.start()
        first_copy.wait()
        gather_keys(n_ctx, k_refs, keys)
        shifted(n_head, n_ctx, start_ref, first_ref, raw_q, out_ref, keys, scores, pooled, lined)
        for copy in sent:
            copy.start()
        for copy in sent:
            copy.wait()


def span_kernel(n_head, n_ctx, start_ref, first_ref, *refs):
    out_ref, keys, scores, pooled, lined = refs[n_head + n_ctx:]
    gather_keys(n_ctx, refs[n_head:n_head + n_ctx], keys)
    shifted(n_head, n_ctx, start_ref, first_ref, refs[:n_head], out_ref, keys, scores, pooled, lined)


def shifted(n_head, n_ctx, start_ref, first_ref, raw_q, out_ref, keys, scores, pooled, lined):
    own, heads, tokens, depth = raw_q[0].shape
    q_refs = [[ref.at[g] for g in range(own)] for ref in raw_q]
    nsel = keys.shape[2]
    scale = math.log2(math.e) / math.sqrt(depth)
    factor = nsel / (2.0 * n_head * heads)
    chunks = n_head * heads * QTILE // CHUNK
    per_chunk = n_head // chunks

    span = SPAN_ROWS
    spans = nsel // span

    def over_spans(body, carry):
        return lax.fori_loop(0, spans, lambda n, c: body(pl.multiple_of(n * span, span), c), carry)

    def tile(index, _):
        begin = pl.multiple_of(index * QTILE, QTILE)
        first = first_ref[index]
        row4, reach = limits(n_ctx, tokens, begin, start_ref[0])

        for g in range(own):
            weights = []
            for c in range(chunks):
                columns = tile_columns(q_refs[c * per_chunk:(c + 1) * per_chunk], g, begin)

                def scores_span(base, tops):
                    tops = list(tops)
                    rows = jnp.concatenate([keys[g, s, pl.ds(base, span), :] for s in range(4)], axis=0)
                    piece = lax.dot_general(rows, columns, NT, preferred_element_type=jnp.float32)
                    for s in range(4):
                        for r in range(0, span, 8):
                            mask = visible(nsel, n_ctx * tokens, r, s, first, row4, reach, base)
                            for n in range(CHUNK // LANES):
                                part = piece[s * span + r:s * span + r + 8, n * LANES:(n + 1) * LANES]
                                if mask is not None:
                                    part = jnp.where(mask, part, MASKED)
                                scores[0, s, pl.ds(base + r, 8), n * LANES:(n + 1) * LANES] = part
                                tops[n] = jnp.maximum(tops[n], part)
                    return tuple(tops)

                tops = over_spans(scores_span, (jnp.full((8, LANES), MASKED, jnp.float32),) * (CHUNK // LANES))
                for n in range(CHUNK // LANES):
                    at = (c * CHUNK // LANES + n) * LANES

                    def exps_span(base, total):
                        for r in range(0, span, 8):
                            here = pl.ds(base + r, 8)
                            parts = [
                                jnp.exp2((scores[0, s, here, n * LANES:(n + 1) * LANES] - tops[n]) * scale)
                                for s in range(4)
                            ]
                            rest = parts[1] + parts[2] + parts[3]
                            pooled[0, 0, here, at:at + LANES] = parts[0]
                            pooled[0, 1, here, at:at + LANES] = rest
                            total = total + (parts[0] + rest)
                        return total

                    total = over_spans(exps_span, jnp.zeros((8, LANES), jnp.float32))
                    top = jnp.max(tops[n], axis=0, keepdims=True)
                    lowered = jnp.exp2((tops[n] - top) * scale)
                    weights.append(lowered * (factor / jnp.sum(total * lowered, axis=0, keepdims=True)))

            def sums_span(base, _):
                for r in range(0, span, 8):
                    lead, rest = [
                        sum(
                            (pooled[0, p, pl.ds(base + r, 8), n * LANES:(n + 1) * LANES] * weights[n] for n in range(1, len(weights))),
                            pooled[0, p, pl.ds(base + r, 8), 0:LANES] * weights[0],
                        )
                        for p in range(2)
                    ]
                    lined[0, 0, pl.ds(base + 8 + r, 8), :] = lead
                    lined[0, 1, pl.ds(base + 8 + r, 8), :] = lead + 2.0 * rest
                return 0

            lined[0, 1, 0:8, :] = jnp.zeros((8, LANES), jnp.float32)
            over_spans(sums_span, 0)
            blocks = lined[0, 0, 8:8 + nsel, :] + lined[0, 1, 7:7 + nsel, :]
            turned = blocks.T
            out_ref[pl.ds(begin, QTILE), g, :] = turned[:QTILE] + turned[QTILE:]
        return 0

    lax.fori_loop(0, tokens // QTILE, tile, 0)


def in_hbm(array):
    return pltpu.with_memory_space_constraint(array, pltpu.HBM)


def per_device(n_head, n_ctx, queries, keys, span_start, tile_first):
    tokens, key_heads, heads, depth = queries.shape
    blocks = keys.shape[0]
    own = key_heads // n_head
    nsel = blocks * n_ctx
    vmem = pl.BlockSpec(memory_space=pltpu.VMEM)
    smem = pl.BlockSpec(memory_space=pltpu.SMEM)
    hbm = pl.BlockSpec(memory_space=pltpu.HBM)
    q_part = jax.ShapeDtypeStruct((own, heads, tokens, depth), queries.dtype)
    k_part = jax.ShapeDtypeStruct((own, 4, blocks, depth), keys.dtype)
    packed = pl.pallas_call(
        partial(pack_kernel, n_head, key_heads, heads),
        out_shape=[q_part] * n_head + [k_part, jax.ShapeDtypeStruct((tokens // QTILE, 8, LANES), jnp.int32)],
        in_specs=[hbm] * 3,
        out_specs=[vmem] * (n_head + 2),
        scratch_shapes=[
            pltpu.VMEM((tokens * key_heads * heads, depth), queries.dtype),
            pltpu.VMEM((blocks * 4, own, depth), keys.dtype),
            pltpu.SMEM(tile_first.shape, jnp.int32),
            pltpu.SemaphoreType.DMA((Q_COPIES,)),
            pltpu.SemaphoreType.DMA((K_COPIES,)),
            pltpu.SemaphoreType.DMA,
        ],
        compiler_params=pltpu.CompilerParams(vmem_limit_bytes=16 * 2 ** 20),
        name="pack",
    )(in_hbm(queries.reshape(-1, depth)), in_hbm(keys.reshape(-1, n_head, own, depth)), in_hbm(tile_first))
    q_parts, k_parts = list(packed[:n_head]), [packed[n_head]]

    def swap(array, axis, size, bit):
        return lax.ppermute(array, axis, [(i, i ^ bit) for i in range(size)])

    for d in range(1, n_head):
        q_parts[d] = swap(q_parts[d], "head", n_head, d)
    bit = n_ctx // 2
    k_parts = {0: packed[n_head]}
    while bit:
        for j in list(k_parts):
            k_parts[j | bit] = swap(k_parts[j], "ctx", n_ctx, bit)
        bit //= 2
    k_parts = [k_parts[j] for j in range(n_ctx)]
    columns = n_head * heads * QTILE
    tiles = tokens // QTILE
    limit = pltpu.CompilerParams(vmem_limit_bytes=20 * 2 ** 20)
    scratch = [
        pltpu.VMEM((own, 4, nsel, depth), keys.dtype),
        pltpu.VMEM((1, 4, nsel, columns), jnp.float32),
        pltpu.VMEM((1, 2, nsel, columns), jnp.float32),
    ]
    result = jax.ShapeDtypeStruct((tokens, own, nsel), jnp.float32)
    if (n_ctx, n_head, blocks, heads * QTILE) != (4, 4, BLOCK, LANES):
        return pl.pallas_call(
            partial(span_kernel, n_head, n_ctx),
            out_shape=result,
            in_specs=[smem, smem] + [vmem] * (n_head + n_ctx),
            out_specs=vmem,
            scratch_shapes=scratch + [pltpu.VMEM((1, 2, 8 + nsel, LANES), jnp.float32)],
            compiler_params=pltpu.CompilerParams(vmem_limit_bytes=52 * 2 ** 20),
            name="importance",
        )(span_start, tile_first, *q_parts, *k_parts)
    early = []
    for sources in (q_parts[:3], q_parts[3:]):
        lanes = len(sources) * LANES
        early += pl.pallas_call(
            partial(early_kernel, n_ctx, len(early[1:])),
            out_shape=[
                jax.ShapeDtypeStruct((tiles, own, 2, 3 * BLOCK, lanes), jnp.float32),
                jax.ShapeDtypeStruct((tiles, own, 8, lanes), jnp.float32),
            ],
            in_specs=[smem, vmem] + [pl.BlockSpec(memory_space=pl.ANY)] * len(early[1:]) + [vmem] * (len(sources) + 3),
            out_specs=[vmem, vmem],
            compiler_params=limit,
            name="early",
        )(span_start, packed[n_head + 1], *early[1:], *sources, *k_parts[:3])
    return pl.pallas_call(
        partial(late_kernel, n_head, n_ctx),
        out_shape=result,
        in_specs=[smem, hbm] + [vmem] * (n_head + n_ctx + 5),
        out_specs=hbm,
        scratch_shapes=scratch + [
            pltpu.VMEM((2, 2, 8 + nsel, LANES), jnp.float32),
            pltpu.VMEM((2, 2, BLOCK, columns), jnp.float32),
            pltpu.VMEM((tokens, own, nsel), jnp.float32),
            pltpu.SMEM(tile_first.shape, jnp.int32),
            pltpu.SemaphoreType.DMA((tiles,)),
        ],
        compiler_params=limit,
        name="late",
    )(span_start, in_hbm(tile_first), packed[n_head + 1], *q_parts, *k_parts, *early)


def solution(mesh):
    placed = (
        P(("groups", "ctx"), None, "head", None),
        P(("groups", "ctx"), None, None, None),
        P("groups"),
        P(("groups", "ctx")),
    )
    return jax.shard_map(
        partial(per_device, mesh.shape["head"], mesh.shape["ctx"]),
        mesh=mesh,
        in_specs=placed,
        out_specs=P(("groups", "ctx"), "head", None),
        check_vma=False,
    )
```

```python
import math
from functools import partial

import jax
import jax.numpy as jnp
from jax import lax
from jax.experimental import pallas as pl
from jax.experimental.pallas import tpu as pltpu
from jax.sharding import PartitionSpec as P

QTILE = 64
PACK = 16
K_COPIES = 2
Q_COPIES = 4
LANES = 128
CHUNK = 512
SPAN_ROWS = 256
BLOCK = 64
SAFE = 2.0 ** 64
MASKED = -1e30
NT = (((1,), (1,)), ((), ()))


def pack_kernel(n_head, key_heads, heads, q_hbm, k_hbm, first_hbm, *refs):
    q_outs, (k_out, spread, q_ref, k_ref, first, q_sems, k_sems, sem) = refs[:n_head], refs[n_head:]
    first_copy = pltpu.make_async_copy(first_hbm, first, sem)
    me = lax.axis_index("head")
    own = key_heads // n_head
    width = own * heads
    tokens = q_outs[0].shape[2]
    blocks = k_out.shape[2]
    q_rows = PACK * key_heads * heads
    k_rows = PACK * 4
    k_copies, q_copies = [], []
    k_each, q_each = blocks // PACK // K_COPIES, tokens // PACK // Q_COPIES
    for n in range(K_COPIES):
        at = pl.ds(n * k_each * k_rows, k_each * k_rows)
        k_copies.append(pltpu.make_async_copy(k_hbm.at[at, me], k_ref.at[at], k_sems.at[n]))
    for n in range(Q_COPIES):
        at = pl.ds(n * q_each * q_rows, q_each * q_rows)
        q_copies.append(pltpu.make_async_copy(q_hbm.at[at], q_ref.at[at], q_sems.at[n]))
    for copy in k_copies + q_copies + [first_copy]:
        copy.start()

    def bits(value, low, count):
        return (value >> low.bit_length() - 1) & (count - 1)

    out_row = lax.broadcasted_iota(jnp.int32, (own * k_rows, own * k_rows), 0)
    in_row = lax.broadcasted_iota(jnp.int32, (own * k_rows, own * k_rows), 1)
    source = (bits(out_row, 1, PACK) * 4 + bits(out_row, PACK, 4)) * own + bits(out_row, k_rows, own)
    k_select = jnp.where(in_row == source, 1.0, 0.0).astype(jnp.bfloat16)
    out_row = lax.broadcasted_iota(jnp.int32, (n_head * width * PACK, q_rows), 0)
    in_row = lax.broadcasted_iota(jnp.int32, (n_head * width * PACK, q_rows), 1)
    unit = (bits(out_row, width * PACK, n_head) ^ me) * width + bits(out_row, PACK, width)
    q_select = jnp.where(in_row == bits(out_row, 1, PACK) * (key_heads * heads) + unit, 1.0, 0.0).astype(jnp.bfloat16)

    for block in range(tokens // PACK):
        if block % q_each == 0:
            q_copies[block // q_each].wait()
        moved = jnp.dot(
            q_select, q_ref[block * q_rows:(block + 1) * q_rows, :], preferred_element_type=jnp.float32
        ).astype(jnp.bfloat16)
        for d in range(n_head):
            for u in range(width):
                at = (d * width + u) * PACK
                q_outs[d][u // heads, u % heads, block * PACK:(block + 1) * PACK, :] = moved[at:at + PACK]
    for block in range(blocks // PACK):
        if block % k_each == 0:
            k_copies[block // k_each].wait()
        rows = k_ref[block * k_rows:(block + 1) * k_rows].reshape(own * k_rows, k_ref.shape[2])
        moved = jnp.dot(k_select, rows, preferred_element_type=jnp.float32).astype(jnp.bfloat16)
        for u in range(own * 4):
            k_out[u // 4, u % 4, block * PACK:(block + 1) * PACK, :] = moved[u * PACK:(u + 1) * PACK]
    first_copy.wait()
    for t in range(first_hbm.shape[0]):
        spread[t] = jnp.full((8, LANES), first[t], jnp.int32)


def gather_keys(n_ctx, k_refs, keys):
    me = lax.axis_index("ctx")
    local = k_refs[0].shape[2]
    for j in range(n_ctx):
        at = pl.ds(pl.multiple_of((me ^ j) * local, local), local)
        keys[:, :, at, :] = k_refs[j][...]


def limits(n_ctx, tokens, begin, start):
    lane = lax.broadcasted_iota(jnp.int32, (8, LANES), 1)
    row = lax.broadcasted_iota(jnp.int32, (8, LANES), 0)
    place = start + lax.axis_index("ctx") * tokens + begin + lane % QTILE
    return 4 * row, place - 31 - 64 * row


def visible(nsel, span_tokens, r, s, first, row4, reach, base=None):
    least_position = 16 * 4 * nsel * 7 // 8 - span_tokens
    most_first = nsel - 1
    at = r if base is None else base + r
    mask = None
    if base is not None or 4 * r + s <= most_first:
        mask = row4 >= first - (4 * at + s)
    if base is not None or 16 * (4 * (r + 7) + s) + 31 > least_position:
        below = reach >= 64 * at + 16 * s
        mask = below if mask is None else mask & below
    return mask


def tile_columns(q_refs, g, begin):
    return jnp.concatenate(
        [q[g][h, pl.ds(begin, QTILE), :] for q in q_refs for h in range(q[g].shape[0])], axis=0
    )


def interleave(*stages):
    lengths = [length for length, _ in stages]
    done = [0] * len(stages)
    for tick in range(1, max(lengths) + 1):
        for n, (length, stage) in enumerate(stages):
            while done[n] * max(lengths) < tick * length:
                next(stage, None)
                done[n] += 1
    for _, stage in stages:
        for _ in stage:
            pass


def pooled_exponentials(q_refs, k_refs, t, group, spans, scale, masks_at, put, totals):
    for sources, j in spans:
        pieces = {}
        for g in group:
            rows = jnp.concatenate([k_refs[j][g, s] for s in range(4)], axis=0)
            columns = tile_columns([q_refs[n] for n in sources], g, t * QTILE)
            pieces[g] = lax.dot_general(rows, columns, NT, preferred_element_type=jnp.float32)
        for r in range(0, BLOCK, 8):
            masks = masks_at(t, j, r)
            for g in group:
                for at, n in enumerate(sources):
                    parts = []
                    for s in range(4):
                        part = pieces[g][s * BLOCK + r:s * BLOCK + r + 8, at * LANES:(at + 1) * LANES]
                        parts.append(jnp.exp2(jnp.where(masks[s], part, MASKED) * scale))
                    rest = parts[1] + parts[2] + parts[3]
                    put(g, n, j, r, parts[0], rest)
                    both = parts[0] + rest
                    totals[g, n] = totals[g, n] + both if (g, n) in totals else both
            yield


def mask_maker(n_ctx, tokens, start, spread):
    me = lax.axis_index("ctx")
    tiles = tokens // QTILE
    edges = [limits(n_ctx, tokens, t * QTILE, start) for t in range(tiles)]
    edges = [(row4 - spread[t], reach) for t, (row4, reach) in enumerate(edges)]

    def masks_at(t, j, r):
        low, high = edges[t]
        at = (me ^ j) * BLOCK + r
        return [(low >= -(4 * at + s)) & (high >= 64 * at + 16 * s) for s in range(4)]

    return masks_at


def early_kernel(n_ctx, n_before, start_ref, spread, *refs):
    refs = refs[n_before:]
    q_refs, k_refs, (pooled, total_ref) = refs[:-2 - n_ctx + 1], refs[-2 - n_ctx + 1:-2], refs[-2:]
    own, heads, tokens, depth = q_refs[0].shape
    q_refs = [[ref.at[g] for g in range(own)] for ref in q_refs]
    scale = math.log2(math.e) / math.sqrt(depth)
    masks_at = mask_maker(n_ctx, tokens, start_ref[0], spread)
    for t in range(tokens // QTILE):
        def put(g, n, j, r, lead, rest):
            pooled[t, g, 0, j * BLOCK + r:j * BLOCK + r + 8, n * LANES:(n + 1) * LANES] = lead
            pooled[t, g, 1, j * BLOCK + r:j * BLOCK + r + 8, n * LANES:(n + 1) * LANES] = rest

        totals = {}
        spans = [(tuple(range(len(q_refs))), j) for j in range(n_ctx - 1)]
        for _ in pooled_exponentials(q_refs, k_refs, t, range(own), spans, scale, masks_at, put, totals):
            pass
        for (g, n), total in totals.items():
            total_ref[t, g, :, n * LANES:(n + 1) * LANES] = total


def late_kernel(n_head, n_ctx, start_ref, first_hbm, spread, *refs):
    raw_q, k_refs, early = refs[:n_head], refs[n_head:n_head + n_ctx], refs[n_head + n_ctx:-9]
    out_hbm, keys, scores, pooled, lined, corner, out_ref, first_ref, sems = refs[-9:]
    own, heads, tokens, depth = raw_q[0].shape
    q_refs = [[ref.at[g] for g in range(own)] for ref in raw_q]
    nsel = keys.shape[2]
    scale = math.log2(math.e) / math.sqrt(depth)
    factor = nsel / (2.0 * n_head * heads)
    me = lax.axis_index("ctx")
    masks_at = mask_maker(n_ctx, tokens, start_ref[0], spread)
    tiles = tokens // QTILE
    last = n_ctx - 1
    weights, totals = {}, []
    sent = [
        pltpu.make_async_copy(out_ref.at[pl.ds(t * QTILE, QTILE)], out_hbm.at[pl.ds(t * QTILE, QTILE)], sems.at[t])
        for t in range(tiles)
    ]

    units = [(t, g) for t in range(tiles) for g in range(own)]

    def earlier(n):
        kept, total = early[:2] if n < n_head - 1 else early[2:]
        n = n if n < n_head - 1 else 0
        return kept, slice(n * LANES, (n + 1) * LANES), total

    def exponentials(u):
        t, g = units[u]

        def put(_, n, j, r, lead, rest):
            corner[u % 2, 0, r:r + 8, n * LANES:(n + 1) * LANES] = lead
            corner[u % 2, 1, r:r + 8, n * LANES:(n + 1) * LANES] = rest

        found = {}
        spans = [(tuple(range(n_head)), last)]
        yield from pooled_exponentials(q_refs, k_refs, t, [g], spans, scale, masks_at, put, found)
        for (_, n), total in found.items():
            _, at_n, early_total = earlier(n)
            total = jnp.sum(total + early_total[t, g, :, at_n], axis=0, keepdims=True)
            weights[u, n] = factor / total
            totals.append(total)

    def sums(u):
        t, g = units[u]
        lined[u % 2, 1, 0:8, :] = jnp.zeros((8, LANES), jnp.float32)
        for j in range(n_ctx):
            for r in range(0, BLOCK, 8):
                both = []
                for p in range(2):
                    value = None
                    for n in range(n_head):
                        if j == last:
                            part = corner[u % 2, p, r:r + 8, n * LANES:(n + 1) * LANES]
                        else:
                            kept, at_n, _ = earlier(n)
                            part = kept[t, g, p, j * BLOCK + r:j * BLOCK + r + 8, at_n]
                        part = part * weights[u, n]
                        value = part if value is None else value + part
                    both.append(value)
                here = pl.ds(pl.multiple_of(8 + (me ^ j) * BLOCK + r, 8), 8)
                lined[u % 2, 0, here, :] = both[0]
                lined[u % 2, 1, here, :] = both[0] + 2.0 * both[1]
                yield
        turned = (lined[u % 2, 0, 8:8 + nsel, :] + lined[u % 2, 1, 7:7 + nsel, :]).T
        out_ref[t * QTILE:(t + 1) * QTILE, g, :] = turned[:QTILE] + turned[QTILE:]
        if g == own - 1:
            sent[t].start()
        yield

    for step in range(len(units) + 1):
        stages = []
        if step < len(units):
            stages.append((BLOCK // 8, exponentials(step)))
        if step >= 1:
            stages.append((nsel // 8 + 1, sums(step - 1)))
        interleave(*stages)

    least, most = totals[0], totals[0]
    for part in totals[1:]:
        least, most = jnp.minimum(least, part), jnp.maximum(most, part)
    safe = (jnp.min(least) >= 1.0 / SAFE) & (jnp.max(most) <= SAFE)
    for copy in sent:
        copy.wait()

    @pl.when(jnp.logical_not(safe))
    def _():
        first_copy = pltpu.make_async_copy(first_hbm, first_ref, sems.at[0])
        first_copy.start()
        first_copy.wait()
        gather_keys(n_ctx, k_refs, keys)
        shifted(n_head, n_ctx, start_ref, first_ref, raw_q, out_ref, keys, scores, pooled, lined)
        for copy in sent:
            copy.start()
        for copy in sent:
            copy.wait()


def span_kernel(n_head, n_ctx, start_ref, first_ref, *refs):
    out_ref, keys, scores, pooled, lined = refs[n_head + n_ctx:]
    gather_keys(n_ctx, refs[n_head:n_head + n_ctx], keys)
    shifted(n_head, n_ctx, start_ref, first_ref, refs[:n_head], out_ref, keys, scores, pooled, lined)


def shifted(n_head, n_ctx, start_ref, first_ref, raw_q, out_ref, keys, scores, pooled, lined):
    own, heads, tokens, depth = raw_q[0].shape
    q_refs = [[ref.at[g] for g in range(own)] for ref in raw_q]
    nsel = keys.shape[2]
    scale = math.log2(math.e) / math.sqrt(depth)
    factor = nsel / (2.0 * n_head * heads)
    chunks = n_head * heads * QTILE // CHUNK
    per_chunk = n_head // chunks

    span = SPAN_ROWS
    spans = nsel // span

    def over_spans(body, carry):
        return lax.fori_loop(0, spans, lambda n, c: body(pl.multiple_of(n * span, span), c), carry)

    def tile(index, _):
        begin = pl.multiple_of(index * QTILE, QTILE)
        first = first_ref[index]
        row4, reach = limits(n_ctx, tokens, begin, start_ref[0])

        for g in range(own):
            weights = []
            for c in range(chunks):
                columns = tile_columns(q_refs[c * per_chunk:(c + 1) * per_chunk], g, begin)

                def scores_span(base, tops):
                    tops = list(tops)
                    rows = jnp.concatenate([keys[g, s, pl.ds(base, span), :] for s in range(4)], axis=0)
                    piece = lax.dot_general(rows, columns, NT, preferred_element_type=jnp.float32)
                    for s in range(4):
                        for r in range(0, span, 8):
                            mask = visible(nsel, n_ctx * tokens, r, s, first, row4, reach, base)
                            for n in range(CHUNK // LANES):
                                part = piece[s * span + r:s * span + r + 8, n * LANES:(n + 1) * LANES]
                                if mask is not None:
                                    part = jnp.where(mask, part, MASKED)
                                scores[0, s, pl.ds(base + r, 8), n * LANES:(n + 1) * LANES] = part
                                tops[n] = jnp.maximum(tops[n], part)
                    return tuple(tops)

                tops = over_spans(scores_span, (jnp.full((8, LANES), MASKED, jnp.float32),) * (CHUNK // LANES))
                for n in range(CHUNK // LANES):
                    at = (c * CHUNK // LANES + n) * LANES

                    def exps_span(base, total):
                        for r in range(0, span, 8):
                            here = pl.ds(base + r, 8)
                            parts = [
                                jnp.exp2((scores[0, s, here, n * LANES:(n + 1) * LANES] - tops[n]) * scale)
                                for s in range(4)
                            ]
                            rest = parts[1] + parts[2] + parts[3]
                            pooled[0, 0, here, at:at + LANES] = parts[0]
                            pooled[0, 1, here, at:at + LANES] = rest
                            total = total + (parts[0] + rest)
                        return total

                    total = over_spans(exps_span, jnp.zeros((8, LANES), jnp.float32))
                    top = jnp.max(tops[n], axis=0, keepdims=True)
                    lowered = jnp.exp2((tops[n] - top) * scale)
                    weights.append(lowered * (factor / jnp.sum(total * lowered, axis=0, keepdims=True)))

            def sums_span(base, _):
                for r in range(0, span, 8):
                    lead, rest = [
                        sum(
                            (pooled[0, p, pl.ds(base + r, 8), n * LANES:(n + 1) * LANES] * weights[n] for n in range(1, len(weights))),
                            pooled[0, p, pl.ds(base + r, 8), 0:LANES] * weights[0],
                        )
                        for p in range(2)
                    ]
                    lined[0, 0, pl.ds(base + 8 + r, 8), :] = lead
                    lined[0, 1, pl.ds(base + 8 + r, 8), :] = lead + 2.0 * rest
                return 0

            lined[0, 1, 0:8, :] = jnp.zeros((8, LANES), jnp.float32)
            over_spans(sums_span, 0)
            blocks = lined[0, 0, 8:8 + nsel, :] + lined[0, 1, 7:7 + nsel, :]
            turned = blocks.T
            out_ref[pl.ds(begin, QTILE), g, :] = turned[:QTILE] + turned[QTILE:]
        return 0

    lax.fori_loop(0, tokens // QTILE, tile, 0)


def in_hbm(array):
    return pltpu.with_memory_space_constraint(array, pltpu.HBM)


def per_device(n_head, n_ctx, queries, keys, span_start, tile_first):
    tokens, key_heads, heads, depth = queries.shape
    blocks = keys.shape[0]
    own = key_heads // n_head
    nsel = blocks * n_ctx
    vmem = pl.BlockSpec(memory_space=pltpu.VMEM)
    smem = pl.BlockSpec(memory_space=pltpu.SMEM)
    hbm = pl.BlockSpec(memory_space=pltpu.HBM)
    q_part = jax.ShapeDtypeStruct((own, heads, tokens, depth), queries.dtype)
    k_part = jax.ShapeDtypeStruct((own, 4, blocks, depth), keys.dtype)
    packed = pl.pallas_call(
        partial(pack_kernel, n_head, key_heads, heads),
        out_shape=[q_part] * n_head + [k_part, jax.ShapeDtypeStruct((tokens // QTILE, 8, LANES), jnp.int32)],
        in_specs=[hbm] * 3,
        out_specs=[vmem] * (n_head + 2),
        scratch_shapes=[
            pltpu.VMEM((tokens * key_heads * heads, depth), queries.dtype),
            pltpu.VMEM((blocks * 4, own, depth), keys.dtype),
            pltpu.SMEM(tile_first.shape, jnp.int32),
            pltpu.SemaphoreType.DMA((Q_COPIES,)),
            pltpu.SemaphoreType.DMA((K_COPIES,)),
            pltpu.SemaphoreType.DMA,
        ],
        compiler_params=pltpu.CompilerParams(vmem_limit_bytes=16 * 2 ** 20),
        name="pack",
    )(in_hbm(queries.reshape(-1, depth)), in_hbm(keys.reshape(-1, n_head, own, depth)), in_hbm(tile_first))
    q_parts, k_parts = list(packed[:n_head]), [packed[n_head]]

    def swap(array, axis, size, bit):
        return lax.ppermute(array, axis, [(i, i ^ bit) for i in range(size)])

    for d in range(1, n_head):
        q_parts[d] = swap(q_parts[d], "head", n_head, d)
    bit = n_ctx // 2
    k_parts = {0: packed[n_head]}
    while bit:
        for j in list(k_parts):
            k_parts[j | bit] = swap(k_parts[j], "ctx", n_ctx, bit)
        bit //= 2
    k_parts = [k_parts[j] for j in range(n_ctx)]
    columns = n_head * heads * QTILE
    tiles = tokens // QTILE
    limit = pltpu.CompilerParams(vmem_limit_bytes=20 * 2 ** 20)
    scratch = [
        pltpu.VMEM((own, 4, nsel, depth), keys.dtype),
        pltpu.VMEM((1, 4, nsel, columns), jnp.float32),
        pltpu.VMEM((1, 2, nsel, columns), jnp.float32),
    ]
    result = jax.ShapeDtypeStruct((tokens, own, nsel), jnp.float32)
    if (n_ctx, n_head, blocks, heads * QTILE) != (4, 4, BLOCK, LANES):
        return pl.pallas_call(
            partial(span_kernel, n_head, n_ctx),
            out_shape=result,
            in_specs=[smem, smem] + [vmem] * (n_head + n_ctx),
            out_specs=vmem,
            scratch_shapes=scratch + [pltpu.VMEM((1, 2, 8 + nsel, LANES), jnp.float32)],
            compiler_params=pltpu.CompilerParams(vmem_limit_bytes=52 * 2 ** 20),
            name="importance",
        )(span_start, tile_first, *q_parts, *k_parts)
    early = []
    for sources in (q_parts[:3], q_parts[3:]):
        lanes = len(sources) * LANES
        early += pl.pallas_call(
            partial(early_kernel, n_ctx, len(early[1:])),
            out_shape=[
                jax.ShapeDtypeStruct((tiles, own, 2, 3 * BLOCK, lanes), jnp.float32),
                jax.ShapeDtypeStruct((tiles, own, 8, lanes), jnp.float32),
            ],
            in_specs=[smem, vmem] + [pl.BlockSpec(memory_space=pl.ANY)] * len(early[1:]) + [vmem] * (len(sources) + 3),
            out_specs=[vmem, vmem],
            compiler_params=limit,
            name="early",
        )(span_start, packed[n_head + 1], *early[1:], *sources, *k_parts[:3])
    return pl.pallas_call(
        partial(late_kernel, n_head, n_ctx),
        out_shape=result,
        in_specs=[smem, hbm] + [vmem] * (n_head + n_ctx + 5),
        out_specs=hbm,
        scratch_shapes=scratch + [
            pltpu.VMEM((2, 2, 8 + nsel, LANES), jnp.float32),
            pltpu.VMEM((2, 2, BLOCK, columns), jnp.float32),
            pltpu.VMEM((tokens, own, nsel), jnp.float32),
            pltpu.SMEM(tile_first.shape, jnp.int32),
            pltpu.SemaphoreType.DMA((tiles,)),
        ],
        compiler_params=limit,
        name="late",
    )(span_start, in_hbm(tile_first), packed[n_head + 1], *q_parts, *k_parts, *early)


def solution(mesh):
    placed = (
        P(("groups", "ctx"), None, "head", None),
        P(("groups", "ctx"), None, None, None),
        P("groups"),
        P(("groups", "ctx")),
    )
    return jax.shard_map(
        partial(per_device, mesh.shape["head"], mesh.shape["ctx"]),
        mesh=mesh,
        in_specs=placed,
        out_specs=P(("groups", "ctx"), "head", None),
        check_vma=False,
    )
```

```python
import math
from functools import partial

import jax
import jax.numpy as jnp
from jax import lax
from jax.experimental import pallas as pl
from jax.experimental.pallas import tpu as pltpu
from jax.sharding import PartitionSpec as P

QTILE = 64
PACK = 16
K_COPIES = 2
Q_COPIES = 3
LANES = 128
CHUNK = 512
SPAN_ROWS = 256
BLOCK = 64
SAFE = 2.0 ** 64
MASKED = -1e30
NT = (((1,), (1,)), ((), ()))


def pack_kernel(n_head, key_heads, heads, q_hbm, k_hbm, first_hbm, *refs):
    q_outs, (k_out, spread, q_ref, k_ref, first, q_sems, k_sems, sem) = refs[:n_head], refs[n_head:]
    first_copy = pltpu.make_async_copy(first_hbm, first, sem)
    me = lax.axis_index("head")
    own = key_heads // n_head
    width = own * heads
    tokens = q_outs[0].shape[2]
    blocks = k_out.shape[2]
    q_rows = PACK * key_heads * heads
    k_rows = PACK * 4 * key_heads
    k_copies, q_copies = [], []
    k_each, q_each = blocks // PACK // K_COPIES, tokens // PACK // Q_COPIES
    for n in range(K_COPIES):
        at = pl.ds(n * k_each * k_rows, k_each * k_rows)
        k_copies.append(pltpu.make_async_copy(k_hbm.at[at], k_ref.at[at], k_sems.at[n]))
    for n in range(Q_COPIES):
        at = pl.ds(n * q_each * q_rows, q_each * q_rows)
        q_copies.append(pltpu.make_async_copy(q_hbm.at[at], q_ref.at[at], q_sems.at[n]))
    for copy in k_copies + q_copies + [first_copy]:
        copy.start()

    def bits(value, low, count):
        return (value >> low.bit_length() - 1) & (count - 1)

    out_row = lax.broadcasted_iota(jnp.int32, (own * 4 * PACK, k_rows), 0)
    in_row = lax.broadcasted_iota(jnp.int32, (own * 4 * PACK, k_rows), 1)
    source = (bits(out_row, 1, PACK) * 4 + bits(out_row, PACK, 4)) * key_heads + me * own + bits(out_row, 4 * PACK, own)
    k_select = jnp.where(in_row == source, 1.0, 0.0).astype(jnp.bfloat16)
    out_row = lax.broadcasted_iota(jnp.int32, (n_head * width * PACK, q_rows), 0)
    in_row = lax.broadcasted_iota(jnp.int32, (n_head * width * PACK, q_rows), 1)
    unit = (bits(out_row, width * PACK, n_head) ^ me) * width + bits(out_row, PACK, width)
    q_select = jnp.where(in_row == bits(out_row, 1, PACK) * (key_heads * heads) + unit, 1.0, 0.0).astype(jnp.bfloat16)

    first_copy.wait()
    for t in range(first_hbm.shape[0]):
        spread[t] = jnp.full((8, LANES), first[t], jnp.int32)
    for block in range(blocks // PACK):
        if block % k_each == 0:
            k_copies[block // k_each].wait()
        moved = jnp.dot(
            k_select, k_ref[block * k_rows:(block + 1) * k_rows, :], preferred_element_type=jnp.float32
        ).astype(jnp.bfloat16)
        for u in range(own * 4):
            k_out[u // 4, u % 4, block * PACK:(block + 1) * PACK, :] = moved[u * PACK:(u + 1) * PACK]
    for block in range(tokens // PACK):
        if block % q_each == 0:
            q_copies[block // q_each].wait()
        moved = jnp.dot(
            q_select, q_ref[block * q_rows:(block + 1) * q_rows, :], preferred_element_type=jnp.float32
        ).astype(jnp.bfloat16)
        for d in range(n_head):
            for u in range(width):
                at = (d * width + u) * PACK
                q_outs[d][u // heads, u % heads, block * PACK:(block + 1) * PACK, :] = moved[at:at + PACK]


def gather_keys(n_ctx, k_refs, keys):
    me = lax.axis_index("ctx")
    local = k_refs[0].shape[2]
    for j in range(n_ctx):
        at = pl.ds(pl.multiple_of((me ^ j) * local, local), local)
        keys[:, :, at, :] = k_refs[j][...]


def limits(n_ctx, tokens, begin, start):
    lane = lax.broadcasted_iota(jnp.int32, (8, LANES), 1)
    row = lax.broadcasted_iota(jnp.int32, (8, LANES), 0)
    place = start + lax.axis_index("ctx") * tokens + begin + lane % QTILE
    return 4 * row, place - 31 - 64 * row


def visible(nsel, span_tokens, r, s, first, row4, reach, base=None):
    least_position = 16 * 4 * nsel * 7 // 8 - span_tokens
    most_first = nsel - 1
    at = r if base is None else base + r
    mask = None
    if base is not None or 4 * r + s <= most_first:
        mask = row4 >= first - (4 * at + s)
    if base is not None or 16 * (4 * (r + 7) + s) + 31 > least_position:
        below = reach >= 64 * at + 16 * s
        mask = below if mask is None else mask & below
    return mask


def tile_columns(q_refs, g, begin):
    return jnp.concatenate(
        [q[g][h, pl.ds(begin, QTILE), :] for q in q_refs for h in range(q[g].shape[0])], axis=0
    )


def interleave(*stages):
    lengths = [length for length, _ in stages]
    done = [0] * len(stages)
    for tick in range(1, max(lengths) + 1):
        for n, (length, stage) in enumerate(stages):
            while done[n] * max(lengths) < tick * length:
                next(stage, None)
                done[n] += 1
    for _, stage in stages:
        for _ in stage:
            pass


def pooled_exponentials(q_refs, k_refs, t, group, spans, scale, masks_at, put, totals):
    for sources, j in spans:
        pieces = {}
        for g in group:
            rows = jnp.concatenate([k_refs[j][g, s] for s in range(4)], axis=0)
            columns = tile_columns([q_refs[n] for n in sources], g, t * QTILE)
            pieces[g] = lax.dot_general(rows, columns, NT, preferred_element_type=jnp.float32)
        for r in range(0, BLOCK, 8):
            masks = masks_at(t, j, r)
            for g in group:
                for at, n in enumerate(sources):
                    parts = []
                    for s in range(4):
                        part = pieces[g][s * BLOCK + r:s * BLOCK + r + 8, at * LANES:(at + 1) * LANES]
                        parts.append(jnp.exp2(jnp.where(masks[s], part, MASKED) * scale))
                    rest = parts[1] + parts[2] + parts[3]
                    put(g, n, j, r, parts[0], rest)
                    both = parts[0] + rest
                    totals[g, n] = totals[g, n] + both if (g, n) in totals else both
            yield


def mask_maker(n_ctx, tokens, start, spread):
    me = lax.axis_index("ctx")
    tiles = tokens // QTILE
    edges = [limits(n_ctx, tokens, t * QTILE, start) for t in range(tiles)]
    edges = [(row4 - spread[t], reach) for t, (row4, reach) in enumerate(edges)]

    def masks_at(t, j, r):
        low, high = edges[t]
        at = (me ^ j) * BLOCK + r
        return [(low >= -(4 * at + s)) & (high >= 64 * at + 16 * s) for s in range(4)]

    return masks_at


def early_kernel(n_ctx, n_before, start_ref, spread, *refs):
    refs = refs[n_before:]
    q_refs, k_refs, (pooled, total_ref) = refs[:-2 - n_ctx + 1], refs[-2 - n_ctx + 1:-2], refs[-2:]
    own, heads, tokens, depth = q_refs[0].shape
    q_refs = [[ref.at[g] for g in range(own)] for ref in q_refs]
    scale = math.log2(math.e) / math.sqrt(depth)
    masks_at = mask_maker(n_ctx, tokens, start_ref[0], spread)
    for t in range(tokens // QTILE):
        def put(g, n, j, r, lead, rest):
            pooled[t, g, 0, j * BLOCK + r:j * BLOCK + r + 8, n * LANES:(n + 1) * LANES] = lead
            pooled[t, g, 1, j * BLOCK + r:j * BLOCK + r + 8, n * LANES:(n + 1) * LANES] = rest

        totals = {}
        spans = [(tuple(range(len(q_refs))), j) for j in range(n_ctx - 1)]
        for _ in pooled_exponentials(q_refs, k_refs, t, range(own), spans, scale, masks_at, put, totals):
            pass
        for (g, n), total in totals.items():
            total_ref[t, g, :, n * LANES:(n + 1) * LANES] = total


def late_kernel(n_head, n_ctx, start_ref, first_hbm, spread, *refs):
    raw_q, k_refs, early = refs[:n_head], refs[n_head:n_head + n_ctx], refs[n_head + n_ctx:-9]
    out_hbm, keys, scores, pooled, lined, corner, out_ref, first_ref, sems = refs[-9:]
    own, heads, tokens, depth = raw_q[0].shape
    q_refs = [[ref.at[g] for g in range(own)] for ref in raw_q]
    nsel = keys.shape[2]
    scale = math.log2(math.e) / math.sqrt(depth)
    factor = nsel / (2.0 * n_head * heads)
    me = lax.axis_index("ctx")
    masks_at = mask_maker(n_ctx, tokens, start_ref[0], spread)
    tiles = tokens // QTILE
    last = n_ctx - 1
    weights, totals = {}, []
    sent = [
        pltpu.make_async_copy(out_ref.at[pl.ds(t * QTILE, QTILE)], out_hbm.at[pl.ds(t * QTILE, QTILE)], sems.at[t])
        for t in range(tiles)
    ]

    units = [(t, g) for t in range(tiles) for g in range(own)]

    def earlier(n):
        kept, total = early[:2] if n < n_head - 1 else early[2:]
        n = n if n < n_head - 1 else 0
        return kept, slice(n * LANES, (n + 1) * LANES), total

    def exponentials(u):
        t, g = units[u]

        def put(_, n, j, r, lead, rest):
            corner[u % 2, 0, r:r + 8, n * LANES:(n + 1) * LANES] = lead
            corner[u % 2, 1, r:r + 8, n * LANES:(n + 1) * LANES] = rest

        found = {}
        spans = [(tuple(range(n_head)), last)]
        yield from pooled_exponentials(q_refs, k_refs, t, [g], spans, scale, masks_at, put, found)
        for (_, n), total in found.items():
            _, at_n, early_total = earlier(n)
            total = jnp.sum(total + early_total[t, g, :, at_n], axis=0, keepdims=True)
            weights[u, n] = factor / total
            totals.append(total)

    def sums(u):
        t, g = units[u]
        lined[u % 2, 1, 0:8, :] = jnp.zeros((8, LANES), jnp.float32)
        for j in range(n_ctx):
            for r in range(0, BLOCK, 8):
                both = []
                for p in range(2):
                    value = None
                    for n in range(n_head):
                        if j == last:
                            part = corner[u % 2, p, r:r + 8, n * LANES:(n + 1) * LANES]
                        else:
                            kept, at_n, _ = earlier(n)
                            part = kept[t, g, p, j * BLOCK + r:j * BLOCK + r + 8, at_n]
                        part = part * weights[u, n]
                        value = part if value is None else value + part
                    both.append(value)
                here = pl.ds(pl.multiple_of(8 + (me ^ j) * BLOCK + r, 8), 8)
                lined[u % 2, 0, here, :] = both[0]
                lined[u % 2, 1, here, :] = both[0] + 2.0 * both[1]
                yield
        turned = (lined[u % 2, 0, 8:8 + nsel, :] + lined[u % 2, 1, 7:7 + nsel, :]).T
        out_ref[t * QTILE:(t + 1) * QTILE, g, :] = turned[:QTILE] + turned[QTILE:]
        if g == own - 1:
            sent[t].start()
        yield

    for step in range(len(units) + 1):
        stages = []
        if step < len(units):
            stages.append((BLOCK // 8, exponentials(step)))
        if step >= 1:
            stages.append((nsel // 8 + 1, sums(step - 1)))
        interleave(*stages)

    least, most = totals[0], totals[0]
    for part in totals[1:]:
        least, most = jnp.minimum(least, part), jnp.maximum(most, part)
    safe = (jnp.min(least) >= 1.0 / SAFE) & (jnp.max(most) <= SAFE)
    for copy in sent:
        copy.wait()

    @pl.when(jnp.logical_not(safe))
    def _():
        first_copy = pltpu.make_async_copy(first_hbm, first_ref, sems.at[0])
        first_copy.start()
        first_copy.wait()
        gather_keys(n_ctx, k_refs, keys)
        shifted(n_head, n_ctx, start_ref, first_ref, raw_q, out_ref, keys, scores, pooled, lined)
        for copy in sent:
            copy.start()
        for copy in sent:
            copy.wait()


def span_kernel(n_head, n_ctx, start_ref, first_ref, *refs):
    out_ref, keys, scores, pooled, lined = refs[n_head + n_ctx:]
    gather_keys(n_ctx, refs[n_head:n_head + n_ctx], keys)
    shifted(n_head, n_ctx, start_ref, first_ref, refs[:n_head], out_ref, keys, scores, pooled, lined)


def shifted(n_head, n_ctx, start_ref, first_ref, raw_q, out_ref, keys, scores, pooled, lined):
    own, heads, tokens, depth = raw_q[0].shape
    q_refs = [[ref.at[g] for g in range(own)] for ref in raw_q]
    nsel = keys.shape[2]
    scale = math.log2(math.e) / math.sqrt(depth)
    factor = nsel / (2.0 * n_head * heads)
    chunks = n_head * heads * QTILE // CHUNK
    per_chunk = n_head // chunks

    span = SPAN_ROWS
    spans = nsel // span

    def over_spans(body, carry):
        return lax.fori_loop(0, spans, lambda n, c: body(pl.multiple_of(n * span, span), c), carry)

    def tile(index, _):
        begin = pl.multiple_of(index * QTILE, QTILE)
        first = first_ref[index]
        row4, reach = limits(n_ctx, tokens, begin, start_ref[0])

        for g in range(own):
            weights = []
            for c in range(chunks):
                columns = tile_columns(q_refs[c * per_chunk:(c + 1) * per_chunk], g, begin)

                def scores_span(base, tops):
                    tops = list(tops)
                    rows = jnp.concatenate([keys[g, s, pl.ds(base, span), :] for s in range(4)], axis=0)
                    piece = lax.dot_general(rows, columns, NT, preferred_element_type=jnp.float32)
                    for s in range(4):
                        for r in range(0, span, 8):
                            mask = visible(nsel, n_ctx * tokens, r, s, first, row4, reach, base)
                            for n in range(CHUNK // LANES):
                                part = piece[s * span + r:s * span + r + 8, n * LANES:(n + 1) * LANES]
                                if mask is not None:
                                    part = jnp.where(mask, part, MASKED)
                                scores[0, s, pl.ds(base + r, 8), n * LANES:(n + 1) * LANES] = part
                                tops[n] = jnp.maximum(tops[n], part)
                    return tuple(tops)

                tops = over_spans(scores_span, (jnp.full((8, LANES), MASKED, jnp.float32),) * (CHUNK // LANES))
                for n in range(CHUNK // LANES):
                    at = (c * CHUNK // LANES + n) * LANES

                    def exps_span(base, total):
                        for r in range(0, span, 8):
                            here = pl.ds(base + r, 8)
                            parts = [
                                jnp.exp2((scores[0, s, here, n * LANES:(n + 1) * LANES] - tops[n]) * scale)
                                for s in range(4)
                            ]
                            rest = parts[1] + parts[2] + parts[3]
                            pooled[0, 0, here, at:at + LANES] = parts[0]
                            pooled[0, 1, here, at:at + LANES] = rest
                            total = total + (parts[0] + rest)
                        return total

                    total = over_spans(exps_span, jnp.zeros((8, LANES), jnp.float32))
                    top = jnp.max(tops[n], axis=0, keepdims=True)
                    lowered = jnp.exp2((tops[n] - top) * scale)
                    weights.append(lowered * (factor / jnp.sum(total * lowered, axis=0, keepdims=True)))

            def sums_span(base, _):
                for r in range(0, span, 8):
                    lead, rest = [
                        sum(
                            (pooled[0, p, pl.ds(base + r, 8), n * LANES:(n + 1) * LANES] * weights[n] for n in range(1, len(weights))),
                            pooled[0, p, pl.ds(base + r, 8), 0:LANES] * weights[0],
                        )
                        for p in range(2)
                    ]
                    lined[0, 0, pl.ds(base + 8 + r, 8), :] = lead
                    lined[0, 1, pl.ds(base + 8 + r, 8), :] = lead + 2.0 * rest
                return 0

            lined[0, 1, 0:8, :] = jnp.zeros((8, LANES), jnp.float32)
            over_spans(sums_span, 0)
            blocks = lined[0, 0, 8:8 + nsel, :] + lined[0, 1, 7:7 + nsel, :]
            turned = blocks.T
            out_ref[pl.ds(begin, QTILE), g, :] = turned[:QTILE] + turned[QTILE:]
        return 0

    lax.fori_loop(0, tokens // QTILE, tile, 0)


def in_hbm(array):
    return pltpu.with_memory_space_constraint(array, pltpu.HBM)


def per_device(n_head, n_ctx, queries, keys, span_start, tile_first):
    tokens, key_heads, heads, depth = queries.shape
    blocks = keys.shape[0]
    own = key_heads // n_head
    nsel = blocks * n_ctx
    vmem = pl.BlockSpec(memory_space=pltpu.VMEM)
    smem = pl.BlockSpec(memory_space=pltpu.SMEM)
    hbm = pl.BlockSpec(memory_space=pltpu.HBM)
    q_part = jax.ShapeDtypeStruct((own, heads, tokens, depth), queries.dtype)
    k_part = jax.ShapeDtypeStruct((own, 4, blocks, depth), keys.dtype)
    packed = pl.pallas_call(
        partial(pack_kernel, n_head, key_heads, heads),
        out_shape=[q_part] * n_head + [k_part, jax.ShapeDtypeStruct((tokens // QTILE, 8, LANES), jnp.int32)],
        in_specs=[hbm] * 3,
        out_specs=[vmem] * (n_head + 2),
        scratch_shapes=[
            pltpu.VMEM((tokens * key_heads * heads, depth), queries.dtype),
            pltpu.VMEM((blocks * 4 * key_heads, depth), keys.dtype),
            pltpu.SMEM(tile_first.shape, jnp.int32),
            pltpu.SemaphoreType.DMA((Q_COPIES,)),
            pltpu.SemaphoreType.DMA((K_COPIES,)),
            pltpu.SemaphoreType.DMA,
        ],
        compiler_params=pltpu.CompilerParams(vmem_limit_bytes=16 * 2 ** 20),
        name="pack",
    )(in_hbm(queries.reshape(-1, depth)), in_hbm(keys.reshape(-1, depth)), in_hbm(tile_first))
    q_parts, k_parts = list(packed[:n_head]), [packed[n_head]]

    def swap(array, axis, size, bit):
        return lax.ppermute(array, axis, [(i, i ^ bit) for i in range(size)])

    for d in range(1, n_head):
        q_parts[d] = swap(q_parts[d], "head", n_head, d)
    bit = n_ctx // 2
    k_parts = {0: packed[n_head]}
    while bit:
        for j in list(k_parts):
            k_parts[j | bit] = swap(k_parts[j], "ctx", n_ctx, bit)
        bit //= 2
    k_parts = [k_parts[j] for j in range(n_ctx)]
    columns = n_head * heads * QTILE
    tiles = tokens // QTILE
    limit = pltpu.CompilerParams(vmem_limit_bytes=20 * 2 ** 20)
    scratch = [
        pltpu.VMEM((own, 4, nsel, depth), keys.dtype),
        pltpu.VMEM((1, 4, nsel, columns), jnp.float32),
        pltpu.VMEM((1, 2, nsel, columns), jnp.float32),
    ]
    result = jax.ShapeDtypeStruct((tokens, own, nsel), jnp.float32)
    if (n_ctx, n_head, blocks, heads * QTILE) != (4, 4, BLOCK, LANES):
        return pl.pallas_call(
            partial(span_kernel, n_head, n_ctx),
            out_shape=result,
            in_specs=[smem, smem] + [vmem] * (n_head + n_ctx),
            out_specs=vmem,
            scratch_shapes=scratch + [pltpu.VMEM((1, 2, 8 + nsel, LANES), jnp.float32)],
            compiler_params=pltpu.CompilerParams(vmem_limit_bytes=52 * 2 ** 20),
            name="importance",
        )(span_start, tile_first, *q_parts, *k_parts)
    early = []
    for sources in (q_parts[:3], q_parts[3:]):
        lanes = len(sources) * LANES
        early += pl.pallas_call(
            partial(early_kernel, n_ctx, len(early[1:])),
            out_shape=[
                jax.ShapeDtypeStruct((tiles, own, 2, 3 * BLOCK, lanes), jnp.float32),
                jax.ShapeDtypeStruct((tiles, own, 8, lanes), jnp.float32),
            ],
            in_specs=[smem, vmem] + [pl.BlockSpec(memory_space=pl.ANY)] * len(early[1:]) + [vmem] * (len(sources) + 3),
            out_specs=[vmem, vmem],
            compiler_params=limit,
            name="early",
        )(span_start, packed[n_head + 1], *early[1:], *sources, *k_parts[:3])
    return pl.pallas_call(
        partial(late_kernel, n_head, n_ctx),
        out_shape=result,
        in_specs=[smem, hbm] + [vmem] * (n_head + n_ctx + 5),
        out_specs=hbm,
        scratch_shapes=scratch + [
            pltpu.VMEM((2, 2, 8 + nsel, LANES), jnp.float32),
            pltpu.VMEM((2, 2, BLOCK, columns), jnp.float32),
            pltpu.VMEM((tokens, own, nsel), jnp.float32),
            pltpu.SMEM(tile_first.shape, jnp.int32),
            pltpu.SemaphoreType.DMA((tiles,)),
        ],
        compiler_params=limit,
        name="late",
    )(span_start, in_hbm(tile_first), packed[n_head + 1], *q_parts, *k_parts, *early)


def solution(mesh):
    placed = (
        P(("groups", "ctx"), None, "head", None),
        P(("groups", "ctx"), None, None, None),
        P("groups"),
        P(("groups", "ctx")),
    )
    return jax.shard_map(
        partial(per_device, mesh.shape["head"], mesh.shape["ctx"]),
        mesh=mesh,
        in_specs=placed,
        out_specs=P(("groups", "ctx"), "head", None),
        check_vma=False,
    )
```

```python
import math
from functools import partial

import jax
import jax.numpy as jnp
from jax import lax
from jax.experimental import pallas as pl
from jax.experimental.pallas import tpu as pltpu
from jax.sharding import PartitionSpec as P

QTILE = 64
PACK = 16
K_COPIES = 2
Q_COPIES = 6
LANES = 128
CHUNK = 512
SPAN_ROWS = 256
BLOCK = 64
SAFE = 2.0 ** 64
MASKED = -1e30
NT = (((1,), (1,)), ((), ()))


def pack_kernel(n_head, key_heads, heads, q_hbm, k_hbm, first_hbm, *refs):
    q_outs, (k_out, spread, q_ref, k_ref, first, q_sems, k_sems, sem) = refs[:n_head], refs[n_head:]
    first_copy = pltpu.make_async_copy(first_hbm, first, sem)
    me = lax.axis_index("head")
    own = key_heads // n_head
    width = own * heads
    tokens = q_outs[0].shape[2]
    blocks = k_out.shape[2]
    q_rows = PACK * key_heads * heads
    k_rows = PACK * 4 * key_heads
    k_copies, q_copies = [], []
    k_each, q_each = blocks // PACK // K_COPIES, tokens // PACK // Q_COPIES
    for n in range(K_COPIES):
        at = pl.ds(n * k_each * k_rows, k_each * k_rows)
        k_copies.append(pltpu.make_async_copy(k_hbm.at[at], k_ref.at[at], k_sems.at[n]))
    for n in range(Q_COPIES):
        at = pl.ds(n * q_each * q_rows, q_each * q_rows)
        q_copies.append(pltpu.make_async_copy(q_hbm.at[at], q_ref.at[at], q_sems.at[n]))
    for copy in k_copies + q_copies + [first_copy]:
        copy.start()

    def bits(value, low, count):
        return (value >> low.bit_length() - 1) & (count - 1)

    out_row = lax.broadcasted_iota(jnp.int32, (own * 4 * PACK, k_rows), 0)
    in_row = lax.broadcasted_iota(jnp.int32, (own * 4 * PACK, k_rows), 1)
    source = (bits(out_row, 1, PACK) * 4 + bits(out_row, PACK, 4)) * key_heads + me * own + bits(out_row, 4 * PACK, own)
    k_select = jnp.where(in_row == source, 1.0, 0.0).astype(jnp.bfloat16)
    out_row = lax.broadcasted_iota(jnp.int32, (n_head * width * PACK, q_rows), 0)
    in_row = lax.broadcasted_iota(jnp.int32, (n_head * width * PACK, q_rows), 1)
    unit = (bits(out_row, width * PACK, n_head) ^ me) * width + bits(out_row, PACK, width)
    q_select = jnp.where(in_row == bits(out_row, 1, PACK) * (key_heads * heads) + unit, 1.0, 0.0).astype(jnp.bfloat16)

    first_copy.wait()
    for t in range(first_hbm.shape[0]):
        spread[t] = jnp.full((8, LANES), first[t], jnp.int32)
    for block in range(blocks // PACK):
        if block % k_each == 0:
            k_copies[block // k_each].wait()
        moved = jnp.dot(
            k_select, k_ref[block * k_rows:(block + 1) * k_rows, :], preferred_element_type=jnp.float32
        ).astype(jnp.bfloat16)
        for u in range(own * 4):
            k_out[u // 4, u % 4, block * PACK:(block + 1) * PACK, :] = moved[u * PACK:(u + 1) * PACK]
    for block in range(tokens // PACK):
        if block % q_each == 0:
            q_copies[block // q_each].wait()
        moved = jnp.dot(
            q_select, q_ref[block * q_rows:(block + 1) * q_rows, :], preferred_element_type=jnp.float32
        ).astype(jnp.bfloat16)
        for d in range(n_head):
            for u in range(width):
                at = (d * width + u) * PACK
                q_outs[d][u // heads, u % heads, block * PACK:(block + 1) * PACK, :] = moved[at:at + PACK]


def gather_keys(n_ctx, k_refs, keys):
    me = lax.axis_index("ctx")
    local = k_refs[0].shape[2]
    for j in range(n_ctx):
        at = pl.ds(pl.multiple_of((me ^ j) * local, local), local)
        keys[:, :, at, :] = k_refs[j][...]


def limits(n_ctx, tokens, begin, start):
    lane = lax.broadcasted_iota(jnp.int32, (8, LANES), 1)
    row = lax.broadcasted_iota(jnp.int32, (8, LANES), 0)
    place = start + lax.axis_index("ctx") * tokens + begin + lane % QTILE
    return 4 * row, place - 31 - 64 * row


def visible(nsel, span_tokens, r, s, first, row4, reach, base=None):
    least_position = 16 * 4 * nsel * 7 // 8 - span_tokens
    most_first = nsel - 1
    at = r if base is None else base + r
    mask = None
    if base is not None or 4 * r + s <= most_first:
        mask = row4 >= first - (4 * at + s)
    if base is not None or 16 * (4 * (r + 7) + s) + 31 > least_position:
        below = reach >= 64 * at + 16 * s
        mask = below if mask is None else mask & below
    return mask


def tile_columns(q_refs, g, begin):
    return jnp.concatenate(
        [q[g][h, pl.ds(begin, QTILE), :] for q in q_refs for h in range(q[g].shape[0])], axis=0
    )


def interleave(*stages):
    lengths = [length for length, _ in stages]
    done = [0] * len(stages)
    for tick in range(1, max(lengths) + 1):
        for n, (length, stage) in enumerate(stages):
            while done[n] * max(lengths) < tick * length:
                next(stage, None)
                done[n] += 1
    for _, stage in stages:
        for _ in stage:
            pass


def pooled_exponentials(q_refs, k_refs, t, group, spans, scale, masks_at, put, totals):
    for sources, j in spans:
        pieces = {}
        for g in group:
            rows = jnp.concatenate([k_refs[j][g, s] for s in range(4)], axis=0)
            columns = tile_columns([q_refs[n] for n in sources], g, t * QTILE)
            pieces[g] = lax.dot_general(rows, columns, NT, preferred_element_type=jnp.float32)
        for r in range(0, BLOCK, 8):
            masks = masks_at(t, j, r)
            for g in group:
                for at, n in enumerate(sources):
                    parts = []
                    for s in range(4):
                        part = pieces[g][s * BLOCK + r:s * BLOCK + r + 8, at * LANES:(at + 1) * LANES]
                        parts.append(jnp.exp2(jnp.where(masks[s], part, MASKED) * scale))
                    rest = parts[1] + parts[2] + parts[3]
                    put(g, n, j, r, parts[0], rest)
                    both = parts[0] + rest
                    totals[g, n] = totals[g, n] + both if (g, n) in totals else both
            yield


def mask_maker(n_ctx, tokens, start, spread):
    me = lax.axis_index("ctx")
    tiles = tokens // QTILE
    edges = [limits(n_ctx, tokens, t * QTILE, start) for t in range(tiles)]
    edges = [(row4 - spread[t], reach) for t, (row4, reach) in enumerate(edges)]

    def masks_at(t, j, r):
        low, high = edges[t]
        at = (me ^ j) * BLOCK + r
        return [(low >= -(4 * at + s)) & (high >= 64 * at + 16 * s) for s in range(4)]

    return masks_at


def early_kernel(n_ctx, n_before, start_ref, spread, *refs):
    refs = refs[n_before:]
    q_refs, k_refs, (pooled, total_ref) = refs[:-2 - n_ctx + 1], refs[-2 - n_ctx + 1:-2], refs[-2:]
    own, heads, tokens, depth = q_refs[0].shape
    q_refs = [[ref.at[g] for g in range(own)] for ref in q_refs]
    scale = math.log2(math.e) / math.sqrt(depth)
    masks_at = mask_maker(n_ctx, tokens, start_ref[0], spread)
    for t in range(tokens // QTILE):
        def put(g, n, j, r, lead, rest):
            pooled[t, g, 0, j * BLOCK + r:j * BLOCK + r + 8, n * LANES:(n + 1) * LANES] = lead
            pooled[t, g, 1, j * BLOCK + r:j * BLOCK + r + 8, n * LANES:(n + 1) * LANES] = rest

        totals = {}
        spans = [(tuple(range(len(q_refs))), j) for j in range(n_ctx - 1)]
        for _ in pooled_exponentials(q_refs, k_refs, t, range(own), spans, scale, masks_at, put, totals):
            pass
        for (g, n), total in totals.items():
            total_ref[t, g, :, n * LANES:(n + 1) * LANES] = total


def late_kernel(n_head, n_ctx, start_ref, first_hbm, spread, *refs):
    raw_q, k_refs, early = refs[:n_head], refs[n_head:n_head + n_ctx], refs[n_head + n_ctx:-9]
    out_hbm, keys, scores, pooled, lined, corner, out_ref, first_ref, sems = refs[-9:]
    own, heads, tokens, depth = raw_q[0].shape
    q_refs = [[ref.at[g] for g in range(own)] for ref in raw_q]
    nsel = keys.shape[2]
    scale = math.log2(math.e) / math.sqrt(depth)
    factor = nsel / (2.0 * n_head * heads)
    me = lax.axis_index("ctx")
    masks_at = mask_maker(n_ctx, tokens, start_ref[0], spread)
    tiles = tokens // QTILE
    last = n_ctx - 1
    weights, totals = {}, []
    sent = [
        pltpu.make_async_copy(out_ref.at[pl.ds(t * QTILE, QTILE)], out_hbm.at[pl.ds(t * QTILE, QTILE)], sems.at[t])
        for t in range(tiles)
    ]

    units = [(t, g) for t in range(tiles) for g in range(own)]

    def earlier(n):
        kept, total = early[:2] if n < n_head - 1 else early[2:]
        n = n if n < n_head - 1 else 0
        return kept, slice(n * LANES, (n + 1) * LANES), total

    def exponentials(u):
        t, g = units[u]

        def put(_, n, j, r, lead, rest):
            corner[u % 2, 0, r:r + 8, n * LANES:(n + 1) * LANES] = lead
            corner[u % 2, 1, r:r + 8, n * LANES:(n + 1) * LANES] = rest

        found = {}
        spans = [(tuple(range(n_head)), last)]
        yield from pooled_exponentials(q_refs, k_refs, t, [g], spans, scale, masks_at, put, found)
        for (_, n), total in found.items():
            _, at_n, early_total = earlier(n)
            total = jnp.sum(total + early_total[t, g, :, at_n], axis=0, keepdims=True)
            weights[u, n] = factor / total
            totals.append(total)

    def sums(u):
        t, g = units[u]
        lined[u % 2, 1, 0:8, :] = jnp.zeros((8, LANES), jnp.float32)
        for j in range(n_ctx):
            for r in range(0, BLOCK, 8):
                both = []
                for p in range(2):
                    value = None
                    for n in range(n_head):
                        if j == last:
                            part = corner[u % 2, p, r:r + 8, n * LANES:(n + 1) * LANES]
                        else:
                            kept, at_n, _ = earlier(n)
                            part = kept[t, g, p, j * BLOCK + r:j * BLOCK + r + 8, at_n]
                        part = part * weights[u, n]
                        value = part if value is None else value + part
                    both.append(value)
                here = pl.ds(pl.multiple_of(8 + (me ^ j) * BLOCK + r, 8), 8)
                lined[u % 2, 0, here, :] = both[0]
                lined[u % 2, 1, here, :] = both[0] + 2.0 * both[1]
                yield
        turned = (lined[u % 2, 0, 8:8 + nsel, :] + lined[u % 2, 1, 7:7 + nsel, :]).T
        out_ref[t * QTILE:(t + 1) * QTILE, g, :] = turned[:QTILE] + turned[QTILE:]
        if g == own - 1:
            sent[t].start()
        yield

    for step in range(len(units) + 1):
        stages = []
        if step < len(units):
            stages.append((BLOCK // 8, exponentials(step)))
        if step >= 1:
            stages.append((nsel // 8 + 1, sums(step - 1)))
        interleave(*stages)

    least, most = totals[0], totals[0]
    for part in totals[1:]:
        least, most = jnp.minimum(least, part), jnp.maximum(most, part)
    safe = (jnp.min(least) >= 1.0 / SAFE) & (jnp.max(most) <= SAFE)
    for copy in sent:
        copy.wait()

    @pl.when(jnp.logical_not(safe))
    def _():
        first_copy = pltpu.make_async_copy(first_hbm, first_ref, sems.at[0])
        first_copy.start()
        first_copy.wait()
        gather_keys(n_ctx, k_refs, keys)
        shifted(n_head, n_ctx, start_ref, first_ref, raw_q, out_ref, keys, scores, pooled, lined)
        for copy in sent:
            copy.start()
        for copy in sent:
            copy.wait()


def span_kernel(n_head, n_ctx, start_ref, first_ref, *refs):
    out_ref, keys, scores, pooled, lined = refs[n_head + n_ctx:]
    gather_keys(n_ctx, refs[n_head:n_head + n_ctx], keys)
    shifted(n_head, n_ctx, start_ref, first_ref, refs[:n_head], out_ref, keys, scores, pooled, lined)


def shifted(n_head, n_ctx, start_ref, first_ref, raw_q, out_ref, keys, scores, pooled, lined):
    own, heads, tokens, depth = raw_q[0].shape
    q_refs = [[ref.at[g] for g in range(own)] for ref in raw_q]
    nsel = keys.shape[2]
    scale = math.log2(math.e) / math.sqrt(depth)
    factor = nsel / (2.0 * n_head * heads)
    chunks = n_head * heads * QTILE // CHUNK
    per_chunk = n_head // chunks

    span = SPAN_ROWS
    spans = nsel // span

    def over_spans(body, carry):
        return lax.fori_loop(0, spans, lambda n, c: body(pl.multiple_of(n * span, span), c), carry)

    def tile(index, _):
        begin = pl.multiple_of(index * QTILE, QTILE)
        first = first_ref[index]
        row4, reach = limits(n_ctx, tokens, begin, start_ref[0])

        for g in range(own):
            weights = []
            for c in range(chunks):
                columns = tile_columns(q_refs[c * per_chunk:(c + 1) * per_chunk], g, begin)

                def scores_span(base, tops):
                    tops = list(tops)
                    rows = jnp.concatenate([keys[g, s, pl.ds(base, span), :] for s in range(4)], axis=0)
                    piece = lax.dot_general(rows, columns, NT, preferred_element_type=jnp.float32)
                    for s in range(4):
                        for r in range(0, span, 8):
                            mask = visible(nsel, n_ctx * tokens, r, s, first, row4, reach, base)
                            for n in range(CHUNK // LANES):
                                part = piece[s * span + r:s * span + r + 8, n * LANES:(n + 1) * LANES]
                                if mask is not None:
                                    part = jnp.where(mask, part, MASKED)
                                scores[0, s, pl.ds(base + r, 8), n * LANES:(n + 1) * LANES] = part
                                tops[n] = jnp.maximum(tops[n], part)
                    return tuple(tops)

                tops = over_spans(scores_span, (jnp.full((8, LANES), MASKED, jnp.float32),) * (CHUNK // LANES))
                for n in range(CHUNK // LANES):
                    at = (c * CHUNK // LANES + n) * LANES

                    def exps_span(base, total):
                        for r in range(0, span, 8):
                            here = pl.ds(base + r, 8)
                            parts = [
                                jnp.exp2((scores[0, s, here, n * LANES:(n + 1) * LANES] - tops[n]) * scale)
                                for s in range(4)
                            ]
                            rest = parts[1] + parts[2] + parts[3]
                            pooled[0, 0, here, at:at + LANES] = parts[0]
                            pooled[0, 1, here, at:at + LANES] = rest
                            total = total + (parts[0] + rest)
                        return total

                    total = over_spans(exps_span, jnp.zeros((8, LANES), jnp.float32))
                    top = jnp.max(tops[n], axis=0, keepdims=True)
                    lowered = jnp.exp2((tops[n] - top) * scale)
                    weights.append(lowered * (factor / jnp.sum(total * lowered, axis=0, keepdims=True)))

            def sums_span(base, _):
                for r in range(0, span, 8):
                    lead, rest = [
                        sum(
                            (pooled[0, p, pl.ds(base + r, 8), n * LANES:(n + 1) * LANES] * weights[n] for n in range(1, len(weights))),
                            pooled[0, p, pl.ds(base + r, 8), 0:LANES] * weights[0],
                        )
                        for p in range(2)
                    ]
                    lined[0, 0, pl.ds(base + 8 + r, 8), :] = lead
                    lined[0, 1, pl.ds(base + 8 + r, 8), :] = lead + 2.0 * rest
                return 0

            lined[0, 1, 0:8, :] = jnp.zeros((8, LANES), jnp.float32)
            over_spans(sums_span, 0)
            blocks = lined[0, 0, 8:8 + nsel, :] + lined[0, 1, 7:7 + nsel, :]
            turned = blocks.T
            out_ref[pl.ds(begin, QTILE), g, :] = turned[:QTILE] + turned[QTILE:]
        return 0

    lax.fori_loop(0, tokens // QTILE, tile, 0)


def in_hbm(array):
    return pltpu.with_memory_space_constraint(array, pltpu.HBM)


def per_device(n_head, n_ctx, queries, keys, span_start, tile_first):
    tokens, key_heads, heads, depth = queries.shape
    blocks = keys.shape[0]
    own = key_heads // n_head
    nsel = blocks * n_ctx
    vmem = pl.BlockSpec(memory_space=pltpu.VMEM)
    smem = pl.BlockSpec(memory_space=pltpu.SMEM)
    hbm = pl.BlockSpec(memory_space=pltpu.HBM)
    q_part = jax.ShapeDtypeStruct((own, heads, tokens, depth), queries.dtype)
    k_part = jax.ShapeDtypeStruct((own, 4, blocks, depth), keys.dtype)
    packed = pl.pallas_call(
        partial(pack_kernel, n_head, key_heads, heads),
        out_shape=[q_part] * n_head + [k_part, jax.ShapeDtypeStruct((tokens // QTILE, 8, LANES), jnp.int32)],
        in_specs=[hbm] * 3,
        out_specs=[vmem] * (n_head + 2),
        scratch_shapes=[
            pltpu.VMEM((tokens * key_heads * heads, depth), queries.dtype),
            pltpu.VMEM((blocks * 4 * key_heads, depth), keys.dtype),
            pltpu.SMEM(tile_first.shape, jnp.int32),
            pltpu.SemaphoreType.DMA((Q_COPIES,)),
            pltpu.SemaphoreType.DMA((K_COPIES,)),
            pltpu.SemaphoreType.DMA,
        ],
        compiler_params=pltpu.CompilerParams(vmem_limit_bytes=16 * 2 ** 20),
        name="pack",
    )(in_hbm(queries.reshape(-1, depth)), in_hbm(keys.reshape(-1, depth)), in_hbm(tile_first))
    q_parts, k_parts = list(packed[:n_head]), [packed[n_head]]

    def swap(array, axis, size, bit):
        return lax.ppermute(array, axis, [(i, i ^ bit) for i in range(size)])

    for d in range(1, n_head):
        q_parts[d] = swap(q_parts[d], "head", n_head, d)
    if n_head > 2:
        q_parts[1], q_parts[2] = q_parts[2], q_parts[1]
    bit = n_ctx // 2
    k_parts = {0: packed[n_head]}
    while bit:
        for j in list(k_parts):
            k_parts[j | bit] = swap(k_parts[j], "ctx", n_ctx, bit)
        bit //= 2
    k_parts = [k_parts[j] for j in range(n_ctx)]
    columns = n_head * heads * QTILE
    tiles = tokens // QTILE
    limit = pltpu.CompilerParams(vmem_limit_bytes=20 * 2 ** 20)
    scratch = [
        pltpu.VMEM((own, 4, nsel, depth), keys.dtype),
        pltpu.VMEM((1, 4, nsel, columns), jnp.float32),
        pltpu.VMEM((1, 2, nsel, columns), jnp.float32),
    ]
    result = jax.ShapeDtypeStruct((tokens, own, nsel), jnp.float32)
    if (n_ctx, n_head, blocks, heads * QTILE) != (4, 4, BLOCK, LANES):
        return pl.pallas_call(
            partial(span_kernel, n_head, n_ctx),
            out_shape=result,
            in_specs=[smem, smem] + [vmem] * (n_head + n_ctx),
            out_specs=vmem,
            scratch_shapes=scratch + [pltpu.VMEM((1, 2, 8 + nsel, LANES), jnp.float32)],
            compiler_params=pltpu.CompilerParams(vmem_limit_bytes=52 * 2 ** 20),
            name="importance",
        )(span_start, tile_first, *q_parts, *k_parts)
    early = []
    for sources in (q_parts[:3], q_parts[3:]):
        lanes = len(sources) * LANES
        early += pl.pallas_call(
            partial(early_kernel, n_ctx, len(early[1:])),
            out_shape=[
                jax.ShapeDtypeStruct((tiles, own, 2, 3 * BLOCK, lanes), jnp.float32),
                jax.ShapeDtypeStruct((tiles, own, 8, lanes), jnp.float32),
            ],
            in_specs=[smem, vmem] + [pl.BlockSpec(memory_space=pl.ANY)] * len(early[1:]) + [vmem] * (len(sources) + 3),
            out_specs=[vmem, vmem],
            compiler_params=limit,
            name="early",
        )(span_start, packed[n_head + 1], *early[1:], *sources, *k_parts[:3])
    return pl.pallas_call(
        partial(late_kernel, n_head, n_ctx),
        out_shape=result,
        in_specs=[smem, hbm] + [vmem] * (n_head + n_ctx + 5),
        out_specs=hbm,
        scratch_shapes=scratch + [
            pltpu.VMEM((2, 2, 8 + nsel, LANES), jnp.float32),
            pltpu.VMEM((2, 2, BLOCK, columns), jnp.float32),
            pltpu.VMEM((tokens, own, nsel), jnp.float32),
            pltpu.SMEM(tile_first.shape, jnp.int32),
            pltpu.SemaphoreType.DMA((tiles,)),
        ],
        compiler_params=limit,
        name="late",
    )(span_start, in_hbm(tile_first), packed[n_head + 1], *q_parts, *k_parts, *early)


def solution(mesh):
    placed = (
        P(("groups", "ctx"), None, "head", None),
        P(("groups", "ctx"), None, None, None),
        P("groups"),
        P(("groups", "ctx")),
    )
    return jax.shard_map(
        partial(per_device, mesh.shape["head"], mesh.shape["ctx"]),
        mesh=mesh,
        in_specs=placed,
        out_specs=P(("groups", "ctx"), "head", None),
        check_vma=False,
    )
```

```python
import math
from functools import partial

import jax
import jax.numpy as jnp
from jax import lax
from jax.experimental import pallas as pl
from jax.experimental.pallas import tpu as pltpu
from jax.sharding import PartitionSpec as P

QTILE = 64
PACK = 16
K_COPIES = 1
Q_COPIES = 1
LANES = 128
CHUNK = 512
SPAN_ROWS = 256
BLOCK = 64
SAFE = 2.0 ** 64
MASKED = -1e30
NT = (((1,), (1,)), ((), ()))


def pack_kernel(n_head, key_heads, heads, q_hbm, k_hbm, first_hbm, *refs):
    q_outs, (k_out, spread, q_ref, k_ref, first, q_sems, k_sems, sem) = refs[:n_head], refs[n_head:]
    first_copy = pltpu.make_async_copy(first_hbm, first, sem)
    me = lax.axis_index("head")
    own = key_heads // n_head
    width = own * heads
    tokens = q_outs[0].shape[2]
    blocks = k_out.shape[2]
    q_rows = PACK * key_heads * heads
    k_rows = PACK * 4 * key_heads
    k_copies, q_copies = [], []
    k_each, q_each = blocks // PACK // K_COPIES, tokens // PACK // Q_COPIES
    for n in range(K_COPIES):
        at = pl.ds(n * k_each * k_rows, k_each * k_rows)
        k_copies.append(pltpu.make_async_copy(k_hbm.at[at], k_ref.at[at], k_sems.at[n]))
    for n in range(Q_COPIES):
        at = pl.ds(n * q_each * q_rows, q_each * q_rows)
        q_copies.append(pltpu.make_async_copy(q_hbm.at[at], q_ref.at[at], q_sems.at[n]))
    for copy in k_copies + q_copies + [first_copy]:
        copy.start()

    def bits(value, low, count):
        return (value >> low.bit_length() - 1) & (count - 1)

    out_row = lax.broadcasted_iota(jnp.int32, (own * 4 * PACK, k_rows), 0)
    in_row = lax.broadcasted_iota(jnp.int32, (own * 4 * PACK, k_rows), 1)
    source = (bits(out_row, 1, PACK) * 4 + bits(out_row, PACK, 4)) * key_heads + me * own + bits(out_row, 4 * PACK, own)
    k_select = jnp.where(in_row == source, 1.0, 0.0).astype(jnp.bfloat16)
    out_row = lax.broadcasted_iota(jnp.int32, (n_head * width * PACK, q_rows), 0)
    in_row = lax.broadcasted_iota(jnp.int32, (n_head * width * PACK, q_rows), 1)
    unit = (bits(out_row, width * PACK, n_head) ^ me) * width + bits(out_row, PACK, width)
    q_select = jnp.where(in_row == bits(out_row, 1, PACK) * (key_heads * heads) + unit, 1.0, 0.0).astype(jnp.bfloat16)

    first_copy.wait()
    for t in range(first_hbm.shape[0]):
        spread[t] = jnp.full((8, LANES), first[t], jnp.int32)
    for block in range(blocks // PACK):
        if block % k_each == 0:
            k_copies[block // k_each].wait()
        moved = jnp.dot(
            k_select, k_ref[block * k_rows:(block + 1) * k_rows, :], preferred_element_type=jnp.float32
        ).astype(jnp.bfloat16)
        for u in range(own * 4):
            k_out[u // 4, u % 4, block * PACK:(block + 1) * PACK, :] = moved[u * PACK:(u + 1) * PACK]
    for block in range(tokens // PACK):
        if block % q_each == 0:
            q_copies[block // q_each].wait()
        moved = jnp.dot(
            q_select, q_ref[block * q_rows:(block + 1) * q_rows, :], preferred_element_type=jnp.float32
        ).astype(jnp.bfloat16)
        for d in range(n_head):
            for u in range(width):
                at = (d * width + u) * PACK
                q_outs[d][u // heads, u % heads, block * PACK:(block + 1) * PACK, :] = moved[at:at + PACK]


def gather_keys(n_ctx, k_refs, keys):
    me = lax.axis_index("ctx")
    local = k_refs[0].shape[2]
    for j in range(n_ctx):
        at = pl.ds(pl.multiple_of((me ^ j) * local, local), local)
        keys[:, :, at, :] = k_refs[j][...]


def limits(n_ctx, tokens, begin, start):
    lane = lax.broadcasted_iota(jnp.int32, (8, LANES), 1)
    row = lax.broadcasted_iota(jnp.int32, (8, LANES), 0)
    place = start + lax.axis_index("ctx") * tokens + begin + lane % QTILE
    return 4 * row, place - 31 - 64 * row


def visible(nsel, span_tokens, r, s, first, row4, reach, base=None):
    least_position = 16 * 4 * nsel * 7 // 8 - span_tokens
    most_first = nsel - 1
    at = r if base is None else base + r
    mask = None
    if base is not None or 4 * r + s <= most_first:
        mask = row4 >= first - (4 * at + s)
    if base is not None or 16 * (4 * (r + 7) + s) + 31 > least_position:
        below = reach >= 64 * at + 16 * s
        mask = below if mask is None else mask & below
    return mask


def tile_columns(q_refs, g, begin):
    return jnp.concatenate(
        [q[g][h, pl.ds(begin, QTILE), :] for q in q_refs for h in range(q[g].shape[0])], axis=0
    )


def interleave(*stages):
    lengths = [length for length, _ in stages]
    done = [0] * len(stages)
    for tick in range(1, max(lengths) + 1):
        for n, (length, stage) in enumerate(stages):
            while done[n] * max(lengths) < tick * length:
                next(stage, None)
                done[n] += 1
    for _, stage in stages:
        for _ in stage:
            pass


def pooled_exponentials(q_refs, k_refs, t, group, spans, scale, masks_at, put, totals):
    for sources, j in spans:
        pieces = {}
        for g in group:
            rows = jnp.concatenate([k_refs[j][g, s] for s in range(4)], axis=0)
            columns = tile_columns([q_refs[n] for n in sources], g, t * QTILE)
            pieces[g] = lax.dot_general(rows, columns, NT, preferred_element_type=jnp.float32)
        for r in range(0, BLOCK, 8):
            masks = masks_at(t, j, r)
            for g in group:
                for at, n in enumerate(sources):
                    parts = []
                    for s in range(4):
                        part = pieces[g][s * BLOCK + r:s * BLOCK + r + 8, at * LANES:(at + 1) * LANES]
                        parts.append(jnp.exp2(jnp.where(masks[s], part, MASKED) * scale))
                    rest = parts[1] + parts[2] + parts[3]
                    put(g, n, j, r, parts[0], rest)
                    both = parts[0] + rest
                    totals[g, n] = totals[g, n] + both if (g, n) in totals else both
            yield


def mask_maker(n_ctx, tokens, start, spread):
    me = lax.axis_index("ctx")
    tiles = tokens // QTILE
    edges = [limits(n_ctx, tokens, t * QTILE, start) for t in range(tiles)]
    edges = [(row4 - spread[t], reach) for t, (row4, reach) in enumerate(edges)]

    def masks_at(t, j, r):
        low, high = edges[t]
        at = (me ^ j) * BLOCK + r
        return [(low >= -(4 * at + s)) & (high >= 64 * at + 16 * s) for s in range(4)]

    return masks_at


def early_kernel(n_ctx, n_before, start_ref, spread, *refs):
    refs = refs[n_before:]
    q_refs, k_refs, (pooled, total_ref) = refs[:-2 - n_ctx + 1], refs[-2 - n_ctx + 1:-2], refs[-2:]
    own, heads, tokens, depth = q_refs[0].shape
    q_refs = [[ref.at[g] for g in range(own)] for ref in q_refs]
    scale = math.log2(math.e) / math.sqrt(depth)
    masks_at = mask_maker(n_ctx, tokens, start_ref[0], spread)
    for t in range(tokens // QTILE):
        def put(g, n, j, r, lead, rest):
            pooled[t, g, 0, j * BLOCK + r:j * BLOCK + r + 8, n * LANES:(n + 1) * LANES] = lead
            pooled[t, g, 1, j * BLOCK + r:j * BLOCK + r + 8, n * LANES:(n + 1) * LANES] = rest

        totals = {}
        spans = [(tuple(range(len(q_refs))), j) for j in range(n_ctx - 1)]
        for _ in pooled_exponentials(q_refs, k_refs, t, range(own), spans, scale, masks_at, put, totals):
            pass
        for (g, n), total in totals.items():
            total_ref[t, g, :, n * LANES:(n + 1) * LANES] = total


def late_kernel(n_head, n_ctx, start_ref, first_hbm, spread, *refs):
    raw_q, k_refs, early = refs[:n_head], refs[n_head:n_head + n_ctx], refs[n_head + n_ctx:-9]
    out_hbm, keys, scores, pooled, lined, corner, out_ref, first_ref, sems = refs[-9:]
    own, heads, tokens, depth = raw_q[0].shape
    q_refs = [[ref.at[g] for g in range(own)] for ref in raw_q]
    nsel = keys.shape[2]
    scale = math.log2(math.e) / math.sqrt(depth)
    factor = nsel / (2.0 * n_head * heads)
    me = lax.axis_index("ctx")
    masks_at = mask_maker(n_ctx, tokens, start_ref[0], spread)
    tiles = tokens // QTILE
    last = n_ctx - 1
    weights, totals = {}, []
    sent = [
        pltpu.make_async_copy(out_ref.at[pl.ds(t * QTILE, QTILE)], out_hbm.at[pl.ds(t * QTILE, QTILE)], sems.at[t])
        for t in range(tiles)
    ]

    units = [(t, g) for t in range(tiles) for g in range(own)]

    def earlier(n):
        kept, total = early[:2] if n < n_head - 1 else early[2:]
        n = n if n < n_head - 1 else 0
        return kept, slice(n * LANES, (n + 1) * LANES), total

    def exponentials(u):
        t, g = units[u]

        def put(_, n, j, r, lead, rest):
            corner[u % 2, 0, r:r + 8, n * LANES:(n + 1) * LANES] = lead
            corner[u % 2, 1, r:r + 8, n * LANES:(n + 1) * LANES] = rest

        found = {}
        spans = [(tuple(range(n_head)), last)]
        yield from pooled_exponentials(q_refs, k_refs, t, [g], spans, scale, masks_at, put, found)
        for (_, n), total in found.items():
            _, at_n, early_total = earlier(n)
            total = jnp.sum(total + early_total[t, g, :, at_n], axis=0, keepdims=True)
            weights[u, n] = factor / total
            totals.append(total)

    def sums(u):
        t, g = units[u]
        lined[u % 2, 1, 0:8, :] = jnp.zeros((8, LANES), jnp.float32)
        for j in range(n_ctx):
            for r in range(0, BLOCK, 8):
                both = []
                for p in range(2):
                    value = None
                    for n in range(n_head):
                        if j == last:
                            part = corner[u % 2, p, r:r + 8, n * LANES:(n + 1) * LANES]
                        else:
                            kept, at_n, _ = earlier(n)
                            part = kept[t, g, p, j * BLOCK + r:j * BLOCK + r + 8, at_n]
                        part = part * weights[u, n]
                        value = part if value is None else value + part
                    both.append(value)
                here = pl.ds(pl.multiple_of(8 + (me ^ j) * BLOCK + r, 8), 8)
                lined[u % 2, 0, here, :] = both[0]
                lined[u % 2, 1, here, :] = both[0] + 2.0 * both[1]
                yield
        turned = (lined[u % 2, 0, 8:8 + nsel, :] + lined[u % 2, 1, 7:7 + nsel, :]).T
        out_ref[t * QTILE:(t + 1) * QTILE, g, :] = turned[:QTILE] + turned[QTILE:]
        if g == own - 1:
            sent[t].start()
        yield

    for step in range(len(units) + 1):
        stages = []
        if step < len(units):
            stages.append((BLOCK // 8, exponentials(step)))
        if step >= 1:
            stages.append((nsel // 8 + 1, sums(step - 1)))
        interleave(*stages)

    least, most = totals[0], totals[0]
    for part in totals[1:]:
        least, most = jnp.minimum(least, part), jnp.maximum(most, part)
    safe = (jnp.min(least) >= 1.0 / SAFE) & (jnp.max(most) <= SAFE)
    for copy in sent:
        copy.wait()

    @pl.when(jnp.logical_not(safe))
    def _():
        first_copy = pltpu.make_async_copy(first_hbm, first_ref, sems.at[0])
        first_copy.start()
        first_copy.wait()
        gather_keys(n_ctx, k_refs, keys)
        shifted(n_head, n_ctx, start_ref, first_ref, raw_q, out_ref, keys, scores, pooled, lined)
        for copy in sent:
            copy.start()
        for copy in sent:
            copy.wait()


def span_kernel(n_head, n_ctx, start_ref, first_ref, *refs):
    out_ref, keys, scores, pooled, lined = refs[n_head + n_ctx:]
    gather_keys(n_ctx, refs[n_head:n_head + n_ctx], keys)
    shifted(n_head, n_ctx, start_ref, first_ref, refs[:n_head], out_ref, keys, scores, pooled, lined)


def shifted(n_head, n_ctx, start_ref, first_ref, raw_q, out_ref, keys, scores, pooled, lined):
    own, heads, tokens, depth = raw_q[0].shape
    q_refs = [[ref.at[g] for g in range(own)] for ref in raw_q]
    nsel = keys.shape[2]
    scale = math.log2(math.e) / math.sqrt(depth)
    factor = nsel / (2.0 * n_head * heads)
    chunks = n_head * heads * QTILE // CHUNK
    per_chunk = n_head // chunks

    span = SPAN_ROWS
    spans = nsel // span

    def over_spans(body, carry):
        return lax.fori_loop(0, spans, lambda n, c: body(pl.multiple_of(n * span, span), c), carry)

    def tile(index, _):
        begin = pl.multiple_of(index * QTILE, QTILE)
        first = first_ref[index]
        row4, reach = limits(n_ctx, tokens, begin, start_ref[0])

        for g in range(own):
            weights = []
            for c in range(chunks):
                columns = tile_columns(q_refs[c * per_chunk:(c + 1) * per_chunk], g, begin)

                def scores_span(base, tops):
                    tops = list(tops)
                    rows = jnp.concatenate([keys[g, s, pl.ds(base, span), :] for s in range(4)], axis=0)
                    piece = lax.dot_general(rows, columns, NT, preferred_element_type=jnp.float32)
                    for s in range(4):
                        for r in range(0, span, 8):
                            mask = visible(nsel, n_ctx * tokens, r, s, first, row4, reach, base)
                            for n in range(CHUNK // LANES):
                                part = piece[s * span + r:s * span + r + 8, n * LANES:(n + 1) * LANES]
                                if mask is not None:
                                    part = jnp.where(mask, part, MASKED)
                                scores[0, s, pl.ds(base + r, 8), n * LANES:(n + 1) * LANES] = part
                                tops[n] = jnp.maximum(tops[n], part)
                    return tuple(tops)

                tops = over_spans(scores_span, (jnp.full((8, LANES), MASKED, jnp.float32),) * (CHUNK // LANES))
                for n in range(CHUNK // LANES):
                    at = (c * CHUNK // LANES + n) * LANES

                    def exps_span(base, total):
                        for r in range(0, span, 8):
                            here = pl.ds(base + r, 8)
                            parts = [
                                jnp.exp2((scores[0, s, here, n * LANES:(n + 1) * LANES] - tops[n]) * scale)
                                for s in range(4)
                            ]
                            rest = parts[1] + parts[2] + parts[3]
                            pooled[0, 0, here, at:at + LANES] = parts[0]
                            pooled[0, 1, here, at:at + LANES] = rest
                            total = total + (parts[0] + rest)
                        return total

                    total = over_spans(exps_span, jnp.zeros((8, LANES), jnp.float32))
                    top = jnp.max(tops[n], axis=0, keepdims=True)
                    lowered = jnp.exp2((tops[n] - top) * scale)
                    weights.append(lowered * (factor / jnp.sum(total * lowered, axis=0, keepdims=True)))

            def sums_span(base, _):
                for r in range(0, span, 8):
                    lead, rest = [
                        sum(
                            (pooled[0, p, pl.ds(base + r, 8), n * LANES:(n + 1) * LANES] * weights[n] for n in range(1, len(weights))),
                            pooled[0, p, pl.ds(base + r, 8), 0:LANES] * weights[0],
                        )
                        for p in range(2)
                    ]
                    lined[0, 0, pl.ds(base + 8 + r, 8), :] = lead
                    lined[0, 1, pl.ds(base + 8 + r, 8), :] = lead + 2.0 * rest
                return 0

            lined[0, 1, 0:8, :] = jnp.zeros((8, LANES), jnp.float32)
            over_spans(sums_span, 0)
            blocks = lined[0, 0, 8:8 + nsel, :] + lined[0, 1, 7:7 + nsel, :]
            turned = blocks.T
            out_ref[pl.ds(begin, QTILE), g, :] = turned[:QTILE] + turned[QTILE:]
        return 0

    lax.fori_loop(0, tokens // QTILE, tile, 0)


def in_hbm(array):
    return pltpu.with_memory_space_constraint(array, pltpu.HBM)


def per_device(n_head, n_ctx, queries, keys, span_start, tile_first):
    tokens, key_heads, heads, depth = queries.shape
    blocks = keys.shape[0]
    own = key_heads // n_head
    nsel = blocks * n_ctx
    vmem = pl.BlockSpec(memory_space=pltpu.VMEM)
    smem = pl.BlockSpec(memory_space=pltpu.SMEM)
    hbm = pl.BlockSpec(memory_space=pltpu.HBM)
    q_part = jax.ShapeDtypeStruct((own, heads, tokens, depth), queries.dtype)
    k_part = jax.ShapeDtypeStruct((own, 4, blocks, depth), keys.dtype)
    packed = pl.pallas_call(
        partial(pack_kernel, n_head, key_heads, heads),
        out_shape=[q_part] * n_head + [k_part, jax.ShapeDtypeStruct((tokens // QTILE, 8, LANES), jnp.int32)],
        in_specs=[hbm] * 3,
        out_specs=[vmem] * (n_head + 2),
        scratch_shapes=[
            pltpu.VMEM((tokens * key_heads * heads, depth), queries.dtype),
            pltpu.VMEM((blocks * 4 * key_heads, depth), keys.dtype),
            pltpu.SMEM(tile_first.shape, jnp.int32),
            pltpu.SemaphoreType.DMA((Q_COPIES,)),
            pltpu.SemaphoreType.DMA((K_COPIES,)),
            pltpu.SemaphoreType.DMA,
        ],
        compiler_params=pltpu.CompilerParams(vmem_limit_bytes=16 * 2 ** 20),
        name="pack",
    )(in_hbm(queries.reshape(-1, depth)), in_hbm(keys.reshape(-1, depth)), in_hbm(tile_first))
    q_parts, k_parts = list(packed[:n_head]), [packed[n_head]]

    def swap(array, axis, size, bit):
        return lax.ppermute(array, axis, [(i, i ^ bit) for i in range(size)])

    for d in range(1, n_head):
        q_parts[d] = swap(q_parts[d], "head", n_head, d)
    bit = n_ctx // 2
    k_parts = {0: packed[n_head]}
    while bit:
        for j in list(k_parts):
            k_parts[j | bit] = swap(k_parts[j], "ctx", n_ctx, bit)
        bit //= 2
    k_parts = [k_parts[j] for j in range(n_ctx)]
    columns = n_head * heads * QTILE
    tiles = tokens // QTILE
    limit = pltpu.CompilerParams(vmem_limit_bytes=20 * 2 ** 20)
    scratch = [
        pltpu.VMEM((own, 4, nsel, depth), keys.dtype),
        pltpu.VMEM((1, 4, nsel, columns), jnp.float32),
        pltpu.VMEM((1, 2, nsel, columns), jnp.float32),
    ]
    result = jax.ShapeDtypeStruct((tokens, own, nsel), jnp.float32)
    if (n_ctx, n_head, blocks, heads * QTILE) != (4, 4, BLOCK, LANES):
        return pl.pallas_call(
            partial(span_kernel, n_head, n_ctx),
            out_shape=result,
            in_specs=[smem, smem] + [vmem] * (n_head + n_ctx),
            out_specs=vmem,
            scratch_shapes=scratch + [pltpu.VMEM((1, 2, 8 + nsel, LANES), jnp.float32)],
            compiler_params=pltpu.CompilerParams(vmem_limit_bytes=52 * 2 ** 20),
            name="importance",
        )(span_start, tile_first, *q_parts, *k_parts)
    early = []
    for sources in (q_parts[:3], q_parts[3:]):
        lanes = len(sources) * LANES
        early += pl.pallas_call(
            partial(early_kernel, n_ctx, len(early[1:])),
            out_shape=[
                jax.ShapeDtypeStruct((tiles, own, 2, 3 * BLOCK, lanes), jnp.float32),
                jax.ShapeDtypeStruct((tiles, own, 8, lanes), jnp.float32),
            ],
            in_specs=[smem, vmem] + [pl.BlockSpec(memory_space=pl.ANY)] * len(early[1:]) + [vmem] * (len(sources) + 3),
            out_specs=[vmem, vmem],
            compiler_params=limit,
            name="early",
        )(span_start, packed[n_head + 1], *early[1:], *sources, *k_parts[:3])
    return pl.pallas_call(
        partial(late_kernel, n_head, n_ctx),
        out_shape=result,
        in_specs=[smem, hbm] + [vmem] * (n_head + n_ctx + 5),
        out_specs=hbm,
        scratch_shapes=scratch + [
            pltpu.VMEM((2, 2, 8 + nsel, LANES), jnp.float32),
            pltpu.VMEM((2, 2, BLOCK, columns), jnp.float32),
            pltpu.VMEM((tokens, own, nsel), jnp.float32),
            pltpu.SMEM(tile_first.shape, jnp.int32),
            pltpu.SemaphoreType.DMA((tiles,)),
        ],
        compiler_params=limit,
        name="late",
    )(span_start, in_hbm(tile_first), packed[n_head + 1], *q_parts, *k_parts, *early)


def solution(mesh):
    placed = (
        P(("groups", "ctx"), None, "head", None),
        P(("groups", "ctx"), None, None, None),
        P("groups"),
        P(("groups", "ctx")),
    )
    return jax.shard_map(
        partial(per_device, mesh.shape["head"], mesh.shape["ctx"]),
        mesh=mesh,
        in_specs=placed,
        out_specs=P(("groups", "ctx"), "head", None),
        check_vma=False,
    )
```
